32 devices in a mesh: rep: 2 (over core), fsdp: 16 (over z, y, x).
Axes of the slice: x: 2, y: 2, z: 4, core: 2. Of those that a mesh axis runs over, the one named last changes fastest.
Arguments:
- pixels: bfloat16 [128, 256, 1728], P(('rep', 'fsdp')), may hold values from -6 to 6
- patch_kind: int32 [128], P(('rep', 'fsdp')), may hold values from 0 to 2
- labels: int32 [128], P(('rep', 'fsdp')), may hold values from -1 to 999, as said below
- resize: int32 [3, 576, 1024], replicated, may hold values from -8 to 8
- embed_kernel: float32 [3072, 768], P(None, 'fsdp'), may hold values from -0.109375 to 0.109375
- pos_base: float32 [49, 768], P(None, 'fsdp'), may hold values from -3 to 3
- gains: float32 [6, 768], P(None, 'fsdp')
- attn_weight: float32 [768, 3072], P('fsdp')
- mlp_weight: float32 [768, 6144], P('fsdp'), may hold values from -0.21875 to 0.21875
- head_weight: float32 [768, 1000], P('fsdp'), may hold values from -0.875 to 0.875
- embed_first: float32 [3072, 768], P(None, 'fsdp'), may hold values from -3.8146973e-06 to 3.8146973e-06
- pos_first: float32 [49, 768], P(None, 'fsdp'), may hold values from -3.8146973e-06 to 3.8146973e-06
- gains_first: float32 [6, 768], P(None, 'fsdp'), may hold values from -1.335144e-05 to 1.335144e-05
- attn_first: float32 [768, 3072], P('fsdp'), may hold values from -3.8146973e-06 to 3.8146973e-06
- mlp_first: float32 [768, 6144], P('fsdp'), may hold values from -3.8146973e-06 to 3.8146973e-06
- head_first: float32 [768, 1000], P('fsdp'), may hold values from -3.8146973e-06 to 3.8146973e-06
- embed_second: float32 [3072, 768], P(None, 'fsdp'), may hold values from 3.90342e-14 to 1.561368e-13
- pos_second: float32 [49, 768], P(None, 'fsdp'), may hold values from 3.90342e-14 to 1.561368e-13
- gains_second: float32 [6, 768], P(None, 'fsdp'), may hold values from 3.513078e-13 to 1.4052312e-12
- attn_second: float32 [768, 3072], P('fsdp'), may hold values from 3.90342e-14 to 1.561368e-13
- mlp_second: float32 [768, 6144], P('fsdp'), may hold values from 3.90342e-14 to 1.561368e-13
- head_second: float32 [768, 1000], P('fsdp'), may hold values from 3.90342e-14 to 1.561368e-13
Outputs:
- loss_sum: float32 [], replicated
- image_count: float32 [], replicated
- grad_norm: float32 [], replicated
- embed_kernel_new: float32 [3072, 768], P(None, 'fsdp')
- pos_base_new: float32 [49, 768], P(None, 'fsdp')
- gains_new: float32 [6, 768], P(None, 'fsdp')
- attn_weight_new: float32 [768, 3072], P('fsdp')
- mlp_weight_new: float32 [768, 6144], P('fsdp')
- head_weight_new: float32 [768, 1000], P('fsdp')
- embed_first_new: float32 [3072, 768], P(None, 'fsdp')
- pos_first_new: float32 [49, 768], P(None, 'fsdp')
- gains_first_new: float32 [6, 768], P(None, 'fsdp')
- attn_first_new: float32 [768, 3072], P('fsdp')
- mlp_first_new: float32 [768, 6144], P('fsdp')
- head_first_new: float32 [768, 1000], P('fsdp')
- embed_second_new: float32 [3072, 768], P(None, 'fsdp')
- pos_second_new: float32 [49, 768], P(None, 'fsdp')
- gains_second_new: float32 [6, 768], P(None, 'fsdp')
- attn_second_new: float32 [768, 3072], P('fsdp')
- mlp_second_new: float32 [768, 6144], P('fsdp')
- head_second_new: float32 [768, 1000], P('fsdp')
- embed_kernel_low: bfloat16 [3072, 768], P(None, 'fsdp')
- attn_weight_low: bfloat16 [768, 3072], P('fsdp')
- mlp_weight_low: bfloat16 [768, 6144], P('fsdp')
- head_weight_low: bfloat16 [768, 1000], P('fsdp')
The draws below stay inside these ranges and needn't reach their ends.
Inputs may be any that keep to these rules, and one draw needn't show every extreme that they name: `labels`: -1 marks an image that does not count; otherwise a class below 1000; some image counts.
All inputs are finite; a program needn't handle non-finite values.
Results may differ from the reference program's by a relative error of at most 0.014.
Values may be sent and summed in bfloat16 or wider, within the bound.
No kernel may reach another device: no remote copies, remote signals or barrier semaphores. Data moves between devices by JAX's collectives and lax.ppermute only.
A program may use at most 192 MiB of HBM per device.

```python
import math
import jax
import jax.numpy as jnp
from jax import lax

D = 768
HEADS = 12
HEAD_DIM = 64
FF = 3072
CLASSES = 1000
BASE = 32
GRID0 = 7
MAXP = 24
GRID = 16
STEP = 10
TOK = 256
POS = 49
KDIM = 3072
PFEAT = 1728
FSDP_IMAGES = 64
IMAGES = 128


def draw_labels(key, part):
    key = jax.random.fold_in(key, 11)
    first_key, second_key = jax.random.split(key)
    picks = jax.random.randint(first_key, (IMAGES,), 0, CLASSES)
    position = jnp.arange(IMAGES, dtype=jnp.int32) % FSDP_IMAGES
    chance = jax.random.randint(second_key, (IMAGES,), 0, 3 * (FSDP_IMAGES - 1) + 1)
    counted = chance <= FSDP_IMAGES - 1 + 2 * position
    return jnp.where(counted, picks, -1).astype(jnp.int32)


def draw_attn_weight(key, part):
    key = jax.random.fold_in(key, 12)
    column = jnp.arange(4 * D)
    spread = jnp.where(column < 3 * D, 1.0, 4.0) / jnp.sqrt(D * 1.0)
    base = jnp.clip(jax.random.normal(key, (D, 4 * D), jnp.float32), -6.0, 6.0)
    return (base * spread[None, :]).astype(jnp.float32)


def draw_gains(key, part):
    key = jax.random.fold_in(key, 13)
    first_key, second_key = jax.random.split(key)
    ramp = jnp.arange(D, dtype=jnp.float32) / D
    level = 0.6 + 1.2 * ramp
    shift = 0.3 * jnp.clip(jax.random.normal(second_key, (3, D), jnp.float32), -3.0, 3.0)
    scale = level[None, :] * jax.random.uniform(first_key, (3, D), jnp.float32, 0.75, 1.25)
    return jnp.stack([scale, shift], axis=1).reshape(6, D).astype(jnp.float32)


def touch_ends(drawn, stream_key, low, top_value):
    place = [jax.random.randint(jax.random.fold_in(stream_key, axis), (), 0, length) for axis, length in enumerate(drawn.shape)]
    longest = drawn.shape.index(max(drawn.shape))
    beside = place[:longest] + [(place[longest] + 1) % drawn.shape[longest]] + place[longest + 1:]
    return drawn.at[tuple(place)].set(low).at[tuple(beside)].set(top_value)


def steps_of(key, shape, shards, least, top_value):
    gain = 1.0
    for axis_at, blocks in shards:
        heights = jax.random.uniform(jax.random.fold_in(jax.random.fold_in(key, 6), axis_at), (blocks,), jnp.float32, least / len(shards), top_value / len(shards))
        gain = gain * jnp.repeat(jnp.exp(heights), shape[axis_at] // blocks).reshape((-1,) + (1,) * (len(shape) - 1 - axis_at))
    return gain


def noise(own_key, shape, scale, limit, shards=(), held_as=jnp.bfloat16):
    result = scale * jax.random.normal(own_key, shape, jnp.float32)
    if shards:
        result = result * steps_of(own_key, shape, shards, -0.22, 0.18)
    return jnp.clip(result, -limit, limit).astype(held_as)


def setup_inputs(seed: int = 0) -> dict:
    splits = jax.random.split(jax.random.key(seed), 23)
    pixels = noise(splits[0], (IMAGES, TOK, PFEAT), 1.0, 6.0, ((0, 32),))
    patch_kind = touch_ends(jax.random.randint(splits[1], (IMAGES,), 0, 3), jax.random.fold_in(splits[1], 1), 0, 2).astype(jnp.int32)
    labels = draw_labels(jax.random.fold_in(splits[22], 71), 0)
    resize = touch_ends(jax.random.randint(splits[3], (3, MAXP * MAXP, BASE * BASE), -8, 9), jax.random.fold_in(splits[3], 1), -8, 8).astype(jnp.int32)
    embed_kernel = noise(splits[4], (KDIM, D), KDIM ** -0.5, 0.109375, ((1, 16),), jnp.float32)
    pos_base = noise(splits[5], (POS, D), 0.5, 3.0, ((1, 16),), jnp.float32)
    gains = draw_gains(jax.random.fold_in(splits[22], 71), 0)
    attn_weight = draw_attn_weight(jax.random.fold_in(splits[22], 71), 0)
    mlp_weight = noise(splits[8], (D, 2 * FF), D ** -0.5, 0.21875, ((0, 16),), jnp.float32)
    head_weight = noise(splits[9], (D, CLASSES), (D // 16) ** -0.5, 0.875, ((0, 16),), jnp.float32)
    embed_first = noise(splits[10], (KDIM, D), (0.11 * (0.0004 / (D * (KDIM + POS + 6 + 4 * D + 2 * FF + CLASSES))) ** 0.5), 3.814697265625e-06, ((1, 16),), jnp.float32)
    pos_first = noise(splits[11], (POS, D), (0.11 * (0.0004 / (D * (KDIM + POS + 6 + 4 * D + 2 * FF + CLASSES))) ** 0.5), 3.814697265625e-06, ((1, 16),), jnp.float32)
    gains_first = noise(splits[12], (6, D), (0.33 * (0.0004 / (D * (KDIM + POS + 6 + 4 * D + 2 * FF + CLASSES))) ** 0.5), 1.33514404296875e-05, ((1, 16),), jnp.float32)
    attn_first = noise(splits[13], (D, 4 * D), (0.11 * (0.0004 / (D * (KDIM + POS + 6 + 4 * D + 2 * FF + CLASSES))) ** 0.5), 3.814697265625e-06, ((0, 16),), jnp.float32)
    mlp_first = noise(splits[14], (D, 2 * FF), (0.11 * (0.0004 / (D * (KDIM + POS + 6 + 4 * D + 2 * FF + CLASSES))) ** 0.5), 3.814697265625e-06, ((0, 16),), jnp.float32)
    head_first = noise(splits[15], (D, CLASSES), (0.11 * (0.0004 / (D * (KDIM + POS + 6 + 4 * D + 2 * FF + CLASSES))) ** 0.5), 3.814697265625e-06, ((0, 16),), jnp.float32)
    embed_second = jnp.clip(jnp.exp(math.log(1.5613679511632117e-13) - 1.3862944 * jax.random.uniform(splits[16], (KDIM, D), jnp.float32) ** steps_of(splits[16], (KDIM, D), ((1, 16),), -0.2, 0.2)), 3.903419877908029e-14, 1.5613679511632117e-13)
    pos_second = jnp.clip(jnp.exp(math.log(1.5613679511632117e-13) - 1.3862944 * jax.random.uniform(splits[17], (POS, D), jnp.float32) ** steps_of(splits[17], (POS, D), ((1, 16),), -0.2, 0.2)), 3.903419877908029e-14, 1.5613679511632117e-13)
    gains_second = jnp.clip(jnp.exp(math.log(1.4052311831519448e-12) - 1.3862944 * jax.random.uniform(splits[18], (6, D), jnp.float32) ** steps_of(splits[18], (6, D), ((1, 16),), -0.2, 0.2)), 3.513077957879862e-13, 1.4052311831519448e-12)
    attn_second = jnp.clip(jnp.exp(math.log(1.5613679511632117e-13) - 1.3862944 * jax.random.uniform(splits[19], (D, 4 * D), jnp.float32) ** steps_of(splits[19], (D, 4 * D), ((0, 16),), -0.2, 0.2)), 3.903419877908029e-14, 1.5613679511632117e-13)
    mlp_second = jnp.clip(jnp.exp(math.log(1.5613679511632117e-13) - 1.3862944 * jax.random.uniform(splits[20], (D, 2 * FF), jnp.float32) ** steps_of(splits[20], (D, 2 * FF), ((0, 16),), -0.2, 0.2)), 3.903419877908029e-14, 1.5613679511632117e-13)
    head_second = jnp.clip(jnp.exp(math.log(1.5613679511632117e-13) - 1.3862944 * jax.random.uniform(splits[21], (D, CLASSES), jnp.float32) ** steps_of(splits[21], (D, CLASSES), ((0, 16),), -0.2, 0.2)), 3.903419877908029e-14, 1.5613679511632117e-13)
    return dict(pixels=pixels, patch_kind=patch_kind, labels=labels, resize=resize, embed_kernel=embed_kernel, pos_base=pos_base, gains=gains, attn_weight=attn_weight, mlp_weight=mlp_weight, head_weight=head_weight, embed_first=embed_first, pos_first=pos_first, gains_first=gains_first, attn_first=attn_first, mlp_first=mlp_first, head_first=head_first, embed_second=embed_second, pos_second=pos_second, gains_second=gains_second, attn_second=attn_second, mlp_second=mlp_second, head_second=head_second)


HIGH = lax.Precision.HIGHEST
NORM_EPS = 1e-06
CLIP = 0.02
BETA_ONE = 0.9
BETA_TWO = 0.999
ADAM_EPS = 1e-08
RATE = 0.1
RATE_TABLE = 1.0
DECAY = 0.05

@jax.custom_vjp
def low(v):
    return lax.optimization_barrier(v.astype(jnp.bfloat16)).astype(jnp.float32)

@jax.custom_vjp
def low_back(v):
    return v

def low_keep(v):
    return (low(v), None)

def low_pass(kept, grad):
    return (grad,)

def back_keep(v):
    return (v, None)

def back_low(kept, grad):
    return (low(grad),)
low.defvjp(low_keep, low_pass)
low_back.defvjp(back_keep, back_low)

def grid_matrix():
    target = (jnp.arange(GRID, dtype=jnp.float32) + 0.5) * (GRID0 / GRID) - 0.5
    target = jnp.clip(target, 0.0, GRID0 - 1.0)
    source = jnp.arange(GRID0, dtype=jnp.float32)
    line_weights = jnp.maximum(0.0, 1.0 - jnp.abs(target[:, None] - source[None, :]))
    return (line_weights[:, None, :, None] * line_weights[None, :, None, :]).reshape(GRID * GRID, GRID0 * GRID0)

def chosen_resize(patch_kind, resize):
    chooser = (patch_kind[:, None] == jnp.arange(3, dtype=jnp.int32)[None, :]).astype(jnp.float32)
    side_len = lax.optimization_barrier(jnp.sum(chooser * jnp.array([10.0, 15.0, 24.0], dtype=jnp.float32)[None, :], axis=1))
    places = jnp.arange(MAXP * MAXP, dtype=jnp.float32)
    keeper = (places[None, :] < (side_len * side_len)[:, None]).astype(jnp.float32)
    chosen = jnp.einsum('bk,kqm->bqm', chooser, resize.astype(jnp.float32), precision=HIGH) * keeper[:, :, None]
    return (chosen, 0.25 / side_len)

def reduce_pixels(pixels, patch_kind, resize):
    chosen, factor = chosen_resize(patch_kind, resize)
    flat_pixels = pixels.astype(jnp.float32).reshape(pixels.shape[0], TOK, 3, MAXP * MAXP)
    reduced = jnp.einsum('bscq,bqm->bscm', flat_pixels, chosen, precision=HIGH) * factor[:, None, None, None]
    return low(reduced.reshape(pixels.shape[0], TOK, KDIM))

def layer_norm(values_in, gain_row, shift_row):
    row_mean = lax.optimization_barrier(jnp.mean(values_in, axis=-1, keepdims=True))
    centered = values_in - row_mean
    row_var = lax.optimization_barrier(jnp.mean(centered * centered, axis=-1, keepdims=True))
    return centered * lax.rsqrt(row_var + NORM_EPS) * gain_row + shift_row

def group_loss(rounded, posemb, reduced, labels):
    kernel_in, gain_values, attn_in, mlp_in, head_in = rounded
    stream_in = low_back(jnp.einsum('bsk,kd->bsd', reduced, kernel_in, precision=HIGH)) + posemb[None]
    normed = low(layer_norm(stream_in, gain_values[0], gain_values[1]))
    qkv_all = low_back(low(jnp.einsum('bsd,de->bse', normed, attn_in[:, :3 * D], precision=HIGH)))
    split = qkv_all.reshape(-1, TOK, 3, HEADS, HEAD_DIM)
    scores = low_back(jnp.einsum('bqhd,bkhd->bhqk', split[:, :, 0], split[:, :, 1], precision=HIGH) * HEAD_DIM ** (-0.5))
    soft_probs = low(jax.nn.softmax(scores, axis=-1))
    mixed_heads = low_back(low(jnp.einsum('bhqk,bkhd->bqhd', soft_probs, split[:, :, 2], precision=HIGH)))
    mixed_heads = mixed_heads.reshape(-1, TOK, D)
    middle = stream_in + low_back(jnp.einsum('bsd,de->bse', mixed_heads, attn_in[:, 3 * D:], precision=HIGH))
    normed_two = low(layer_norm(middle, gain_values[2], gain_values[3]))
    hidden_pre = low_back(jnp.einsum('bsd,df->bsf', normed_two, mlp_in[:, :FF], precision=HIGH))
    hidden = low(jax.nn.gelu(hidden_pre, approximate=False))
    final_stream = middle + low_back(jnp.einsum('bsf,df->bsd', hidden, mlp_in[:, FF:], precision=HIGH))
    pooled = low(lax.optimization_barrier(jnp.mean(layer_norm(final_stream, gain_values[4], gain_values[5]), axis=1)))
    logits = low_back(jnp.dot(pooled, head_in, precision=HIGH))
    log_total = jax.nn.logsumexp(logits, axis=-1)
    onehot = (labels[:, None] == jnp.arange(CLASSES, dtype=jnp.int32)[None, :]).astype(jnp.float32)
    target = lax.optimization_barrier(jnp.sum(onehot * logits, axis=-1))
    counted = (labels >= 0).astype(jnp.float32)
    return jnp.sum(counted * (log_total - target))

def adam_step(weight, first_old, second_old, gradient, step_rate, decay_rate):
    first_new = BETA_ONE * first_old + (1.0 - BETA_ONE) * gradient
    second_new = BETA_TWO * second_old + (1.0 - BETA_TWO) * gradient * gradient
    first_hat = first_new / (1.0 - BETA_ONE ** STEP)
    second_hat = second_new / (1.0 - BETA_TWO ** STEP)
    weight_new = weight - step_rate * (first_hat / (jnp.sqrt(second_hat) + ADAM_EPS) + decay_rate * weight)
    return (weight_new, first_new, second_new)

def reference(pixels, patch_kind, labels, resize, embed_kernel, pos_base, gains, attn_weight, mlp_weight, head_weight, embed_first, pos_first, gains_first, attn_first, mlp_first, head_first, embed_second, pos_second, gains_second, attn_second, mlp_second, head_second):
    reduced = reduce_pixels(pixels, patch_kind, resize)
    image_count = jnp.sum((labels >= 0).astype(jnp.float32))
    group_size = math.gcd(IMAGES, 16)
    reduced_groups = reduced.reshape(IMAGES // group_size, group_size, TOK, KDIM)
    label_groups = labels.reshape(IMAGES // group_size, group_size)
    grid_weights = grid_matrix()

    def objective(kernel_in, pos_in, gains_in, attn_in, mlp_in, head_in):
        rounded = (low(kernel_in), low(gains_in), low(attn_in), low(mlp_in), low(head_in))
        posemb = jnp.dot(grid_weights, low(pos_in), precision=HIGH)

        def one_group(running, group_item):
            return (running + group_loss(rounded, posemb, group_item[0], group_item[1]), None)
        running, ignored = lax.scan(jax.checkpoint(one_group), jnp.zeros((), jnp.float32), (reduced_groups, label_groups))
        return (running / image_count, running)
    loss_mean, back_fn, loss_sum = jax.vjp(objective, embed_kernel, pos_base, gains, attn_weight, mlp_weight, head_weight, has_aux=True)
    gradients = back_fn(jnp.ones((), jnp.float32))
    grad_norm = jnp.sqrt(sum((jnp.sum(grad_item * grad_item) for grad_item in gradients)))
    factor = jnp.minimum(1.0, CLIP / grad_norm)
    weights = (embed_kernel, pos_base, gains, attn_weight, mlp_weight, head_weight)
    firsts = (embed_first, pos_first, gains_first, attn_first, mlp_first, head_first)
    seconds = (embed_second, pos_second, gains_second, attn_second, mlp_second, head_second)
    rates = (RATE, RATE_TABLE, RATE_TABLE, RATE, RATE, RATE)
    decays = (DECAY, 0.0, 0.0, DECAY, DECAY, DECAY)
    results = [adam_step(weights[index], firsts[index], seconds[index], gradients[index] * factor, rates[index], decays[index]) for index in range(6)]
    return (loss_sum, image_count, grad_norm, results[0][0], results[1][0], results[2][0], results[3][0], results[4][0], results[5][0], results[0][1], results[1][1], results[2][1], results[3][1], results[4][1], results[5][1], results[0][2], results[1][2], results[2][2], results[3][2], results[4][2], results[5][2], results[0][0].astype(jnp.bfloat16), results[3][0].astype(jnp.bfloat16), results[4][0].astype(jnp.bfloat16), results[5][0].astype(jnp.bfloat16))
```

```python
from functools import partial

import jax
import jax.numpy as jnp
import numpy as np
from jax import lax
from jax.experimental import pallas as pl
from jax.experimental.pallas import tpu as pltpu
from jax.sharding import PartitionSpec as P

HEAD_DIM = 64
BASE = 32
GRID0 = 7
MAXP = 24
GRID = 16
STEP = 10
SIDES = (10, 15, 24)

NORM_EPS = 1e-06
CLIP = 0.02
BETA_ONE = 0.9
BETA_TWO = 0.999
ADAM_EPS = 1e-08
RATE = 0.1
RATE_TABLE = 1.0
DECAY = 0.05
BF = jnp.bfloat16
FL = jnp.float32
SMALL = 128
TILE = 512
LIMIT = 56 * 1024 * 1024


def grid_matrix():
    target = (np.arange(GRID, dtype=np.float32) + np.float32(0.5)) * (GRID0 / GRID) - 0.5
    target = np.clip(target, 0.0, GRID0 - 1.0)
    source = np.arange(GRID0, dtype=np.float32)
    line = np.maximum(0.0, 1.0 - np.abs(target[:, None] - source[None, :]))
    return (line[:, None, :, None] * line[None, :, None, :]).reshape(GRID * GRID, GRID0 * GRID0)


def adam_step(weight, first_old, second_old, gradient, step_rate, decay_rate):
    first_new = BETA_ONE * first_old + (1.0 - BETA_ONE) * gradient
    second_new = BETA_TWO * second_old + (1.0 - BETA_TWO) * gradient * gradient
    first_hat = first_new / (1.0 - BETA_ONE**STEP)
    second_hat = second_new / (1.0 - BETA_TWO**STEP)
    weight_new = weight - step_rate * (
        first_hat / (jnp.sqrt(second_hat) + ADAM_EPS) + decay_rate * weight
    )
    return (weight_new, first_new, second_new)


def partner(value, count, mask):
    return lax.ppermute(value, "fsdp", [(i, i ^ mask) for i in range(count)])


def other_core(value):
    return lax.ppermute(value, "rep", [(0, 1), (1, 0)])


def bits_of(count):
    return [1 << k for k in range(count.bit_length() - 1)]


def order_of(count, preferred):
    return preferred if sorted(preferred) == bits_of(count) else bits_of(count)


def relative_masks(order):
    masks = [0]
    for mask in reversed(order):
        masks = masks + [held ^ mask for held in masks]
    return masks


def tie(*values):
    return lax.optimization_barrier(values)


def gather_relative(shards, count, orders):
    held = [shard[None] for shard in shards]
    for step in range(len(orders[0]) - 1, 0, -1):
        got = [partner(value, count, order[step]) for value, order in zip(held, orders)]
        got = tie(*got)
        held = [jnp.concatenate(pair, axis=0) for pair in zip(held, got)]
    return held, [partner(value, count, order[0]) for value, order in zip(held, orders)]


def add_halves(keep, got):
    half = keep.shape[0] // 2
    if half == 0:
        return (keep[0].astype(FL) + got[0].astype(FL)).astype(BF), None
    return tuple(
        (keep[rows].astype(FL) + got[rows].astype(FL)).astype(BF)
        for rows in (slice(0, half), slice(half, None))
    )


def sum_everywhere(value, count):
    value = value + other_core(value)
    for mask in bits_of(count):
        value = value + partner(value, count, mask)
    return value


def halves(own, other, core):
    return jnp.where(core == 0, own, other), jnp.where(core == 0, other, own)


def dot(a, b):
    return lax.dot_general(a, b, (((1,), (0,)), ((), ())), preferred_element_type=FL)


def dot_t(a, b):
    return lax.dot_general(a, b, (((1,), (1,)), ((), ())), preferred_element_type=FL)


def t_dot(a, b):
    return lax.dot_general(a, b, (((0,), (0,)), ((), ())), preferred_element_type=FL)


def call(kernel, grid, in_specs, out_specs, out_shape, scratch=(), flops=0, moved=0, prefetch=0):
    return pl.pallas_call(
        kernel,
        grid_spec=pltpu.PrefetchScalarGridSpec(
            num_scalar_prefetch=prefetch,
            grid=grid,
            in_specs=in_specs,
            out_specs=out_specs,
            scratch_shapes=list(scratch),
        ),
        out_shape=out_shape,
        compiler_params=pltpu.CompilerParams(vmem_limit_bytes=LIMIT),
        cost_estimate=pl.CostEstimate(
            flops=int(flops), bytes_accessed=int(moved), transcendentals=0
        ),
    )


def whole(shape):
    zeros = (0,) * len(shape)
    return pl.BlockSpec(shape, lambda *a: zeros)


def sds(shape, dtype):
    return jax.ShapeDtypeStruct(shape, dtype)


def norm_parts(values_in):
    row_mean = jnp.mean(values_in, axis=-1, keepdims=True)
    centered = values_in - row_mean
    row_var = jnp.mean(centered * centered, axis=-1, keepdims=True)
    inverse = lax.rsqrt(row_var + NORM_EPS)
    return centered * inverse, inverse


def norm_back(xhat, inverse, gain, dy):
    gained = dy * gain
    one = jnp.mean(gained, axis=-1, keepdims=True)
    two = jnp.mean(gained * xhat, axis=-1, keepdims=True)
    return inverse * (gained - one - xhat * two)


def normal_cdf(x):
    z = jnp.abs(x) * 0.7071067811865476
    t = 1.0 / (1.0 + 0.3275911 * z)
    poly = t * (
        0.254829592
        + t * (-0.284496736 + t * (1.421413741 + t * (-1.453152027 + t * 1.061405429)))
    )
    bell = jnp.exp(-0.5 * x * x)
    tail = 0.5 * poly * bell
    return jnp.where(x >= 0.0, 1.0 - tail, tail), bell


def prepare_kernel(cells, core_ref, labels_ref, embed, pos, gains, attn, mlp, head, one, two, three, rest, held):
    core = core_ref[0]
    rows, width = attn.shape[0], attn.shape[1] // 4
    half, khalf, fhalf = width // 2, embed.shape[1] // 2, mlp.shape[1] // 4

    def cols(ref, base, step, size):
        return ref[:, pl.ds(pl.multiple_of(base + core * step, 128), size)].astype(BF)

    first, other = khalf - 2 * (khalf - 256) // 2, (khalf - 256) // 2
    one[:, :half] = cols(attn, 0, half, half)
    one[:, half : 2 * half] = cols(attn, width, half, half)
    one[:, 2 * half : 2 * half + first] = cols(embed, 0, khalf, first)
    two[:, :half] = cols(attn, 2 * width, half, half)
    two[:, half:] = cols(embed, first, khalf, other)
    three[:, :half] = cols(attn, 3 * width, half, half)
    three[:, half:] = cols(embed, first + other, khalf, other)
    rest[:, :fhalf] = cols(mlp, 0, fhalf, fhalf)
    rest[:, fhalf : 2 * fhalf] = cols(mlp, 2 * fhalf, fhalf, fhalf)
    chalf = rest.shape[1] - 2 * fhalf
    classes = head.shape[1]
    low_half = head[:, :chalf]
    high_half = jnp.concatenate(
        [head[:, chalf:classes], jnp.zeros((rows, 2 * chalf - classes), FL)], axis=1
    )
    rest[:, 2 * fhalf :] = jnp.where(core == 0, low_half, high_half).astype(BF)
    total = jnp.int32(0)
    for image in range(labels_ref.shape[0]):
        total = total + jnp.where(labels_ref[image] >= 0, 1, 0)
    held[...] = jnp.zeros(held.shape, FL)
    held[cells : cells + 6, :rows] = gains[...]
    held[cells + 6 : cells + 7, :] = jnp.full((1, held.shape[1]), total.astype(FL))
    turned = held[...].T
    one[:, 2 * half + first :] = turned[:rows].astype(BF)
    one[:, 2 * half + first : 2 * half + first + cells] = pos[...].astype(BF)


def reduce_kernel(kind_ref, pixels, resize, out):
    kind = kind_ref[pl.program_id(0)]
    side = jnp.where(kind == 0, SIDES[0], jnp.where(kind == 1, SIDES[1], SIDES[2]))
    feats, base = resize.shape[1], resize.shape[2]
    place = lax.broadcasted_iota(jnp.int32, (feats, base), 0)
    chosen = jnp.where(place < side * side, resize[0].astype(FL), 0.0).astype(BF)
    factor = 0.25 / side.astype(FL)
    for channel in range(3):
        part = pixels[0, channel * feats : (channel + 1) * feats, :]
        out[:, channel * base : (channel + 1) * base] = (t_dot(part, chosen) * factor).astype(BF)


def assemble_kernel(plan, cells, where_ref, core_ref, *refs):
    pieces, (kernel_t, attn, small, small_other, gains, counts), sems = refs[:12], refs[12:18], refs[18]
    core = core_ref[0]
    rows, half = pieces[0].shape[1], pieces[0].shape[0]
    targets = (kernel_t, attn, small, small_other)

    def one_block(p, ignored):
        for stream in range(3):
            for top in range(2):
                at = where_ref[stream, p + top * half] * rows
                for swapped in range(2):
                    source = pieces[4 * stream + 2 * swapped + top]
                    for src, size, target, base, step in plan[stream]:
                        if target == 2:
                            dst = targets[2 + swapped].at[pl.ds(at, rows), :]
                            sem = sems.at[2 + swapped]
                        else:
                            side = 1 - core if swapped else core
                            col = pl.multiple_of(base + side * step, 128)
                            dst = targets[target].at[pl.ds(at, rows), pl.ds(col, size)]
                            sem = sems.at[target]
                        pltpu.make_async_copy(
                            source.at[p, :, pl.ds(src, size)], dst, sem
                        ).start()
        return ignored

    lax.fori_loop(0, half, one_block, 0)
    for number, target in enumerate(targets):
        pltpu.make_async_copy(target, target, sems.at[number]).wait()
    turned = small[...].astype(FL).T
    gains[0:6, :] = turned[cells : cells + 6, :]
    gains[6:8, :] = jnp.zeros((2, gains.shape[1]), FL)
    number = turned[cells + 6 : cells + 7, :] + small_other[...].astype(FL).T[cells + 6 : cells + 7, :]
    counts[...] = jnp.sum(number, axis=1, keepdims=True) * (1.0 / rows)


def embed_kernel_body(reduced, kernel_t, cells, pos, gains, start, normed_t):
    posemb = dot_t(cells[:, :SMALL], pos[...]) + dot_t(cells[:, SMALL:], pos[...])
    x = dot_t(reduced[...], kernel_t[...]) + posemb
    start[...] = x
    xhat, ignored = norm_parts(x)
    normed_t[...] = (xhat * gains[0:1, :] + gains[1:2, :]).astype(BF).T


def attend_kernel(normed_t, start, attn, gains, qkv_t, mixed_t, lse, middle, normed_two, two_t, turned):
    width = normed_t.shape[0]
    heads = width // HEAD_DIM

    @pl.when(pl.program_id(0) == 0)
    def turn():
        for at in range(0, 3 * width, 256):
            turned[at : at + 256, :] = attn[:, at : at + 256].T

    qkv_t[...] = dot(turned[...], normed_t[...]).astype(BF)
    for head in range(heads):
        at = head * HEAD_DIM
        q = qkv_t[at : at + HEAD_DIM, :] * jnp.asarray(HEAD_DIM**-0.5, BF)
        k = qkv_t[width + at : width + at + HEAD_DIM, :]
        v = qkv_t[2 * width + at : 2 * width + at + HEAD_DIM, :]
        scores = t_dot(k, q)
        top = jnp.max(scores, axis=0, keepdims=True)
        expd = jnp.exp(scores - top)
        total = jnp.sum(expd, axis=0, keepdims=True)
        probs = (expd * (1.0 / total)).astype(BF)
        lse[0, head : head + 1, :] = top + jnp.log(total)
        mixed_t[at : at + HEAD_DIM, :] = dot(v, probs).astype(BF)
    lse[0, heads:, :] = jnp.zeros((lse.shape[1] - heads, lse.shape[2]), FL)
    x = start[...] + t_dot(mixed_t[...], attn[:, 3 * width :])
    middle[...] = x
    xhat, ignored = norm_parts(x)
    low = (xhat * gains[2:3, :] + gains[3:4, :]).astype(BF)
    normed_two[...] = low
    two_t[...] = low.T


def mlp_kernel(chunk, held, normed_two, up, down, final, hidden, slope):
    @pl.when(pl.program_id(0) == 0)
    def first():
        final[...] = held[...]

    for at in range(0, normed_two.shape[0], chunk):
        rows = slice(at, at + chunk)
        pre = dot(normed_two[rows, :], up[...])
        cdf, bell = normal_cdf(pre)
        low = (pre * cdf).astype(BF)
        hidden[rows, :] = low
        slope[rows, :] = (cdf + pre * bell * 0.3989422804014327).astype(BF)
        final[rows, :] += dot_t(low, down[...])


def head_kernel(
    images, classes, core_ref, final, labels, image_count, gains, own, other,
    d_final, e_low, e_t, own_grad, other_grad, row_grads, loss,
):
    core = core_ref[0]
    tokens = final.shape[0] // images
    width = final.shape[1]
    chalf = own.shape[1]
    gain = gains[4:5, :]
    places = lax.broadcasted_iota(jnp.int32, (8, width), 0)
    means = jnp.zeros((8, width), FL)
    for image in range(images):
        xhat, ignored = norm_parts(final[image * tokens : (image + 1) * tokens, :])
        mean_row = jnp.mean(xhat, axis=0, keepdims=True)
        means = jnp.where(places == image, mean_row, means)
    pooled = jnp.where(places < images, means * gain + gains[5:6, :], 0.0).astype(BF)
    logits = [dot(pooled, own[...]), dot(pooled, other[...])]
    lane = lax.broadcasted_iota(jnp.int32, (8, chalf), 1)
    kinds = [lane + core * chalf, lane + (1 - core) * chalf]
    masked = [jnp.where(kinds[k] < classes, logits[k], -1e30) for k in range(2)]
    top = jnp.maximum(
        jnp.max(masked[0], axis=1, keepdims=True), jnp.max(masked[1], axis=1, keepdims=True)
    )
    expd = [jnp.where(kinds[k] < classes, jnp.exp(masked[k] - top), 0.0) for k in range(2)]
    total = jnp.sum(expd[0], axis=1, keepdims=True) + jnp.sum(expd[1], axis=1, keepdims=True)
    log_total = top + jnp.log(total)
    named = labels[...]
    onehot = [(kinds[k] == named).astype(FL) for k in range(2)]
    target = jnp.sum(onehot[0] * logits[0], axis=1, keepdims=True) + jnp.sum(
        onehot[1] * logits[1], axis=1, keepdims=True
    )
    counted = (named >= 0).astype(FL)
    losses = counted * (log_total - target)
    loss[...] = jnp.broadcast_to(jnp.sum(losses, axis=0, keepdims=True), loss.shape)
    share = counted / image_count[...]
    d_logits = [((expd[k] / total - onehot[k]) * share).astype(BF) for k in range(2)]
    own_grad[...] = t_dot(pooled, d_logits[0])
    other_grad[...] = t_dot(pooled, d_logits[1]).astype(BF)
    d_pooled = dot_t(d_logits[0], own[...]) + dot_t(d_logits[1], other[...])
    row_grads[0:1, :] = jnp.sum(d_pooled * means, axis=0, keepdims=True)
    row_grads[1:2, :] = jnp.sum(d_pooled, axis=0, keepdims=True)
    row_grads[2:8, :] = jnp.zeros((6, width), FL)
    for image in range(images):
        rows = slice(image * tokens, (image + 1) * tokens)
        xhat, inverse = norm_parts(final[rows, :])
        dy = d_pooled[image : image + 1, :] * (1.0 / tokens)
        back = norm_back(xhat, inverse, gain, dy)
        d_final[rows, :] = back
        low = back.astype(BF)
        e_low[rows, :] = low
        e_t[:, rows] = low.T


def mlp_back_other_kernel(
    chunk, e_low, e_t, n_t, hidden, slope, up, down, d_normed, down_grad, up_grad, d_pre
):
    @pl.when(pl.program_id(0) == 0)
    def first():
        d_normed[...] = jnp.zeros(d_normed.shape, FL)

    down_grad[...] = dot(e_t[...], hidden[...]).astype(BF)
    for at in range(0, e_low.shape[0], chunk):
        rows = slice(at, at + chunk)
        d_pre[rows, :] = (dot(e_low[rows, :], down[...]) * slope[rows, :].astype(FL)).astype(BF)
        d_normed[rows, :] += dot_t(d_pre[rows, :], up[...])
    up_grad[...] = dot(n_t[...], d_pre[...]).astype(BF)


def mlp_back_own_kernel(
    chunk, tokens, core_ref, held, e_low, slope, up, down, middle, d_final, gains, mixed_t, four_grads,
    d_pre, d_middle, o_low, row_grads, out_grad, d_normed,
):
    @pl.when(pl.program_id(0) == 0)
    def first():
        d_normed[...] = held[...]

    for at in range(0, e_low.shape[0], chunk):
        rows = slice(at, at + chunk)
        part = (dot(e_low[rows, :], down[...]) * slope[rows, :].astype(FL)).astype(BF)
        d_pre[rows, :] = part
        d_normed[rows, :] += dot_t(part, up[...])

    @pl.when(pl.program_id(0) == pl.num_programs(0) - 1)
    def last():
        width = e_low.shape[1]
        gain_sum = jnp.zeros((1, width), FL)
        shift_sum = jnp.zeros((1, width), FL)
        for at in range(0, e_low.shape[0], tokens):
            rows = slice(at, at + tokens)
            xhat, inverse = norm_parts(middle[rows, :])
            dy = d_normed[rows, :]
            gain_sum += jnp.sum(dy * xhat, axis=0, keepdims=True)
            shift_sum += jnp.sum(dy, axis=0, keepdims=True)
            back = d_final[rows, :] + norm_back(xhat, inverse, gains[2:3, :], dy)
            d_middle[rows, :] = back
            o_low[rows, :] = back.astype(BF)
        row_grads[0:2, :] = jnp.zeros((2, width), FL)
        row_grads[2:3, :] = gain_sum
        row_grads[3:4, :] = shift_sum
        row_grads[4:6, :] = four_grads[0:2, :]
        row_grads[6:8, :] = jnp.zeros((2, width), FL)
        half = width // 2
        other = pl.multiple_of((1 - core_ref[0]) * half, 128)
        out_grad[...] = dot(mixed_t[...], o_low[:, pl.ds(other, half)]).astype(BF)


def place(where_ref, row, rows, value, held, keep, send, col):
    size = value.shape[1]
    if send is None:
        keep[:, col : col + size] = value.astype(BF)
        return
    held[:, :size] = value
    half = keep.shape[0]
    for p in range(half):
        low = pl.multiple_of(where_ref[row, p] * rows, rows)
        high = pl.multiple_of(where_ref[row, half + p] * rows, rows)
        keep[p, :, col : col + size] = held[pl.ds(low, rows), :size].astype(BF)
        send[p, :, col : col + size] = held[pl.ds(high, rows), :size].astype(BF)


def split_outs(refs, aligned, number):
    if aligned:
        return [(refs[2 * k], refs[2 * k + 1]) for k in range(number)], refs[2 * number :]
    return [(refs[k], None) for k in range(number)], refs[number:]


def down_grad_kernel(aligned, rows, where_ref, e_t, hidden, got, *refs):
    ((keep, send),), (held,) = split_outs(refs, aligned, 1)
    value = dot(e_t[...], hidden[...]) + got[...].astype(FL)
    size = hidden.shape[1]
    for tile in range(3):
        @pl.when(pl.program_id(0) == tile)
        def store(tile=tile):
            place(where_ref, 0, rows, value, held, keep, send, tile * size)


def up_grad_kernel(
    aligned, rows, where_ref, core_ref, n_t, d_pre, got, mixed_t, o_low, out_got, head_own, head_got, *refs
):
    ((keep, send), (keep_two, send_two)), (held,) = split_outs(refs, aligned, 2)
    step = pl.program_id(0)

    @pl.when(step == 0)
    def first():
        half = o_low.shape[1] // 2
        own = pl.multiple_of(core_ref[0] * half, 128)
        value = dot(mixed_t[...], o_low[:, pl.ds(own, half)]) + out_got[...].astype(FL)
        place(where_ref, 1, rows, value, held, keep_two, send_two, head_own.shape[1])
        value = head_own[...] + head_got[...].astype(FL)
        place(where_ref, 1, rows, value, held, keep_two, send_two, 0)

    value = dot(n_t[...], d_pre[...]) + got[...].astype(FL)
    size = d_pre.shape[1]
    for tile in range(3):
        @pl.when(step == tile)
        def store(tile=tile):
            place(where_ref, 0, rows, value, held, keep, send, tile * size)


def attend_back_kernel(
    cells_count, final, o_low, attn, qkv_t, lse, d_middle, start, gains, cells, grads_in, *refs
):
    sum_in, refs = (refs[0], refs[3:]) if final else (None, refs)
    d_qkv_t, s_t, sum_out, grads_out, d_mixed_t, summed, row_grads = refs
    width = o_low.shape[1]
    heads = width // HEAD_DIM
    image = pl.program_id(0)

    @pl.when(image == 0)
    def first():
        summed[...] = sum_in[...] if final else jnp.zeros(summed.shape, FL)
        row_grads[...] = grads_in[...]

    scale = HEAD_DIM**-0.5
    d_mixed_t[...] = dot_t(attn[:, 3 * width :], o_low[...]).astype(BF)
    for head in range(heads):
        at = head * HEAD_DIM
        q = qkv_t[at : at + HEAD_DIM, :] * jnp.asarray(scale, BF)
        k = qkv_t[width + at : width + at + HEAD_DIM, :]
        v = qkv_t[2 * width + at : 2 * width + at + HEAD_DIM, :]
        dm = d_mixed_t[at : at + HEAD_DIM, :]
        probs = jnp.exp(t_dot(k, q) - lse[0, head : head + 1, :])
        d_probs = t_dot(v, dm)
        delta = jnp.sum(probs * d_probs, axis=0, keepdims=True)
        d_scores = (probs * (d_probs - delta)).astype(BF)
        d_qkv_t[at : at + HEAD_DIM, :] = (dot(k, d_scores) * scale).astype(BF)
        d_qkv_t[width + at : width + at + HEAD_DIM, :] = dot_t(q, d_scores).astype(BF)
        d_qkv_t[2 * width + at : 2 * width + at + HEAD_DIM, :] = dot_t(
            dm, probs.astype(BF)
        ).astype(BF)
    dy = dot(attn[:, : 3 * width], d_qkv_t[...]).T
    xhat, inverse = norm_parts(start[...])
    back = d_middle[...] + norm_back(xhat, inverse, gains[0:1, :], dy)
    s_t[...] = back.astype(BF).T
    summed[...] += back
    row_grads[0:1, :] += jnp.sum(dy * xhat, axis=0, keepdims=True)
    row_grads[1:2, :] += jnp.sum(dy, axis=0, keepdims=True)

    @pl.when(image == pl.num_programs(0) - 1)
    def last():
        grads_out[...] = row_grads[...]
        if not final:
            sum_out[...] = summed[...]
            return
        total = lax.dot_general(
            cells[...], summed[...], (((0,), (0,)), ((), ())),
            preferred_element_type=FL, precision=lax.Precision.HIGHEST,
        )
        summed[0:SMALL, :] = total
        summed[cells_count : cells_count + 6, :] = row_grads[0:6, :]
        sum_out[...] = summed[0:SMALL, :].T


def plain_grad_kernel(turned, core_ref, x_t, y, out):
    out[...] = (dot_t(x_t[...], y[...]) if turned else dot(x_t[...], y[...])).astype(BF)


def tail_grad_kernel(
    aligned, rows, where_ref, core_ref, n_t, s_t, d_qkv_t, reduced, attn_got, kernel_got, small, small_got, *refs
):
    outs, (held,) = split_outs(refs, aligned, 3)
    step = pl.program_id(0)

    one = dot_t(n_t[...], d_qkv_t[...]) + attn_got[...].astype(FL)
    two = dot(s_t[...], reduced[...]) + kernel_got[...].astype(FL)
    for stream in range(3):
        @pl.when(step == stream)
        def store(stream=stream):
            keep, send = outs[stream]
            place(where_ref, stream, rows, one, held, keep, send, 0)
            place(where_ref, stream, rows, two, held, keep, send, one.shape[1])
            if stream == 0:
                place(
                    where_ref, stream, rows, small[...] + small_got[...], held, keep, send,
                    one.shape[1] + two.shape[1],
                )


def square_kernel(tail_width, loss, *refs):
    *parts, out = refs
    total = jnp.zeros((1, 1), FL)

    def squares(value):
        value = value.astype(FL)
        return jnp.sum(jnp.sum(value * value, axis=0, keepdims=True), axis=1, keepdims=True)

    for number, part in enumerate(parts):
        if number == 0:
            total += squares(part[:, :tail_width]) + 0.5 * squares(part[:, tail_width:])
        else:
            total += squares(part[...])
    lane = lax.broadcasted_iota(jnp.int32, out.shape, 1)
    out[...] = jnp.where(lane == 0, total, jnp.where(lane == 1, loss[...], 0.0))


def update_kernel(cells, classes, core_ref, sums, *refs):
    grads, refs = refs[:12], refs[12:]
    olds, news, lows = refs[:15], refs[15:30], refs[30:]
    core = core_ref[0]
    norm = jnp.sqrt(sums[0:1, 0:1])
    factor = jnp.minimum(1.0, CLIP / norm)

    def step(table, cols, gradient, rate, decay, low):
        weight, first, second = (olds[5 * k + table][cols] for k in range(3))
        results = adam_step(weight, first, second, gradient.astype(FL) * factor, rate, decay)
        for k in range(3):
            news[5 * k + table][cols] = results[k]
        if low is not None:
            lows[low][cols] = results[0].astype(BF)

    def part(side, index, lo, size):
        return grads[6 * side + index][:, lo : lo + size]

    def cols(base, side, half):
        place = 1 - core if side else core
        return (slice(None), pl.ds(pl.multiple_of(base + place * half, 128), half))

    width = olds[2].shape[1] // 4
    fhalf, half, khalf = olds[3].shape[1] // 4, width // 2, olds[0].shape[1] // 2
    third = khalf // 3
    chalf = grads[5].shape[1] - half
    for side in range(2):
        for k in range(3):
            step(2, cols(k * width, side, half), part(side, k, 0, half), RATE, DECAY, 1)
            place = 1 - core if side else core
            at = pl.multiple_of(place * khalf + k * third, 128)
            step(0, (slice(None), pl.ds(at, third)), part(side, k, half, third), RATE, DECAY, 0)
        step(2, cols(3 * width, side, half), part(side, 5, chalf, half), RATE, DECAY, 1)
        for k in range(2):
            step(3, cols(k * 2 * fhalf, side, fhalf), part(side, 4 - k, 0, fhalf), RATE, DECAY, 2)
    own, other = part(0, 5, 0, chalf), part(1, 5, 0, chalf)
    low_half = jnp.where(core == 0, own.astype(FL), other.astype(FL))
    high_half = jnp.where(core == 0, other.astype(FL), own.astype(FL))
    step(4, (slice(None), slice(0, chalf)), low_half, RATE, DECAY, 3)
    step(4, (slice(None), slice(chalf, classes)), high_half[:, : classes - chalf], RATE, DECAY, 3)
    tiny = part(0, 0, half + third, SMALL)
    step(1, (slice(None), slice(0, cells)), tiny[:, :cells], RATE_TABLE, 0.0, None)


def body(
    count,
    pixels,
    patch_kind,
    labels,
    resize,
    embed_kernel,
    pos_base,
    gains,
    attn_weight,
    mlp_weight,
    head_weight,
    embed_first,
    pos_first,
    gains_first,
    attn_first,
    mlp_first,
    head_first,
    embed_second,
    pos_second,
    gains_second,
    attn_second,
    mlp_second,
    head_second,
):
    me = lax.axis_index("fsdp")
    core = lax.axis_index("rep")
    core_at = core.astype(jnp.int32)[None]
    images, tokens = pixels.shape[:2]
    total = images * tokens
    rows, width = attn_weight.shape[0], attn_weight.shape[0] * count
    aligned = rows % 16 == 0 and count & (count - 1) == 0
    ffw = mlp_weight.shape[1] // 2
    classes = head_weight.shape[1]
    kdim = embed_kernel.shape[0]
    cells_count = pos_base.shape[0]
    feats, base = resize.shape[1:]
    chalf = -(-classes // 256) * 128
    half, fhalf, khalf = width // 2, ffw // 2, kdim // 2
    third = khalf // 3
    heads = width // HEAD_DIM
    lse_rows = -(-heads // 8) * 8
    chunk = min(total, 512)
    tiles = fhalf // TILE

    other_first = (khalf - 256) // 2
    widths = (width + 256 + SMALL, half + other_first, half + other_first)
    *pieces, rest = call(
        partial(prepare_kernel, cells_count),
        (1,),
        [
            whole((rows, kdim)),
            whole((rows, cells_count)),
            whole((6, rows)),
            whole((rows, 4 * width)),
            whole((rows, 2 * ffw)),
            whole((rows, classes)),
        ],
        [whole((rows, size)) for size in widths] + [whole((rows, ffw + chalf))],
        [sds((rows, size), BF) for size in widths] + [sds((rows, ffw + chalf), BF)],
        scratch=[pltpu.VMEM((128, 128), FL)],
        moved=rows * (kdim + 4 * width + 2 * ffw + classes) * 5,
        prefetch=2,
    )(core_at, labels, embed_kernel.T, pos_base.T, gains, attn_weight, mlp_weight, head_weight)
    rest_own = lax.all_gather(rest, "fsdp", axis=0, tiled=True)

    fan_orders = [
        order_of(count, [1, 4, 8, 2]),
        order_of(count, [2, 1, 4, 8]),
        order_of(count, [4, 2, 1, 8]),
    ]
    if aligned:
        near, far = gather_relative(pieces, count, fan_orders)
        *near, patch_kind = tie(*near, patch_kind)
    reduced = call(
        reduce_kernel,
        (images,),
        [
            pl.BlockSpec((1, 3 * feats, tokens), lambda b, kind: (b, 0, 0)),
            pl.BlockSpec((1, feats, base), lambda b, kind: (kind[b], 0, 0)),
        ],
        pl.BlockSpec((tokens, kdim), lambda b, kind: (b, 0)),
        sds((total, kdim), BF),
        flops=2 * total * 3 * feats * base,
        moved=total * kdim * 2 + total * 3 * feats * 2 + images * feats * base * 4,
        prefetch=1,
    )(patch_kind, jnp.transpose(pixels, (0, 2, 1)), resize)

    if aligned:
        *far, reduced = tie(*far, reduced)
        gathered = []
        for one, two in zip(near, far):
            gathered += [one, two, other_core(one), other_core(two)]
        where_fan = jnp.stack(
            [me ^ jnp.array(relative_masks(order), jnp.int32) for order in fan_orders]
        )
        plan = (
            (
                (0, half, 1, 0, half),
                (half, half, 1, width, half),
                (width, 256, 0, 0, khalf),
                (width + 256, SMALL, 2, 0, 0),
            ),
            ((0, half, 1, 2 * width, half), (half, other_first, 0, 256, khalf)),
            ((0, half, 1, 3 * width, half), (half, other_first, 0, 256 + other_first, khalf)),
        )
        kernel_t, attn_low, small, small_other, gain_rows, image_count = call(
            partial(assemble_kernel, plan, cells_count),
            (1,),
            [pl.BlockSpec(memory_space=pl.ANY)] * 12,
            [
                whole((width, kdim)),
                whole((width, 4 * width)),
                whole((width, SMALL)),
                whole((width, SMALL)),
                whole((8, width)),
                whole((1, 1)),
            ],
            [
                sds((width, kdim), BF),
                sds((width, 4 * width), BF),
                sds((width, SMALL), BF),
                sds((width, SMALL), BF),
                sds((8, width), FL),
                sds((1, 1), FL),
            ],
            scratch=[pltpu.SemaphoreType.DMA((4,))],
            moved=2 * width * (kdim + 4 * width) * 2,
            prefetch=2,
        )(where_fan, core_at, *gathered)
    else:
        where_fan = jnp.zeros((3, count), jnp.int32)
        own = [lax.all_gather(piece, "fsdp", axis=0, tiled=True) for piece in pieces]
        other = [other_core(value) for value in own]

        def joined(parts):
            one, two, three = parts
            return (
                jnp.concatenate([one[:, width : width + 256], two[:, half:], three[:, half:]], axis=1),
                jnp.stack([one[:, :half], one[:, half:width], two[:, :half], three[:, :half]], axis=1),
                one[:, width + 256 :],
            )

        own_e, own_a, small = joined(own)
        other_e, other_a, small_other = joined(other)
        kernel_t = jnp.concatenate(halves(own_e, other_e, core), axis=1)
        attn_low = jnp.stack(halves(own_a, other_a, core), axis=2).reshape(width, 4 * width)
        gain_rows = jnp.pad(small[:, cells_count : cells_count + 6].astype(FL).T, ((0, 2), (0, 0)))
        number = (small[:, cells_count + 6] + small_other[:, cells_count + 6]).astype(FL)
        image_count = (jnp.sum(number) / rows)[None, None]

    table = np.zeros((tokens, SMALL), np.float32)
    table[:, :cells_count] = grid_matrix()
    high = table.astype(jnp.bfloat16)
    low = (table - high.astype(np.float32)).astype(jnp.bfloat16)
    start, normed_t = call(
        embed_kernel_body,
        (images,),
        [
            pl.BlockSpec((tokens, kdim), lambda b: (b, 0)),
            whole((width, kdim)),
            whole((tokens, 2 * SMALL)),
            whole((width, SMALL)),
            whole((8, width)),
        ],
        [
            pl.BlockSpec((tokens, width), lambda b: (b, 0)),
            pl.BlockSpec((width, tokens), lambda b: (0, b)),
        ],
        [sds((total, width), FL), sds((width, total), BF)],
        flops=2 * total * kdim * width,
        moved=total * kdim * 2 + kdim * width * 2 + total * width * 6,
    )(reduced, kernel_t, jnp.asarray(np.concatenate([high, low], axis=1)), small, gain_rows)

    by_image = pl.BlockSpec((tokens, width), lambda b: (b, 0))
    by_lane = pl.BlockSpec((width, tokens), lambda b: (0, b))
    qkv_spec = pl.BlockSpec((3 * width, tokens), lambda b: (0, b))
    lse_spec = pl.BlockSpec((1, lse_rows, tokens), lambda b: (b, 0, 0))
    qkv_t, mixed_t, lse, middle, normed_two, two_t = call(
        attend_kernel,
        (images,),
        [by_lane, by_image, whole((width, 4 * width)), whole((8, width))],
        [qkv_spec, by_lane, lse_spec, by_image, by_image, by_lane],
        [
            sds((3 * width, total), BF),
            sds((width, total), BF),
            sds((images, lse_rows, tokens), FL),
            sds((total, width), FL),
            sds((total, width), BF),
            sds((width, total), BF),
        ],
        scratch=[pltpu.VMEM((3 * width, width), BF)],
        flops=2 * total * width * (4 * width + 2 * tokens),
        moved=total * width * 20 + 8 * width * width,
    )(normed_t, start, attn_low, gain_rows)
    rest_own, normed_two = tie(rest_own, normed_two)
    rest_other = other_core(rest_own)

    col = lambda offset: pl.BlockSpec((width, TILE), lambda j: (0, offset + j))
    tile_spec = pl.BlockSpec((total, TILE), lambda j: (0, j))
    final = middle
    hidden, slope = [], []
    for part in (rest_own, rest_other):
        final, one, two = call(
            partial(mlp_kernel, chunk),
            (tiles,),
            [whole((total, width)), whole((total, width)), col(0), col(tiles)],
            [whole((total, width)), tile_spec, tile_spec],
            [sds((total, width), FL), sds((total, fhalf), BF), sds((total, fhalf), BF)],
            flops=4 * total * fhalf * width,
            moved=total * width * 10 + 4 * fhalf * width + 4 * total * fhalf,
        )(final, normed_two, part, part)
        hidden.append(one)
        slope.append(two)

    labels_col = jnp.pad(labels, (0, 8 - images), constant_values=-1)[:, None]
    head_spec = pl.BlockSpec((width, chalf), lambda i, c: (0, ffw // chalf))
    d_final, e_low, e_t, head_own, head_other, four_grads, loss_part = call(
        partial(head_kernel, images, classes),
        (1,),
        [
            whole((total, width)),
            whole((8, 1)),
            whole((1, 1)),
            whole((8, width)),
            head_spec,
            head_spec,
        ],
        [
            whole((total, width)),
            whole((total, width)),
            whole((width, total)),
            whole((width, chalf)),
            whole((width, chalf)),
            whole((8, width)),
            whole((8, 128)),
        ],
        [
            sds((total, width), FL),
            sds((total, width), BF),
            sds((width, total), BF),
            sds((width, chalf), FL),
            sds((width, chalf), BF),
            sds((8, width), FL),
            sds((8, 128), FL),
        ],
        flops=64 * total * width,
        moved=total * width * 10 + width * chalf * 12,
        prefetch=1,
    )(core_at, final, labels_col, image_count, gain_rows, rest_own, rest_other)
    head_got = other_core(head_other)

    d_normed_part, down_other, up_other = call(
        partial(mlp_back_other_kernel, chunk),
        (tiles,),
        [
            whole((total, width)),
            whole((width, total)),
            whole((width, total)),
            tile_spec,
            tile_spec,
            col(0),
            col(tiles),
        ],
        [whole((total, width)), col(0), col(0)],
        [sds((total, width), FL), sds((width, fhalf), BF), sds((width, fhalf), BF)],
        scratch=[pltpu.VMEM((total, TILE), BF)],
        flops=8 * total * fhalf * width,
        moved=total * width * 8 + 8 * fhalf * width + 4 * total * fhalf,
    )(e_low, e_t, two_t, hidden[1], slope[1], rest_other, rest_other)
    down_got = other_core(down_other)
    up_got = other_core(up_other)

    colc = lambda offset: pl.BlockSpec((width, TILE), lambda j, *c: (0, offset + j))
    tilec = pl.BlockSpec((total, TILE), lambda j, *c: (0, j))
    d_pre, d_middle, o_low, grads_in, out_other = call(
        partial(mlp_back_own_kernel, chunk, tokens),
        (tiles,),
        [
            whole((total, width)),
            whole((total, width)),
            tilec,
            colc(0),
            colc(tiles),
            whole((total, width)),
            whole((total, width)),
            whole((8, width)),
            whole((width, total)),
            whole((8, width)),
        ],
        [
            tilec,
            whole((total, width)),
            whole((total, width)),
            whole((8, width)),
            whole((width, half)),
        ],
        [
            sds((total, fhalf), BF),
            sds((total, width), FL),
            sds((total, width), BF),
            sds((8, width), FL),
            sds((width, half), BF),
        ],
        scratch=[pltpu.VMEM((total, width), FL)],
        flops=4 * total * fhalf * width + 2 * total * width * half,
        moved=total * width * 22 + 4 * fhalf * width + 4 * total * fhalf,
        prefetch=1,
    )(core_at, d_normed_part, e_low, slope[0], rest_own, rest_own, middle, d_final, gain_rows, mixed_t, four_grads)
    out_got = other_core(out_other)

    def split_shapes(size):
        if aligned:
            return [sds((count // 2, rows, size), BF)] * 2
        return [sds((width, size), BF)]

    def split_specs(size):
        return [whole(item.shape) for item in split_shapes(size)]

    if aligned:
        down_order = order_of(count, [1, 4, 2, 8])
        up_order = order_of(count, [2, 1, 4, 8])
        rest_order = order_of(count, [4, 2, 1, 8])
        where_down = (me ^ jnp.array(relative_masks(down_order), jnp.int32))[None]
        where_up = jnp.stack(
            [me ^ jnp.array(relative_masks(order), jnp.int32) for order in (up_order, rest_order)]
        )
    else:
        where_down, where_up = jnp.zeros((1, count), jnp.int32), jnp.zeros((2, count), jnp.int32)
    down_parts = call(
        partial(down_grad_kernel, aligned, rows),
        (tiles,),
        [whole((width, total)), tilec, colc(0)],
        split_specs(fhalf),
        split_shapes(fhalf),
        scratch=[pltpu.VMEM((width, TILE), FL)],
        flops=2 * total * fhalf * width,
        moved=total * width * 2 + 4 * fhalf * width + 2 * total * fhalf,
        prefetch=1,
    )(where_down, e_t, hidden[0], down_got)
    rest_width = chalf + half
    up_parts = call(
        partial(up_grad_kernel, aligned, rows),
        (tiles,),
        [
            whole((width, total)),
            tilec,
            colc(0),
            whole((width, total)),
            whole((total, width)),
            whole((width, half)),
            whole((width, chalf)),
            whole((width, chalf)),
        ],
        split_specs(fhalf) + split_specs(rest_width),
        split_shapes(fhalf) + split_shapes(rest_width),
        scratch=[pltpu.VMEM((width, TILE), FL)],
        flops=2 * total * fhalf * width + 2 * total * width * half,
        moved=total * width * 6 + 4 * fhalf * width + 2 * total * fhalf + width * chalf * 6,
        prefetch=2,
    )(where_up, core_at, two_t, d_pre, up_got, mixed_t, o_low, out_got, head_own, head_got)

    pair = max(images // 2, 1)
    shift = lambda k: [
        pl.BlockSpec((tokens, width), lambda b: (b + k, 0)),
        pl.BlockSpec((3 * width, tokens), lambda b: (0, b + k)),
        pl.BlockSpec((1, lse_rows, tokens), lambda b: (b + k, 0, 0)),
        pl.BlockSpec((width, tokens), lambda b: (0, b + k)),
    ]

    def attend_back(k, final, grads_in, o_low, held=()):
        image_spec, qkvs, lses, lanes = shift(k)
        sums = sds((width, SMALL), FL) if final else sds((tokens, width), FL)
        return pl.pallas_call(
            partial(attend_back_kernel, cells_count, final),
            grid=(pair,),
            in_specs=[
                image_spec,
                whole((width, 4 * width)),
                qkvs,
                lses,
                image_spec,
                image_spec,
                whole((8, width)),
                whole((tokens, SMALL)),
                whole((8, width)),
            ]
            + ([whole((tokens, width))] + [pl.BlockSpec(memory_space=pl.ANY)] * 2 if final else []),
            out_specs=[qkvs, lanes, whole(sums.shape), whole((8, width))],
            out_shape=[
                sds((3 * width, total), BF),
                sds((width, total), BF),
                sums,
                sds((8, width), FL),
            ],
            scratch_shapes=[
                pltpu.VMEM((width, tokens), BF),
                pltpu.VMEM((tokens, width), FL),
                pltpu.VMEM((8, width), FL),
            ],
            input_output_aliases={10: 0, 11: 1} if final else {},
            compiler_params=pltpu.CompilerParams(vmem_limit_bytes=LIMIT),
            cost_estimate=pl.CostEstimate(
                flops=total * width * (4 * width + 5 * tokens),
                bytes_accessed=total * width * 12 + 8 * width * width,
                transcendentals=0,
            ),
        )(o_low, attn_low, qkv_t, lse, d_middle, start, gain_rows, jnp.asarray(table), grads_in, *held)

    def send_on(states, *others):
        gots = [partner(send, count, order[0]) for keep, send, order in states]

        def arrive(*others):
            gots_now = tie(*gots, *others)
            after = [
                (*add_halves(keep, got), order[1:])
                for (keep, send, order), got in zip(states, gots_now)
            ]
            return after, gots_now[len(gots) :]

        return arrive

    if aligned:
        o_one, *up_parts = tie(o_low, *up_parts)
        flow_down = [(*down_parts, down_order)]
        flow_up = [(*up_parts[:2], up_order), (*up_parts[2:], rest_order)]
        arrive_down, arrive_up = send_on(flow_down), send_on(flow_up)
    else:
        o_one = o_low
    d_qkv_t, s_t, sum_one, grads_one = attend_back(0, False, grads_in, o_one)
    if aligned:
        flow_down, (d_qkv_t, s_t) = arrive_down(d_qkv_t, s_t)
        arrive_down = send_on(flow_down)
    d_qkv_t, s_t, d_small, ignored = attend_back(
        pair, True, grads_one, o_one, (sum_one, d_qkv_t, s_t)
    )
    small_got = other_core(d_small)
    if aligned:
        flow_up, (d_qkv_t,) = arrive_up(d_qkv_t)
        arrive_up = send_on(flow_up)
        flow_down, (d_qkv_t,) = arrive_down(d_qkv_t)
        arrive_down = send_on(flow_down)
    attn_other = call(
        partial(plain_grad_kernel, True),
        (3,),
        [
            whole((width, total)),
            pl.BlockSpec((half, total), lambda j, c: (2 * j + 1 - c[0], 0)),
        ],
        pl.BlockSpec((width, half), lambda j, c: (0, j)),
        sds((width, 3 * half), BF),
        flops=6 * total * half * width,
        moved=total * width * 2 + 6 * total * half + 6 * width * half,
        prefetch=1,
    )(core_at, normed_t, d_qkv_t)
    attn_got = other_core(attn_other)
    s_other, ignored = tie(s_t, attn_other)
    kernel_other = call(
        partial(plain_grad_kernel, False),
        (3,),
        [
            whole((width, total)),
            pl.BlockSpec((total, third), lambda j, c: (0, 3 * (1 - c[0]) + j)),
        ],
        pl.BlockSpec((width, third), lambda j, c: (0, j)),
        sds((width, khalf), BF),
        flops=2 * total * khalf * width,
        moved=total * width * 2 + 2 * total * khalf + 2 * width * khalf,
        prefetch=1,
    )(core_at, s_other, reduced)
    kernel_got = other_core(kernel_other)
    if aligned:
        flow_up, (s_t,) = arrive_up(s_t)
        arrive_up = send_on(flow_up)
        flow_down, (s_t,) = arrive_down(s_t)
        arrive_down = send_on(flow_down)

    tail_widths = (half + third + SMALL, half + third, half + third)
    tail_parts = call(
        partial(tail_grad_kernel, aligned, rows),
        (3,),
        [
            whole((width, total)),
            whole((width, total)),
            pl.BlockSpec((half, total), lambda j, w, c: (2 * j + c[0], 0)),
            pl.BlockSpec((total, third), lambda j, w, c: (0, 3 * c[0] + j)),
            pl.BlockSpec((width, half), lambda j, w, c: (0, j)),
            pl.BlockSpec((width, third), lambda j, w, c: (0, j)),
            whole((width, SMALL)),
            whole((width, SMALL)),
        ],
        [spec for size in tail_widths for spec in split_specs(size)],
        [shape for size in tail_widths for shape in split_shapes(size)],
        scratch=[pltpu.VMEM((width, max(third, half, SMALL)), FL)],
        flops=2 * total * (3 * half + khalf) * width,
        moved=total * width * 4 + 2 * total * (3 * half + khalf) + 4 * width * (3 * half + khalf),
        prefetch=2,
    )(where_fan, core_at, normed_t, s_t, d_qkv_t, reduced, attn_got, kernel_got, d_small, small_got)
    if aligned:
        flow_up, tail_parts = arrive_up(*tail_parts)
        flow_down, tail_parts = arrive_down(*tail_parts)
        states = flow_down + flow_up + [
            (tail_parts[2 * k], tail_parts[2 * k + 1], fan_orders[k]) for k in range(3)
        ]
        while any(order for keep, send, order in states):
            live = [k for k, state in enumerate(states) if state[2]]
            gone, ignored = send_on([states[k] for k in live])()
            for k, state in zip(live, gone):
                states[k] = state
        g_down, g_up, g_rest, *g_tail = [state[0] for state in states]
    else:
        g_down, g_up, g_rest, *g_tail = [
            lax.psum_scatter(part, "fsdp", scatter_dimension=0, tiled=True)
            for part in (*down_parts, *up_parts, *tail_parts)
        ]

    own_shards = [*g_tail, g_down, g_up, g_rest]
    other_shards = [other_core(item) for item in own_shards]
    sums = call(
        partial(square_kernel, half + third),
        (1,),
        [whole((8, 128))] + [whole(item.shape) for item in own_shards],
        whole((8, 128)),
        sds((8, 128), FL),
        moved=2 * rows * (kdim + 2 * width + ffw + chalf),
    )(loss_part, *own_shards)
    sums = sum_everywhere(sums, count)
    grad_norm = jnp.sqrt(sums[0, 0])
    loss_sum = sums[0, 1]
    tables = (embed_kernel.T, pos_base.T, attn_weight, mlp_weight, head_weight)
    firsts = (embed_first.T, pos_first.T, attn_first, mlp_first, head_first)
    seconds = (embed_second.T, pos_second.T, attn_second, mlp_second, head_second)
    block = 16 if rows % 16 == 0 else rows
    by_rows = lambda item: pl.BlockSpec((block, item.shape[1]), lambda i, c: (i, 0))
    olds = (*tables, *firsts, *seconds)
    lows = [sds(tables[k].shape, BF) for k in (0, 2, 3, 4)]
    outs = call(
        partial(update_kernel, cells_count, classes),
        (rows // block,),
        [whole((8, 128))] + [by_rows(item) for item in (*own_shards, *other_shards, *olds)],
        [by_rows(item) for item in (*olds, *lows)],
        [sds(item.shape, FL) for item in olds] + lows,
        flops=rows * width,
        moved=rows * (kdim + 4 * width + 2 * ffw + classes) * 30,
        prefetch=1,
    )(core_at, sums, *own_shards, *other_shards, *olds)
    new, low = outs[:15], outs[15:]
    tiny = g_tail[0][:, half + third + cells_count : half + third + cells_count + 6].astype(FL).T
    gain_new = adam_step(
        gains, gains_first, gains_second, tiny * jnp.minimum(1.0, CLIP / grad_norm), RATE_TABLE, 0.0
    )
    sets = [
        (new[5 * k].T, new[5 * k + 1].T, gain_new[k], *new[5 * k + 2 : 5 * k + 5]) for k in range(3)
    ]
    return (
        loss_sum,
        image_count[0, 0],
        grad_norm,
        *sets[0],
        *sets[1],
        *sets[2],
        low[0].T,
        *low[1:],
    )


def solution(mesh):
    data = P(("rep", "fsdp"))
    columns, rows = P(None, "fsdp"), P("fsdp", None)
    table = (columns, columns, columns, rows, rows, rows)
    in_specs = (P(("rep", "fsdp"), None, None), data, data, P()) + table * 3
    out_specs = (P(), P(), P()) + table * 3 + (columns, rows, rows, rows)
    return jax.shard_map(
        partial(body, mesh.shape["fsdp"]),
        mesh=mesh,
        in_specs=in_specs,
        out_specs=out_specs,
        check_vma=False,
    )
```

```python
from functools import partial

import jax
import jax.numpy as jnp
import numpy as np
from jax import lax
from jax.experimental import pallas as pl
from jax.experimental.pallas import tpu as pltpu
from jax.sharding import PartitionSpec as P

HEAD_DIM = 64
BASE = 32
GRID0 = 7
MAXP = 24
GRID = 16
STEP = 10
SIDES = (10, 15, 24)

NORM_EPS = 1e-06
CLIP = 0.02
BETA_ONE = 0.9
BETA_TWO = 0.999
ADAM_EPS = 1e-08
RATE = 0.1
RATE_TABLE = 1.0
DECAY = 0.05
BF = jnp.bfloat16
FL = jnp.float32
SMALL = 128
TILE = 512
LIMIT = 40 * 1024 * 1024
MOST = 58 * 1024 * 1024


def grid_matrix():
    target = (np.arange(GRID, dtype=np.float32) + np.float32(0.5)) * (GRID0 / GRID) - 0.5
    target = np.clip(target, 0.0, GRID0 - 1.0)
    source = np.arange(GRID0, dtype=np.float32)
    line = np.maximum(0.0, 1.0 - np.abs(target[:, None] - source[None, :]))
    return (line[:, None, :, None] * line[None, :, None, :]).reshape(GRID * GRID, GRID0 * GRID0)


def adam_step(weight, first_old, second_old, gradient, step_rate, decay_rate):
    first_new = BETA_ONE * first_old + (1.0 - BETA_ONE) * gradient
    second_new = BETA_TWO * second_old + (1.0 - BETA_TWO) * gradient * gradient
    first_hat = first_new / (1.0 - BETA_ONE**STEP)
    second_hat = second_new / (1.0 - BETA_TWO**STEP)
    weight_new = weight - step_rate * (
        first_hat / (jnp.sqrt(second_hat) + ADAM_EPS) + decay_rate * weight
    )
    return (weight_new, first_new, second_new)


def partner(value, count, mask):
    return lax.ppermute(value, "fsdp", [(i, i ^ mask) for i in range(count)])


def other_core(value):
    return lax.ppermute(value, "rep", [(0, 1), (1, 0)])


def bits_of(count):
    return [1 << k for k in range(count.bit_length() - 1)]


def order_of(count, preferred):
    return preferred if sorted(preferred) == bits_of(count) else bits_of(count)


def relative_masks(order):
    masks = [0]
    for mask in reversed(order):
        masks = masks + [held ^ mask for held in masks]
    return masks


def tie(*values):
    return lax.optimization_barrier(values)


def gather_relative(shards, count, orders, late, late_step):
    held = [shard[None] for shard in shards]
    for step in range(len(orders[0]) - 1, 0, -1):
        got = [partner(value, count, order[step]) for value, order in zip(held, orders)]
        if step == late_step:
            *got, late = tie(*got, late)
        else:
            got = tie(*got)
        held = [jnp.concatenate(pair, axis=0) for pair in zip(held, got)]
    return held, [partner(value, count, order[0]) for value, order in zip(held, orders)], late


def add_halves(keep, got):
    half = keep.shape[0] // 2
    if half == 0:
        return (keep[0].astype(FL) + got[0].astype(FL)).astype(BF), None
    return tuple(
        (keep[rows].astype(FL) + got[rows].astype(FL)).astype(BF)
        for rows in (slice(0, half), slice(half, None))
    )


def axis_of(mask, held_masks):
    return held_masks.index(mask)


def side_of(value, mask, held_masks, me, other):
    if me is None:
        return lax.index_in_dim(value, int(other), axis_of(mask, held_masks), keepdims=False)
    bit = jnp.where((me & mask) != 0, 1, 0)
    at = 1 - bit if other else bit
    return lax.dynamic_index_in_dim(value, at, axis_of(mask, held_masks), keepdims=False)


def split_sides(parts, count, order, me):
    held = bits_of(count)[::-1]
    shaped = [part.reshape((2,) * len(held) + (part.shape[0] // count, -1)) for part in parts]
    sides = []
    for other in (False, True):
        pieces = []
        for value in shaped:
            for number, mask in enumerate(order):
                if number == 0:
                    value = side_of(value, mask, held, me, other)
            pieces.append(value)
        sides.append(jnp.concatenate(pieces, axis=-1))
    return sides[0], sides[1], [mask for mask in held if mask != order[0]]


def step_sides(keep, got, held, order, me):
    if not order:
        total = keep.astype(FL) + got.astype(FL)
        return total.astype(BF), None, held
    mask = order[0]
    sides = [
        (
            side_of(keep, mask, held, me, other).astype(FL)
            + side_of(got, mask, held, me, other).astype(FL)
        ).astype(BF)
        for other in (False, True)
    ]
    return sides[0], sides[1], [bit for bit in held if bit != mask]


def sum_everywhere(value, count):
    value = value + other_core(value)
    bits = bits_of(count)
    while bits:
        pair, bits = bits[:2], bits[2:]
        got = [partner(value, count, mask) for mask in (*pair, sum(pair))[: 2 * len(pair) - 1]]
        value = value + got[0]
        if len(pair) == 2:
            value = value + (got[1] + got[2])
    return value


def halves(own, other, core):
    return jnp.where(core == 0, own, other), jnp.where(core == 0, other, own)


def dot(a, b):
    return lax.dot_general(a, b, (((1,), (0,)), ((), ())), preferred_element_type=FL)


def dot_t(a, b):
    return lax.dot_general(a, b, (((1,), (1,)), ((), ())), preferred_element_type=FL)


def t_dot(a, b):
    return lax.dot_general(a, b, (((0,), (0,)), ((), ())), preferred_element_type=FL)


def call(kernel, grid, in_specs, out_specs, out_shape, scratch=(), prefetch=0, limit=LIMIT):
    return pl.pallas_call(
        kernel,
        grid_spec=pltpu.PrefetchScalarGridSpec(
            num_scalar_prefetch=prefetch,
            grid=grid,
            in_specs=in_specs,
            out_specs=out_specs,
            scratch_shapes=list(scratch),
        ),
        out_shape=out_shape,
        compiler_params=pltpu.CompilerParams(vmem_limit_bytes=limit),
        cost_estimate=pl.CostEstimate(flops=1, bytes_accessed=1, transcendentals=0),
    )


def whole(shape):
    zeros = (0,) * len(shape)
    return pl.BlockSpec(shape, lambda *a: zeros)


def sds(shape, dtype):
    return jax.ShapeDtypeStruct(shape, dtype)


def norm_parts(values_in):
    row_mean = jnp.mean(values_in, axis=-1, keepdims=True)
    centered = values_in - row_mean
    row_var = jnp.mean(centered * centered, axis=-1, keepdims=True)
    inverse = lax.rsqrt(row_var + NORM_EPS)
    return centered * inverse, inverse


def norm_back(xhat, inverse, gain, dy):
    gained = dy * gain
    one = jnp.mean(gained, axis=-1, keepdims=True)
    two = jnp.mean(gained * xhat, axis=-1, keepdims=True)
    return inverse * (gained - one - xhat * two)


def normal_cdf(x):
    return 0.5 + 0.5 * lax.erf(x * 0.7071067811865476), jnp.exp(-0.5 * x * x)


def prepare_kernel(cells, core_ref, labels_ref, embed, pos, gains, attn, mlp, head, one, two, three, rest, held):
    core = core_ref[0]
    rows, width = attn.shape[0], attn.shape[1] // 4
    half, khalf, fhalf = width // 2, embed.shape[1] // 2, mlp.shape[1] // 4

    def cols(ref, base, step, size):
        return ref[:, pl.ds(pl.multiple_of(base + core * step, 128), size)].astype(BF)

    first, other = khalf - 2 * (khalf - 256) // 2, (khalf - 256) // 2
    one[:, :half] = cols(attn, 0, half, half)
    one[:, half : 2 * half] = cols(attn, width, half, half)
    one[:, 2 * half : 2 * half + first] = cols(embed, 0, khalf, first)
    two[:, :half] = cols(attn, 2 * width, half, half)
    two[:, half:] = cols(embed, first, khalf, other)
    three[:, :half] = cols(attn, 3 * width, half, half)
    three[:, half:] = cols(embed, first + other, khalf, other)
    rest[:, :fhalf] = cols(mlp, 0, fhalf, fhalf)
    rest[:, fhalf : 2 * fhalf] = cols(mlp, 2 * fhalf, fhalf, fhalf)
    chalf = rest.shape[1] - 2 * fhalf
    classes = head.shape[1]
    low_half = head[:, :chalf]
    high_half = jnp.concatenate(
        [head[:, chalf:classes], jnp.zeros((rows, 2 * chalf - classes), FL)], axis=1
    )
    rest[:, 2 * fhalf :] = jnp.where(core == 0, low_half, high_half).astype(BF)
    total = jnp.int32(0)
    for image in range(labels_ref.shape[0]):
        total = total + jnp.where(labels_ref[image] >= 0, 1, 0)
    held[...] = jnp.zeros(held.shape, FL)
    held[cells : cells + 6, :rows] = gains[...]
    held[cells + 6 : cells + 7, :] = jnp.full((1, held.shape[1]), total.astype(FL))
    turned = held[...].T
    one[:, 2 * half + first :] = turned[:rows].astype(BF)
    one[:, 2 * half + first : 2 * half + first + cells] = pos[...].astype(BF)


def reduce_kernel(kind_ref, core_ref, pixels, resize, own, other):
    kind = kind_ref[pl.program_id(0)]
    side = jnp.where(kind == 0, SIDES[0], jnp.where(kind == 1, SIDES[1], SIDES[2]))
    feats, base = resize.shape[1], resize.shape[2]
    place = lax.broadcasted_iota(jnp.int32, (feats, base), 0)
    chosen = jnp.where(place < side * side, resize[0].astype(FL), 0.0).astype(BF)
    factor = 0.25 / side.astype(FL)
    half = own.shape[1]
    values = []
    for channel in range(3):
        part = pixels[0, channel * feats : (channel + 1) * feats, :]
        values.append((t_dot(part, chosen) * factor).astype(BF))
    for core, sides in enumerate(((own, other), (other, own))):
        @pl.when(core_ref[0] == core)
        def store(sides=sides):
            for channel, value in enumerate(values):
                lo, hi = channel * base, (channel + 1) * base
                for number, side in enumerate(sides):
                    left, right = max(lo, number * half), min(hi, (number + 1) * half)
                    if left < right:
                        side[:, left - number * half : right - number * half] = value[
                            :, left - lo : right - lo
                        ]


def start_pieces(plan, where_ref, core, pieces, targets, sems):
    rows, half = pieces[0].shape[1], pieces[0].shape[0]

    def one_block(p, ignored):
        for stream in range(3):
            for top in range(2):
                at = pl.multiple_of(where_ref[stream, p + top * half] * rows, rows)
                for swapped in range(2):
                    source = pieces[4 * stream + 2 * swapped + top]
                    for src, size, target, base, step in plan[stream]:
                        if target == 2:
                            dst = targets[2 + swapped].at[pl.ds(at, rows), :]
                            sem = sems.at[2 + swapped]
                        else:
                            side = 1 - core if swapped else core
                            if target == 0:
                                side = swapped
                            col = pl.multiple_of(base + side * step, 128)
                            dst = targets[target].at[pl.ds(at, rows), pl.ds(col, size)]
                            sem = sems.at[target]
                        pltpu.make_async_copy(
                            source.at[p, :, pl.ds(src, size)], dst, sem
                        ).start()
        return ignored

    lax.fori_loop(0, half, one_block, 0)


def forward_kernel(plan, cells_count, where_ref, core_ref, *refs):
    joined = plan is not None
    weights, refs = (refs[:12], refs[12:]) if joined else (refs[:6], refs[6:])
    (reduced, reduced_other, cells), refs = refs[:3], refs[3:]
    start, normed_t, qkv_t, mixed_t, lse, middle, normed_two = refs[:7]
    refs = refs[7:]
    if joined:
        attn, gains, counts, turned, scores, probs, kernel_t, small, small_other, sems = refs
        targets = (kernel_t, attn, small, small_other)
    else:
        kernel_t, attn, small, small_other, gains, counts = weights
        turned, scores, probs = refs
    width = normed_t.shape[0]
    heads = width // HEAD_DIM
    first_image = pl.program_id(0) == 0

    if joined:
        @pl.when(first_image)
        def arrive():
            start_pieces(plan, where_ref, core_ref[0], weights, targets, sems)
            for number in (0, 2, 3):
                pltpu.make_async_copy(targets[number], targets[number], sems.at[number]).wait()
            rows = weights[0].shape[1]
            on_side = small[...].astype(FL).T
            gains[0:6, :] = on_side[cells_count : cells_count + 6, :]
            gains[6:8, :] = jnp.zeros((2, width), FL)
            at = slice(cells_count + 6, cells_count + 7)
            number = on_side[at, :] + small_other[...].astype(FL).T[at, :]
            counts[...] = jnp.sum(number, axis=1, keepdims=True) * (1.0 / rows)

    posemb = dot_t(cells[:, :SMALL], small[...]) + dot_t(cells[:, SMALL:], small[...])
    khalf = reduced.shape[1]
    x = dot_t(reduced[...], kernel_t[:, :khalf]) + dot_t(reduced_other[...], kernel_t[:, khalf:])
    x = x + posemb
    start[...] = x
    xhat, ignored = norm_parts(x)
    normed_t[...] = (xhat * gains[0:1, :] + gains[1:2, :]).astype(BF).T

    @pl.when(first_image)
    def turn():
        if joined:
            pltpu.make_async_copy(attn, attn, sems.at[1]).wait()
        for at in range(0, 3 * width, 256):
            turned[at : at + 256, :] = attn[:, at : at + 256].T

    qkv_t[...] = dot(turned[...], normed_t[...]).astype(BF)
    spans = [slice(head * HEAD_DIM, (head + 1) * HEAD_DIM) for head in range(heads)]
    for head, span in enumerate(spans):
        q = qkv_t[span, :] * jnp.asarray(HEAD_DIM**-0.5, BF)
        scores[head] = t_dot(qkv_t[width + span.start : width + span.stop, :], q)
    shares = []
    for head in range(heads):
        top = jnp.max(scores[head], axis=0, keepdims=True)
        expd = jnp.exp(scores[head] - top)
        total = jnp.sum(expd, axis=0, keepdims=True)
        probs[head] = expd.astype(BF)
        lse[0, head : head + 1, :] = top + jnp.log(total)
        shares.append(1.0 / total)
    for head, span in enumerate(spans):
        v = qkv_t[2 * width + span.start : 2 * width + span.stop, :]
        mixed_t[span, :] = (dot(v, probs[head]) * shares[head]).astype(BF)
    lse[0, heads:, :] = jnp.zeros((lse.shape[1] - heads, lse.shape[2]), FL)
    x = start[...] + t_dot(mixed_t[...], attn[:, 3 * width :])
    middle[...] = x
    xhat, ignored = norm_parts(x)
    normed_two[...] = (xhat * gains[2:3, :] + gains[3:4, :]).astype(BF)


def mlp_tile(chunk, normed_two, up, down, final, hidden, slope):
    count = normed_two.shape[0] // chunk
    rows = lambda i: slice(i * chunk, (i + 1) * chunk)
    pre, low = {0: dot(normed_two[rows(0), :], up[...])}, {}
    for i in range(count + 1):
        if i + 1 < count:
            pre[i + 1] = dot(normed_two[rows(i + 1), :], up[...])
        if i < count:
            value = pre.pop(i)
            cdf, bell = normal_cdf(value)
            low[i] = (value * cdf).astype(BF)
            hidden[rows(i), :] = low[i]
            slope[rows(i), :] = (cdf + value * bell * 0.3989422804014327).astype(BF)
        if i > 0:
            final[rows(i - 1), :] += dot_t(low.pop(i - 1), down[...])


def mlp_kernel(chunk, held, normed_two, up, down, final, hidden, slope):
    @pl.when(pl.program_id(0) == 0)
    def first():
        final[...] = held[...]

    mlp_tile(chunk, normed_two, up, down, final, hidden, slope)


def head_part(
    images, classes, core, final, labels, image_count, gains, own, other,
    d_final, e_low, own_grad, other_grad, row_grads, loss,
):
    tokens = final.shape[0] // images
    width = final.shape[1]
    chalf = own.shape[1]
    gain = gains[4:5, :]
    places = lax.broadcasted_iota(jnp.int32, (8, width), 0)
    means = jnp.zeros((8, width), FL)
    for image in range(images):
        xhat, ignored = norm_parts(final[image * tokens : (image + 1) * tokens, :])
        mean_row = jnp.mean(xhat, axis=0, keepdims=True)
        means = jnp.where(places == image, mean_row, means)
    pooled = jnp.where(places < images, means * gain + gains[5:6, :], 0.0).astype(BF)
    logits = [dot(pooled, own[...]), dot(pooled, other[...])]
    lane = lax.broadcasted_iota(jnp.int32, (8, chalf), 1)
    kinds = [lane + core * chalf, lane + (1 - core) * chalf]
    masked = [jnp.where(kinds[k] < classes, logits[k], -1e30) for k in range(2)]
    top = jnp.maximum(
        jnp.max(masked[0], axis=1, keepdims=True), jnp.max(masked[1], axis=1, keepdims=True)
    )
    expd = [jnp.where(kinds[k] < classes, jnp.exp(masked[k] - top), 0.0) for k in range(2)]
    total = jnp.sum(expd[0], axis=1, keepdims=True) + jnp.sum(expd[1], axis=1, keepdims=True)
    log_total = top + jnp.log(total)
    named = labels[...]
    onehot = [(kinds[k] == named).astype(FL) for k in range(2)]
    target = jnp.sum(onehot[0] * logits[0], axis=1, keepdims=True) + jnp.sum(
        onehot[1] * logits[1], axis=1, keepdims=True
    )
    counted = (named >= 0).astype(FL)
    losses = counted * (log_total - target)
    loss[...] = jnp.broadcast_to(jnp.sum(losses, axis=0, keepdims=True), loss.shape)
    share = counted / image_count[...]
    d_logits = [((expd[k] / total - onehot[k]) * share).astype(BF) for k in range(2)]
    own_grad[...] = t_dot(pooled, d_logits[0])
    other_grad[...] = t_dot(pooled, d_logits[1]).astype(BF)
    d_pooled = dot_t(d_logits[0], own[...]) + dot_t(d_logits[1], other[...])
    row_grads[0:1, :] = jnp.sum(d_pooled * means, axis=0, keepdims=True)
    row_grads[1:2, :] = jnp.sum(d_pooled, axis=0, keepdims=True)
    row_grads[2:8, :] = jnp.zeros((6, width), FL)
    for image in range(images):
        rows = slice(image * tokens, (image + 1) * tokens)
        xhat, inverse = norm_parts(final[rows, :])
        dy = d_pooled[image : image + 1, :] * (1.0 / tokens)
        back = norm_back(xhat, inverse, gain, dy)
        d_final[rows, :] = back
        e_low[rows, :] = back.astype(BF)


def middle_kernel(
    images, classes, chunk, core_ref, held, normed_two, up, down, labels, image_count, gains,
    head_own, head_other, d_final, e_low, own_grad, other_grad, row_grads, loss, hidden, slope, final,
):
    step = pl.program_id(0)

    @pl.when(step == 0)
    def first():
        final[...] = held[...]

    mlp_tile(chunk, normed_two, up, down, final, hidden, slope)

    @pl.when(step == pl.num_programs(0) - 1)
    def head():
        head_part(
            images, classes, core_ref[0], final, labels, image_count, gains, head_own, head_other,
            d_final, e_low, own_grad, other_grad, row_grads, loss,
        )


def mm(a, b, dims):
    return lax.dot_general(a, b, (dims, ((), ())), preferred_element_type=FL)


def norm_two_kernel(
    core_ref, d_normed, middle, d_final, gains, mixed_t, four_grads,
    d_middle, o_low, row_grads, out_grad, sums, product,
):
    image = pl.program_id(0)
    width = middle.shape[1]
    half = width // 2
    xhat, inverse = norm_parts(middle[...])
    dy = d_normed[...]
    back = d_final[...] + norm_back(xhat, inverse, gains[2:3, :], dy)
    d_middle[...] = back
    o_low[...] = back.astype(BF)

    @pl.when(image == 0)
    def first():
        sums[...] = jnp.zeros(sums.shape, FL)
        product[...] = jnp.zeros(product.shape, FL)

    sums[0:1, :] += jnp.sum(dy * xhat, axis=0, keepdims=True)
    sums[1:2, :] += jnp.sum(dy, axis=0, keepdims=True)
    other = pl.multiple_of((1 - core_ref[0]) * half, 128)
    product[...] += dot(mixed_t[...], o_low[:, pl.ds(other, half)])

    @pl.when(image == pl.num_programs(0) - 1)
    def last():
        row_grads[0:2, :] = jnp.zeros((2, width), FL)
        row_grads[2:4, :] = sums[0:2, :]
        row_grads[4:6, :] = four_grads[0:2, :]
        row_grads[6:8, :] = jnp.zeros((2, width), FL)
        out_grad[...] = product[...].astype(BF)


def place(where_ref, row, rows, value, held, keep, send, col):
    size = value.shape[1]
    if send is None:
        keep[:, col : col + size] = value.astype(BF)
        return
    held[:, :size] = value
    half = keep.shape[0]
    for p in range(half):
        low = pl.multiple_of(where_ref[row, p] * rows, rows)
        high = pl.multiple_of(where_ref[row, half + p] * rows, rows)
        keep[p, :, col : col + size] = held[pl.ds(low, rows), :size].astype(BF)
        send[p, :, col : col + size] = held[pl.ds(high, rows), :size].astype(BF)


def split_outs(refs, aligned, number):
    if aligned:
        return [(refs[2 * k], refs[2 * k + 1]) for k in range(number)], refs[2 * number :]
    return [(refs[k], None) for k in range(number)], refs[number:]


class Loads:
    def __init__(self, sems):
        self.sems, self.targets = sems, []

    def add(self, target, *pairs):
        sem = self.sems.at[len(self.targets)]
        for source, place in pairs:
            pltpu.make_async_copy(source, place, sem).start()
        self.targets.append(target)
        return len(self.targets) - 1

    def wait(self, number):
        target = self.targets[number]
        pltpu.make_async_copy(target, target, self.sems.at[number]).wait()


def in_turn(products, stores):
    value = products[0]()
    for number, store in enumerate(stores):
        following = products[number + 1]() if number + 1 < len(products) else None
        store(value)
        value = following


def attend_back_kernel(
    cells_count, final, core_ref, o_low, attn, qkv_t, lse, d_middle, start, gains, cells, grads_in, *refs
):
    sum_in, refs = (refs[0], refs[1:]) if final else (None, refs)
    d_own, sent, sum_out, grads_out, d_qkv_t, d_mixed_t, summed, row_grads = refs[:8]
    scores, d_probs, probs, d_scores = refs[8:]
    width = o_low.shape[1]
    heads = width // HEAD_DIM
    image = pl.program_id(0)

    @pl.when(image == 0)
    def first():
        summed[...] = sum_in[...] if final else jnp.zeros(summed.shape, FL)
        row_grads[...] = grads_in[...]

    scale = HEAD_DIM**-0.5
    d_mixed_t[...] = dot_t(attn[:, 3 * width :], o_low[...]).astype(BF)
    spans = [slice(head * HEAD_DIM, (head + 1) * HEAD_DIM) for head in range(heads)]
    part = lambda ref, k, span: ref[k * width + span.start : k * width + span.stop, :]
    for head, span in enumerate(spans):
        q = part(qkv_t, 0, span) * jnp.asarray(scale, BF)
        scores[head] = t_dot(part(qkv_t, 1, span), q)
        d_probs[head] = t_dot(part(qkv_t, 2, span), d_mixed_t[span, :])
    for head in range(heads):
        soft = jnp.exp(scores[head] - lse[0, head : head + 1, :])
        probs[head] = soft.astype(BF)
        delta = jnp.sum(soft * d_probs[head], axis=0, keepdims=True)
        d_scores[head] = (soft * (d_probs[head] - delta)).astype(BF)
    for head, span in enumerate(spans):
        q = part(qkv_t, 0, span) * jnp.asarray(scale, BF)
        at = span.start
        d_qkv_t[at : at + HEAD_DIM, :] = (
            dot(part(qkv_t, 1, span), d_scores[head]) * scale
        ).astype(BF)
        d_qkv_t[width + at : width + at + HEAD_DIM, :] = dot_t(q, d_scores[head]).astype(BF)
        d_qkv_t[2 * width + at : 2 * width + at + HEAD_DIM, :] = dot_t(
            d_mixed_t[span, :], probs[head]
        ).astype(BF)
    half = width // 2
    for k in range(3):
        for ref, side in ((d_own, core_ref[0]), (sent, 1 - core_ref[0])):
            at = pl.multiple_of(k * width + side * half, 128)
            ref[k * half : (k + 1) * half, :] = d_qkv_t[pl.ds(at, half), :]
    dy = dot(attn[:, : 3 * width], d_qkv_t[...]).T
    xhat, inverse = norm_parts(start[...])
    back = d_middle[...] + norm_back(xhat, inverse, gains[0:1, :], dy)
    sent[3 * half :, :] = back.astype(BF).T
    summed[...] += back
    row_grads[0:1, :] += jnp.sum(dy * xhat, axis=0, keepdims=True)
    row_grads[1:2, :] += jnp.sum(dy, axis=0, keepdims=True)

    @pl.when(image == pl.num_programs(0) - 1)
    def last():
        grads_out[...] = row_grads[...]
        if not final:
            sum_out[...] = summed[...]
            return
        total = lax.dot_general(
            cells[...], summed[...], (((0,), (0,)), ((), ())),
            preferred_element_type=FL, precision=lax.Precision.HIGHEST,
        )
        summed[0:SMALL, :] = total
        summed[cells_count : cells_count + 6, :] = row_grads[0:6, :]
        sum_out[...] = summed[0:SMALL, :].T


def tail_grad_kernel(aligned, rows, spread, where_ref, core_ref, *refs):
    n_parts, own_parts, sent_parts, got_parts, r_parts = (
        refs[:2], refs[2:4], refs[4:6], refs[6:8], refs[8:10]
    )
    (small_hbm, small_got_hbm, mixed_hbm, o_hbm, out_hbm), refs = refs[10:15], refs[15:]
    d_parts, s_parts = (*own_parts, *got_parts), (*sent_parts, *got_parts)
    outs, scratch = split_outs(refs, aligned, 3)
    held, n_t, d_t, s_t, reduced, small, small_got, mixed_t, o_low, out_got, sems = scratch
    half, span = d_t.shape[1], own_parts[0].shape[1]
    width = s_t.shape[0]
    tokens = r_parts[0].shape[0]
    loads = Loads(sems)
    own = pl.multiple_of(core_ref[0] * half, 128)

    def load_tile(tile):
        at = pl.ds(tile * half, half)
        pairs = [(r_parts[k].at[:, at], reduced.at[tile, pl.ds(k * tokens, tokens), :]) for k in range(2)]
        return loads.add(reduced.at[tile], *pairs)

    def load_rows(tile):
        at = pl.ds(tile * half, half)
        pairs = [(d_parts[k].at[at, :], d_t.at[tile, :, pl.ds(k * span, span)]) for k in range(4)]
        return loads.add(d_t.at[tile], *pairs)

    out_ready = [
        loads.add(mixed_t, (mixed_hbm, mixed_t)),
        loads.add(o_low, (o_hbm.at[:, pl.ds(own, half)], o_low)),
        loads.add(out_got, (out_hbm, out_got)),
    ]
    tile_ready = [load_tile(0)]
    s_ready = loads.add(s_t, *[
            (s_parts[k].at[pl.ds(3 * half, width), :], s_t.at[:, pl.ds(k * span, span)])
            for k in range(4)
        ])
    tile_ready += [load_tile(1), load_tile(2), load_tile(3)]
    n_ready = loads.add(n_t, *[(n_parts[k], n_t.at[:, pl.ds(k * tokens, tokens)]) for k in range(2)])
    row_ready = [load_rows(0), load_rows(1), load_rows(2)]
    small_ready = [loads.add(small, (small_hbm, small)), loads.add(small_got, (small_got_hbm, small_got))]

    def put(stream, col, number, value):
        place(where_ref, stream, rows, value, held.at[number], *outs[stream], col)

    def out_product():
        for number in out_ready:
            loads.wait(number)
        return dot(mixed_t[...], o_low[...])

    def out_store(value):
        put(2, half, 0, value + out_got[...].astype(FL))

    def kernel_product(tile):
        if tile == 0:
            loads.wait(s_ready)
        loads.wait(tile_ready[tile])
        return dot(s_t[...], reduced[tile])

    def kernel_store(tile, value):
        for stream, col, lo, hi in spread[tile]:
            put(stream, col, (tile + 1) % 2, value[:, lo:hi])

    def attend_product(tile):
        if tile == 0:
            loads.wait(n_ready)
        loads.wait(row_ready[tile])
        return dot_t(n_t[...], d_t[tile])

    def attend_store(tile, value):
        put(tile, 0, (tile + 1) % 2, value)

    in_turn(
        [out_product]
        + [partial(kernel_product, tile) for tile in range(4)]
        + [partial(attend_product, tile) for tile in range(3)],
        [out_store]
        + [partial(kernel_store, tile) for tile in range(4)]
        + [partial(attend_store, tile) for tile in range(3)],
    )
    for number in small_ready:
        loads.wait(number)
    put(0, half, 0, small[...] + small_got[...])


def square_kernel(low, high, loss, *refs):
    *parts, out = refs
    total = jnp.zeros((1, 1), FL)

    def squares(value):
        value = value.astype(FL)
        return jnp.sum(jnp.sum(value * value, axis=0, keepdims=True), axis=1, keepdims=True)

    for number, part in enumerate(parts):
        total += squares(part[...])
        if number == 0:
            total -= 0.5 * squares(part[:, low:high])
    lane = lax.broadcasted_iota(jnp.int32, out.shape, 1)
    out[...] = jnp.where(lane == 0, total, jnp.where(lane == 1, loss[...], 0.0))


def update_kernel(cells, classes, spread, core_ref, sums, turned, *refs):
    grads, refs = refs[:10], refs[10:]
    olds, news, lows = refs[:18], refs[18:36], refs[36:]
    core = core_ref[0]
    norm = jnp.sqrt(sums[0:1, 0:1])
    factor = jnp.minimum(1.0, CLIP / norm)

    def step(table, cols, gradient, rate, decay, low):
        weight, first, second = (olds[6 * k + table][cols] for k in range(3))
        results = adam_step(weight, first, second, gradient.astype(FL) * factor, rate, decay)
        for k in range(3):
            news[6 * k + table][cols] = results[k]
        if low is not None:
            lows[low][cols] = results[0].astype(BF)

    def part(side, index, lo, size):
        return grads[5 * side + index][:, lo : lo + size]

    def cols(base, side, half):
        place = 1 - core if side else core
        return (slice(None), pl.ds(pl.multiple_of(base + place * half, 128), half))

    width = olds[2].shape[1] // 4
    fhalf, half, khalf = olds[3].shape[1] // 4, width // 2, olds[0].shape[1] // 2
    chalf = grads[3].shape[1] - fhalf
    for side in range(2):
        for k in range(3):
            step(2, cols(k * width, side, half), part(side, k, 0, half), RATE, DECAY, 1)
        step(2, cols(3 * width, side, half), part(side, 2, half, half), RATE, DECAY, 1)
        place = 1 - core if side else core
        for tile in range(4):
            for stream, col, lo, hi in spread[tile]:
                at = pl.multiple_of(place * khalf + tile * half + lo, 128)
                value = part(side, stream, col, hi - lo)
                step(0, (slice(None), pl.ds(at, hi - lo)), value, RATE, DECAY, 0)
        for k in range(2):
            step(3, cols(k * 2 * fhalf, side, fhalf), part(side, 4 - k, 0, fhalf), RATE, DECAY, 2)
    own, other = part(0, 3, fhalf, chalf), part(1, 3, fhalf, chalf)
    low_half = jnp.where(core == 0, own.astype(FL), other.astype(FL))
    high_half = jnp.where(core == 0, other.astype(FL), own.astype(FL))
    step(4, (slice(None), slice(0, chalf)), low_half, RATE, DECAY, 3)
    step(4, (slice(None), slice(chalf, classes)), high_half[:, : classes - chalf], RATE, DECAY, 3)
    tiny = part(0, 0, half, SMALL)
    step(1, (slice(None), slice(0, cells)), tiny[:, :cells], RATE_TABLE, 0.0, None)

    @pl.when(pl.program_id(0) == 0)
    def gains():
        on_side = turned[:, half : half + SMALL].astype(FL).T
        step(5, (slice(None), slice(None)), on_side[cells : cells + 6, :], RATE_TABLE, 0.0, None)


def body(
    count,
    pixels,
    patch_kind,
    labels,
    resize,
    embed_kernel,
    pos_base,
    gains,
    attn_weight,
    mlp_weight,
    head_weight,
    embed_first,
    pos_first,
    gains_first,
    attn_first,
    mlp_first,
    head_first,
    embed_second,
    pos_second,
    gains_second,
    attn_second,
    mlp_second,
    head_second,
):
    me = lax.axis_index("fsdp")
    core = lax.axis_index("rep")
    core_at = core.astype(jnp.int32)[None]
    images, tokens = pixels.shape[:2]
    total = images * tokens
    rows, width = attn_weight.shape[0], attn_weight.shape[0] * count
    aligned = rows % 16 == 0 and count & (count - 1) == 0
    ffw = mlp_weight.shape[1] // 2
    classes = head_weight.shape[1]
    kdim = embed_kernel.shape[0]
    cells_count = pos_base.shape[0]
    feats, base = resize.shape[1:]
    chalf = -(-classes // 256) * 128
    half, fhalf, khalf = width // 2, ffw // 2, kdim // 2
    heads = width // HEAD_DIM
    lse_rows = -(-heads // 8) * 8
    chunk = min(total, 256)
    tiles = fhalf // TILE

    other_first = (khalf - 256) // 2
    widths = (width + 256 + SMALL, half + other_first, half + other_first)
    *pieces, rest = call(
        partial(prepare_kernel, cells_count),
        (1,),
        [
            whole((rows, kdim)),
            whole((rows, cells_count)),
            whole((6, rows)),
            whole((rows, 4 * width)),
            whole((rows, 2 * ffw)),
            whole((rows, classes)),
        ],
        [whole((rows, size)) for size in widths] + [whole((rows, ffw + chalf))],
        [sds((rows, size), BF) for size in widths] + [sds((rows, ffw + chalf), BF)],
        scratch=[pltpu.VMEM((128, 128), FL)],
        limit=MOST,
        prefetch=2,
    )(core_at, labels, embed_kernel.T, pos_base.T, gains, attn_weight, mlp_weight, head_weight)

    fan_orders = [
        order_of(count, [1, 4, 8, 2]),
        order_of(count, [2, 1, 4, 8]),
        order_of(count, [4, 2, 1, 8]),
    ]
    if aligned:
        near, far, rest = gather_relative(pieces, count, fan_orders, rest, len(bits_of(count)) - 1)
        *near, patch_kind = tie(*near, patch_kind)
    rest_own = lax.all_gather(rest, "fsdp", axis=0, tiled=True)
    r_own, r_other = call(
        reduce_kernel,
        (images,),
        [
            pl.BlockSpec((1, 3 * feats, tokens), lambda b, kind, c: (b, 0, 0)),
            pl.BlockSpec((1, feats, base), lambda b, kind, c: (kind[b], 0, 0)),
        ],
        [pl.BlockSpec((tokens, khalf), lambda b, kind, c: (b, 0))] * 2,
        [sds((total, khalf), BF)] * 2,
        prefetch=2,
    )(patch_kind, core_at, jnp.transpose(pixels, (0, 2, 1)), resize)

    if aligned:
        *far, r_own, r_other = tie(*far, r_own, r_other)
        gathered = []
        for one, two in zip(near, far):
            gathered += [one, two, other_core(one), other_core(two)]
        where_fan = jnp.stack(
            [me ^ jnp.array(relative_masks(order), jnp.int32) for order in fan_orders]
        )
        plan = (
            (
                (0, half, 1, 0, half),
                (half, half, 1, width, half),
                (width, 256, 0, 0, khalf),
                (width + 256, SMALL, 2, 0, 0),
            ),
            ((0, half, 1, 2 * width, half), (half, other_first, 0, 256, khalf)),
            ((0, half, 1, 3 * width, half), (half, other_first, 0, 256 + other_first, khalf)),
        )
    else:
        where_fan = jnp.zeros((3, count), jnp.int32)
        own = [lax.all_gather(piece, "fsdp", axis=0, tiled=True) for piece in pieces]
        other = [other_core(value) for value in own]

        def joined(parts):
            one, two, three = parts
            return (
                jnp.concatenate([one[:, width : width + 256], two[:, half:], three[:, half:]], axis=1),
                jnp.stack([one[:, :half], one[:, half:width], two[:, :half], three[:, :half]], axis=1),
                one[:, width + 256 :],
            )

        own_e, own_a, small = joined(own)
        other_e, other_a, small_other = joined(other)
        kernel_t = jnp.concatenate([own_e, other_e], axis=1)
        attn_low = jnp.stack(halves(own_a, other_a, core), axis=2).reshape(width, 4 * width)
        gain_rows = jnp.pad(small[:, cells_count : cells_count + 6].astype(FL).T, ((0, 2), (0, 0)))
        number = (small[:, cells_count + 6] + small_other[:, cells_count + 6]).astype(FL)
        image_count = (jnp.sum(number) / rows)[None, None]

    table = np.zeros((tokens, SMALL), np.float32)
    table[:, :cells_count] = grid_matrix()
    high = table.astype(jnp.bfloat16)
    low = (table - high.astype(np.float32)).astype(jnp.bfloat16)
    by_image = pl.BlockSpec((tokens, width), lambda b, *c: (b, 0))
    by_lane = pl.BlockSpec((width, tokens), lambda b, *c: (0, b))
    qkv_spec = pl.BlockSpec((3 * width, tokens), lambda b, *c: (0, b))
    lse_spec = pl.BlockSpec((1, lse_rows, tokens), lambda b, *c: (b, 0, 0))
    if aligned:
        weights_in = gathered
        weight_specs = [pl.BlockSpec(memory_space=pl.ANY)] * 12
        more_out = [sds((width, 4 * width), BF), sds((8, width), FL), sds((1, 1), FL)]
        more_scratch = [
            pltpu.VMEM((width, kdim), BF),
            pltpu.VMEM((width, SMALL), BF),
            pltpu.VMEM((width, SMALL), BF),
            pltpu.SemaphoreType.DMA((4,)),
        ]
    else:
        plan = None
        weights_in = (kernel_t, attn_low, small, small_other, gain_rows, image_count)
        weight_specs = [whole(item.shape) for item in weights_in]
        more_out, more_scratch = [], []
    start, normed_t, qkv_t, mixed_t, lse, middle, normed_two, *more = call(
        partial(forward_kernel, plan, cells_count),
        (images,),
        weight_specs + [pl.BlockSpec((tokens, khalf), lambda b, *c: (b, 0))] * 2
        + [whole((tokens, 2 * SMALL))],
        [by_image, by_lane, qkv_spec, by_lane, lse_spec, by_image, by_image]
        + [whole(item.shape) for item in more_out],
        [
            sds((total, width), FL),
            sds((width, total), BF),
            sds((3 * width, total), BF),
            sds((width, total), BF),
            sds((images, lse_rows, tokens), FL),
            sds((total, width), FL),
            sds((total, width), BF),
        ]
        + more_out,
        scratch=[
            pltpu.VMEM((3 * width, width), BF),
            pltpu.VMEM((heads, tokens, tokens), FL),
            pltpu.VMEM((heads, tokens, tokens), BF),
        ]
        + more_scratch,
        limit=MOST,
        prefetch=2,
    )(where_fan, core_at, *weights_in, r_own, r_other, jnp.asarray(np.concatenate([high, low], axis=1)))
    if aligned:
        attn_low, gain_rows, image_count = more
    rest_own, normed_two = tie(rest_own, normed_two)
    rest_other = other_core(rest_own)
    r_got, n_got = other_core(r_other), other_core(normed_t)

    col = lambda offset: pl.BlockSpec((width, TILE), lambda j: (0, offset + j))
    tile_spec = pl.BlockSpec((total, TILE), lambda j: (0, j))
    final, hidden, slope = call(
        partial(mlp_kernel, chunk),
        (tiles,),
        [whole((total, width)), whole((total, width)), col(0), col(tiles)],
        [whole((total, width)), tile_spec, tile_spec],
        [sds((total, width), FL), sds((total, fhalf), BF), sds((total, fhalf), BF)],
    )(middle, normed_two, rest_own, rest_own)

    labels_col = jnp.pad(labels, (0, 8 - images), constant_values=-1)[:, None]
    head_spec = pl.BlockSpec((width, chalf), lambda i, c: (0, ffw // chalf))
    colc = lambda offset: pl.BlockSpec((width, TILE), lambda j, c: (0, offset + j))
    tilec = pl.BlockSpec((total, TILE), lambda j, c: (0, j))
    (
        d_final, e_low, head_own, head_other, four_grads, loss_part, hidden_other, slope_other,
    ) = call(
        partial(middle_kernel, images, classes, chunk),
        (tiles,),
        [
            whole((total, width)),
            whole((total, width)),
            colc(0),
            colc(tiles),
            whole((8, 1)),
            whole((1, 1)),
            whole((8, width)),
            head_spec,
            head_spec,
        ],
        [
            whole((total, width)),
            whole((total, width)),
            whole((width, chalf)),
            whole((width, chalf)),
            whole((8, width)),
            whole((8, 128)),
            tilec,
            tilec,
        ],
        [
            sds((total, width), FL),
            sds((total, width), BF),
            sds((width, chalf), FL),
            sds((width, chalf), BF),
            sds((8, width), FL),
            sds((8, 128), FL),
            sds((total, fhalf), BF),
            sds((total, fhalf), BF),
        ],
        scratch=[pltpu.VMEM((total, width), FL)],
        prefetch=1,
    )(
        core_at, final, normed_two, rest_other, rest_other, labels_col, image_count, gain_rows,
        rest_own, rest_other,
    )

    up_of = lambda part: part[:, :fhalf]
    down_of = lambda part: part[:, fhalf:ffw]
    down_other = mm(e_low, hidden_other, ((0,), (0,))).astype(BF)
    down_got, head_got = other_core(down_other), other_core(head_other)
    e_low, ignored = tie(e_low, down_other)
    d_pre_other = (
        mm(e_low, down_of(rest_other), ((1,), (0,))) * slope_other.astype(FL)
    ).astype(BF)
    up_other = mm(normed_two, d_pre_other, ((0,), (0,))).astype(BF)
    up_got = other_core(up_other)
    e_low, ignored = tie(e_low, up_other)
    d_pre = (mm(e_low, down_of(rest_own), ((1,), (0,))) * slope.astype(FL)).astype(BF)
    hidden, d_pre = tie(hidden, d_pre)
    d_down = (mm(e_low, hidden, ((0,), (0,))) + down_got.astype(FL)).astype(BF)
    d_head = (head_own + head_got.astype(FL)).astype(BF)
    d_pre, ignored = tie(d_pre, d_down)
    d_up = (mm(normed_two, d_pre, ((0,), (0,))) + up_got.astype(FL)).astype(BF)

    def split_shapes(size):
        if aligned:
            return [sds((count // 2, rows, size), BF)] * 2
        return [sds((width, size), BF)]

    def split_specs(size):
        return [whole(item.shape) for item in split_shapes(size)]

    def begin(parts, order):
        keep, send, held = split_sides(parts, count, order, me)
        return partner(send, count, order[0]), keep, held, order, me

    def arrive(flows, *others):
        given = tie(*[flow[0] for flow in flows], *others)
        following = []
        for (ignored, keep, held, order, who), got in zip(flows, given):
            keep, send, held = step_sides(keep, got, held, order[1:], who)
            got = None if send is None else partner(send, count, order[1])
            following.append((got, keep, held, order[1:], who))
        return following, given[len(flows) :]

    if aligned:
        flow_down = begin([d_down, d_head], order_of(count, [1, 4, 8, 2]))
        flow_up = begin([d_up], order_of(count, [2, 1, 4, 8]))
    d_pre, d_pre_other, ignored = tie(d_pre, d_pre_other, d_up)
    d_normed_two = mm(d_pre_other, up_of(rest_other), ((1,), (1,))) + mm(
        d_pre, up_of(rest_own), ((1,), (1,))
    )
    row_image = pl.BlockSpec((tokens, width), lambda b, c: (b, 0))
    d_middle, o_low, grads_in, out_other = call(
        norm_two_kernel,
        (images,),
        [
            row_image,
            row_image,
            row_image,
            whole((8, width)),
            pl.BlockSpec((width, tokens), lambda b, c: (0, b)),
            whole((8, width)),
        ],
        [row_image, row_image, whole((8, width)), whole((width, half))],
        [
            sds((total, width), FL),
            sds((total, width), BF),
            sds((8, width), FL),
            sds((width, half), BF),
        ],
        scratch=[pltpu.VMEM((8, width), FL), pltpu.VMEM((width, half), FL)],
        prefetch=1,
    )(core_at, d_normed_two, middle, d_final, gain_rows, mixed_t, four_grads)
    out_got = other_core(out_other)
    pair = max(images // 2, 1)
    shift = lambda k: [
        pl.BlockSpec((tokens, width), lambda b, c: (b + k, 0)),
        pl.BlockSpec((3 * width, tokens), lambda b, c: (0, b + k)),
        pl.BlockSpec((1, lse_rows, tokens), lambda b, c: (b + k, 0, 0)),
        pl.BlockSpec((width, tokens), lambda b, c: (0, b + k)),
    ]

    def attend_back(k, final, grads_in, o_low, sum_in=()):
        image_spec, qkvs, lses, lanes = shift(k)
        sums = sds((width, SMALL), FL) if final else sds((tokens, width), FL)
        own_lanes = lambda size: pl.BlockSpec((size, tokens), lambda b, c: (0, b))
        return call(
            partial(attend_back_kernel, cells_count, final),
            (pair,),
            [
                image_spec,
                whole((width, 4 * width)),
                qkvs,
                lses,
                image_spec,
                image_spec,
                whole((8, width)),
                whole((tokens, SMALL)),
                whole((8, width)),
            ]
            + [whole((tokens, width))] * len(sum_in),
            [own_lanes(3 * half), own_lanes(3 * half + width), whole(sums.shape), whole((8, width))],
            [
                sds((3 * half, pair * tokens), BF),
                sds((3 * half + width, pair * tokens), BF),
                sums,
                sds((8, width), FL),
            ],
            scratch=[
                pltpu.VMEM((3 * width, tokens), BF),
                pltpu.VMEM((width, tokens), BF),
                pltpu.VMEM((tokens, width), FL),
                pltpu.VMEM((8, width), FL),
                pltpu.VMEM((heads, tokens, tokens), FL),
                pltpu.VMEM((heads, tokens, tokens), FL),
                pltpu.VMEM((heads, tokens, tokens), BF),
                pltpu.VMEM((heads, tokens, tokens), BF),
            ],
            prefetch=1,
        )(core_at, o_low, attn_low, qkv_t, lse, d_middle, start, gain_rows, jnp.asarray(table), grads_in, *sum_in)

    d_own_one, sent_one, sum_one, grads_one = attend_back(0, False, grads_in, o_low)
    if aligned:
        (flow_down, flow_up), (sum_one, sent_one) = arrive([flow_down, flow_up], sum_one, sent_one)
    got_one = other_core(sent_one)
    d_own_two, sent_two, d_small, ignored = attend_back(pair, True, grads_one, o_low, (sum_one,))
    if aligned:
        (flow_down, flow_up), (sent_two, d_small) = arrive([flow_down, flow_up], sent_two, d_small)
    got_two, small_got = other_core(sent_two), other_core(d_small)

    spread = (
        ((0, half + SMALL, 0, half),),
        ((1, half, 0, half),),
        ((1, 2 * half, 0, 2 * SMALL), (0, 2 * half + SMALL, 2 * SMALL, half)),
        ((0, 2 * half + 2 * SMALL, 0, SMALL), (2, 2 * half, SMALL, half)),
    )
    tail_widths = (2 * half + 3 * SMALL, 2 * half + 2 * SMALL, 3 * half - SMALL)
    tail_parts = call(
        partial(tail_grad_kernel, aligned, rows, spread),
        (1,),
        [pl.BlockSpec(memory_space=pl.ANY)] * 15,
        [spec for size in tail_widths for spec in split_specs(size)],
        [shape for size in tail_widths for shape in split_shapes(size)],
        scratch=[
            pltpu.VMEM((2, width, half), FL),
            pltpu.VMEM((width, 2 * total), BF),
            pltpu.VMEM((3, half, 2 * total), BF),
            pltpu.VMEM((width, 4 * pair * tokens), BF),
            pltpu.VMEM((4, 2 * total, half), BF),
            pltpu.VMEM((width, SMALL), FL),
            pltpu.VMEM((width, SMALL), FL),
            pltpu.VMEM((width, total), BF),
            pltpu.VMEM((total, half), BF),
            pltpu.VMEM((width, half), BF),
            pltpu.SemaphoreType.DMA((14,)),
        ],
        prefetch=2,
    )(
        where_fan, core_at, normed_t, n_got, d_own_one, d_own_two, sent_one, sent_two, got_one, got_two,
        r_own, r_got, d_small, small_got,
        mixed_t, o_low, out_got,
    )
    if aligned:
        (flow_down, flow_up), tail_parts = arrive([flow_down, flow_up], *tail_parts)
        flows = [flow_down, flow_up]
        for k, order in enumerate(fan_orders):
            keep, send = tail_parts[2 * k : 2 * k + 2]
            shape = (2,) * (len(order) - 1) + keep.shape[1:]
            got = partner(send, count, order[0]).reshape(shape)
            flows.append((got, keep.reshape(shape), order[1:], order, None))
        while any(flow[0] is not None for flow in flows):
            live = [k for k, flow in enumerate(flows) if flow[0] is not None]
            after, ignored = arrive([flows[k] for k in live])
            for k, flow in zip(live, after):
                flows[k] = flow
        g_down, g_up, *g_tail = [flow[1] for flow in flows]
    else:
        g_down, g_up, *g_tail = [
            lax.psum_scatter(part, "fsdp", scatter_dimension=0, tiled=True)
            for part in (jnp.concatenate([d_down, d_head], axis=1), d_up, *tail_parts)
        ]

    own_shards = [*g_tail, g_down, g_up]
    other_shards = [other_core(item) for item in own_shards]
    sums = call(
        partial(square_kernel, half, half + SMALL),
        (1,),
        [whole((8, 128))] + [whole(item.shape) for item in own_shards],
        whole((8, 128)),
        sds((8, 128), FL),
    )(loss_part, *own_shards)
    sums = sum_everywhere(sums, count)
    tables = (embed_kernel.T, pos_base.T, attn_weight, mlp_weight, head_weight, gains)
    firsts = (embed_first.T, pos_first.T, attn_first, mlp_first, head_first, gains_first)
    seconds = (embed_second.T, pos_second.T, attn_second, mlp_second, head_second, gains_second)
    block = 16 if rows % 16 == 0 else rows

    def by_rows(item):
        if item.shape[0] != rows:
            return whole(item.shape)
        return pl.BlockSpec((block, item.shape[1]), lambda i, c: (i, 0))

    olds = (*tables, *firsts, *seconds)
    lows = [sds(tables[k].shape, BF) for k in (0, 2, 3, 4)]
    outs = call(
        partial(update_kernel, cells_count, classes, spread),
        (rows // block,),
        [whole((8, 128)), whole(g_tail[0].shape)]
        + [by_rows(item) for item in (*own_shards, *other_shards, *olds)],
        [by_rows(item) for item in (*olds, *lows)],
        [sds(item.shape, FL) for item in olds] + lows,
        prefetch=1,
    )(core_at, sums, g_tail[0], *own_shards, *other_shards, *olds)
    new, low = outs[:18], outs[18:]
    sets = [
        (new[6 * k].T, new[6 * k + 1].T, new[6 * k + 5], *new[6 * k + 2 : 6 * k + 5])
        for k in range(3)
    ]
    return (
        sums[0, 1],
        image_count[0, 0],
        jnp.sqrt(sums[0, 0]),
        *sets[0],
        *sets[1],
        *sets[2],
        low[0].T,
        *low[1:],
    )


def solution(mesh):
    data = P(("rep", "fsdp"))
    columns, rows = P(None, "fsdp"), P("fsdp", None)
    table = (columns, columns, columns, rows, rows, rows)
    in_specs = (P(("rep", "fsdp"), None, None), data, data, P()) + table * 3
    out_specs = (P(), P(), P()) + table * 3 + (columns, rows, rows, rows)
    return jax.shard_map(
        partial(body, mesh.shape["fsdp"]),
        mesh=mesh,
        in_specs=in_specs,
        out_specs=out_specs,
        check_vma=False,
    )
```

```python
from functools import partial

import jax
import jax.numpy as jnp
import numpy as np
from jax import lax
from jax.experimental import pallas as pl
from jax.experimental.pallas import tpu as pltpu
from jax.sharding import PartitionSpec as P

HEAD_DIM = 64
BASE = 32
GRID0 = 7
MAXP = 24
GRID = 16
STEP = 10
SIDES = (10, 15, 24)

NORM_EPS = 1e-06
CLIP = 0.02
BETA_ONE = 0.9
BETA_TWO = 0.999
ADAM_EPS = 1e-08
RATE = 0.1
RATE_TABLE = 1.0
DECAY = 0.05
BF = jnp.bfloat16
FL = jnp.float32
SMALL = 128
TILE = 512
LIMIT = 30 * 1024 * 1024
MORE = 40 * 1024 * 1024
MOST = 58 * 1024 * 1024


def grid_matrix():
    target = (np.arange(GRID, dtype=np.float32) + np.float32(0.5)) * (GRID0 / GRID) - 0.5
    target = np.clip(target, 0.0, GRID0 - 1.0)
    source = np.arange(GRID0, dtype=np.float32)
    line = np.maximum(0.0, 1.0 - np.abs(target[:, None] - source[None, :]))
    return (line[:, None, :, None] * line[None, :, None, :]).reshape(GRID * GRID, GRID0 * GRID0)


def adam_step(weight, first_old, second_old, gradient, step_rate, decay_rate):
    first_new = BETA_ONE * first_old + (1.0 - BETA_ONE) * gradient
    second_new = BETA_TWO * second_old + (1.0 - BETA_TWO) * gradient * gradient
    first_hat = first_new / (1.0 - BETA_ONE**STEP)
    second_hat = second_new / (1.0 - BETA_TWO**STEP)
    weight_new = weight - step_rate * (
        first_hat / (jnp.sqrt(second_hat) + ADAM_EPS) + decay_rate * weight
    )
    return (weight_new, first_new, second_new)


def partner(value, count, mask):
    return lax.ppermute(value, "fsdp", [(i, i ^ mask) for i in range(count)])


def other_core(value):
    return lax.ppermute(value, "rep", [(0, 1), (1, 0)])


def bits_of(count):
    return [1 << k for k in range(count.bit_length() - 1)]


def order_of(count, preferred):
    return preferred if sorted(preferred) == bits_of(count) else bits_of(count)


def relative_masks(order):
    masks = [0]
    for mask in reversed(order):
        masks = masks + [held ^ mask for held in masks]
    return masks


def tie(*values):
    return lax.optimization_barrier(values)


def gather_relative(shards, count, orders, late, late_step):
    held = [shard[None] for shard in shards]
    for step in range(len(orders[0]) - 1, 0, -1):
        got = [partner(value, count, order[step]) for value, order in zip(held, orders)]
        if step == late_step:
            *got, late = tie(*got, late)
        else:
            got = tie(*got)
        held = [jnp.concatenate(pair, axis=0) for pair in zip(held, got)]
    return held, [partner(value, count, order[0]) for value, order in zip(held, orders)], late


def add_halves(keep, got):
    half = keep.shape[0] // 2
    if half == 0:
        return (keep[0].astype(FL) + got[0].astype(FL)).astype(BF), None
    return tuple(
        (keep[rows].astype(FL) + got[rows].astype(FL)).astype(BF)
        for rows in (slice(0, half), slice(half, None))
    )


def axis_of(mask, held_masks):
    return held_masks.index(mask)


def side_of(value, mask, held_masks, me, other):
    if me is None:
        return lax.index_in_dim(value, int(other), axis_of(mask, held_masks), keepdims=False)
    bit = jnp.where((me & mask) != 0, 1, 0)
    at = 1 - bit if other else bit
    return lax.dynamic_index_in_dim(value, at, axis_of(mask, held_masks), keepdims=False)


def split_sides(parts, count, order, me):
    held = bits_of(count)[::-1]
    shaped = [part.reshape((2,) * len(held) + (part.shape[0] // count, -1)) for part in parts]
    sides = []
    for other in (False, True):
        pieces = []
        for value in shaped:
            for number, mask in enumerate(order):
                if number == 0:
                    value = side_of(value, mask, held, me, other)
            pieces.append(value)
        sides.append(jnp.concatenate(pieces, axis=-1))
    return sides[0], sides[1], [mask for mask in held if mask != order[0]]


def step_sides(keep, got, held, order, me):
    if not order:
        total = keep.astype(FL) + got.astype(FL)
        return total.astype(BF), None, held
    mask = order[0]
    sides = [
        (
            side_of(keep, mask, held, me, other).astype(FL)
            + side_of(got, mask, held, me, other).astype(FL)
        ).astype(BF)
        for other in (False, True)
    ]
    return sides[0], sides[1], [bit for bit in held if bit != mask]


def sum_everywhere(value, count):
    value = value + other_core(value)
    bits = bits_of(count)
    while bits:
        pair, bits = bits[:2], bits[2:]
        got = [partner(value, count, mask) for mask in (*pair, sum(pair))[: 2 * len(pair) - 1]]
        value = value + got[0]
        if len(pair) == 2:
            value = value + (got[1] + got[2])
    return value


def halves(own, other, core):
    return jnp.where(core == 0, own, other), jnp.where(core == 0, other, own)


def dot(a, b):
    return lax.dot_general(a, b, (((1,), (0,)), ((), ())), preferred_element_type=FL)


def dot_t(a, b):
    return lax.dot_general(a, b, (((1,), (1,)), ((), ())), preferred_element_type=FL)


def t_dot(a, b):
    return lax.dot_general(a, b, (((0,), (0,)), ((), ())), preferred_element_type=FL)


def call(kernel, grid, in_specs, out_specs, out_shape, scratch=(), prefetch=0, limit=LIMIT):
    return pl.pallas_call(
        kernel,
        grid_spec=pltpu.PrefetchScalarGridSpec(
            num_scalar_prefetch=prefetch,
            grid=grid,
            in_specs=in_specs,
            out_specs=out_specs,
            scratch_shapes=list(scratch),
        ),
        out_shape=out_shape,
        compiler_params=pltpu.CompilerParams(vmem_limit_bytes=limit),
        cost_estimate=pl.CostEstimate(flops=1, bytes_accessed=1, transcendentals=0),
    )


def whole(shape):
    zeros = (0,) * len(shape)
    return pl.BlockSpec(shape, lambda *a: zeros, pipeline_mode=pl.Buffered(1))


def sds(shape, dtype):
    return jax.ShapeDtypeStruct(shape, dtype)


def norm_parts(values_in):
    row_mean = jnp.mean(values_in, axis=-1, keepdims=True)
    centered = values_in - row_mean
    row_var = jnp.mean(centered * centered, axis=-1, keepdims=True)
    inverse = lax.rsqrt(row_var + NORM_EPS)
    return centered * inverse, inverse


def norm_back(xhat, inverse, gain, dy):
    gained = dy * gain
    one = jnp.mean(gained, axis=-1, keepdims=True)
    two = jnp.mean(gained * xhat, axis=-1, keepdims=True)
    return inverse * (gained - one - xhat * two)


def normal_cdf(x):
    return 0.5 + 0.5 * lax.erf(x * 0.7071067811865476), jnp.exp(-0.5 * x * x)


def prepare_kernel(cells, core_ref, labels_ref, embed, pos, gains, attn, one, two, three, held):
    core = core_ref[0]
    rows, width = attn.shape[0], attn.shape[1] // 4
    half, khalf = width // 2, embed.shape[1] // 2

    def cols(ref, base, step, size):
        return ref[:, pl.ds(pl.multiple_of(base + core * step, 128), size)].astype(BF)

    first, other = khalf - 2 * (khalf - 256) // 2, (khalf - 256) // 2
    one[:, :half] = cols(attn, 0, half, half)
    one[:, half : 2 * half] = cols(attn, width, half, half)
    one[:, 2 * half : 2 * half + first] = cols(embed, 0, khalf, first)
    two[:, :half] = cols(attn, 2 * width, half, half)
    two[:, half:] = cols(embed, first, khalf, other)
    three[:, :half] = cols(attn, 3 * width, half, half)
    three[:, half:] = cols(embed, first + other, khalf, other)
    total = jnp.int32(0)
    for image in range(labels_ref.shape[0]):
        total = total + jnp.where(labels_ref[image] >= 0, 1, 0)
    held[...] = jnp.zeros(held.shape, FL)
    held[cells : cells + 6, :rows] = gains[...]
    held[cells + 6 : cells + 7, :] = jnp.full((1, held.shape[1]), total.astype(FL))
    turned = held[...].T
    one[:, 2 * half + first :] = turned[:rows].astype(BF)
    one[:, 2 * half + first : 2 * half + first + cells] = pos[...].astype(BF)


def prepare_rest_kernel(core_ref, mlp, head, rest):
    core = core_ref[0]
    rows, fhalf = mlp.shape[0], mlp.shape[1] // 4

    def cols(base):
        return mlp[:, pl.ds(pl.multiple_of(base + core * fhalf, 128), fhalf)].astype(BF)

    rest[:, :fhalf] = cols(0)
    rest[:, fhalf : 2 * fhalf] = cols(2 * fhalf)
    chalf = rest.shape[1] - 2 * fhalf
    classes = head.shape[1]
    low_half = head[:, :chalf]
    high_half = jnp.concatenate(
        [head[:, chalf:classes], jnp.zeros((rows, 2 * chalf - classes), FL)], axis=1
    )
    rest[:, 2 * fhalf :] = jnp.where(core == 0, low_half, high_half).astype(BF)


def reduce_kernel(kind_ref, core_ref, pixels, resize, own, other):
    kind = kind_ref[pl.program_id(0)]
    side = jnp.where(kind == 0, SIDES[0], jnp.where(kind == 1, SIDES[1], SIDES[2]))
    feats, base = resize.shape[1], resize.shape[2]
    place = lax.broadcasted_iota(jnp.int32, (feats, base), 0)
    chosen = jnp.where(place < side * side, resize[0].astype(FL), 0.0).astype(BF)
    factor = 0.25 / side.astype(FL)
    half = own.shape[1]
    values = []
    for channel in range(3):
        part = pixels[0, channel * feats : (channel + 1) * feats, :]
        values.append((t_dot(part, chosen) * factor).astype(BF))
    for core, sides in enumerate(((own, other), (other, own))):
        @pl.when(core_ref[0] == core)
        def store(sides=sides):
            for channel, value in enumerate(values):
                lo, hi = channel * base, (channel + 1) * base
                for number, side in enumerate(sides):
                    left, right = max(lo, number * half), min(hi, (number + 1) * half)
                    if left < right:
                        side[:, left - number * half : right - number * half] = value[
                            :, left - lo : right - lo
                        ]


def start_pieces(plan, where_ref, core, pieces, targets, sems, later):
    rows, half = pieces[0].shape[1], pieces[0].shape[0]

    def one_block(p, ignored):
        for stream in range(3):
            for top in range(2):
                at = pl.multiple_of(where_ref[stream, p + top * half] * rows, rows)
                for swapped in range(2):
                    source = pieces[4 * stream + 2 * swapped + top]
                    for src, size, target, base, step in plan[stream]:
                        if (target == 1) != later:
                            continue
                        if target == 2:
                            dst = targets[2 + swapped].at[pl.ds(at, rows), :]
                            sem = sems.at[2 + swapped]
                        else:
                            side = 1 - core if swapped else core
                            if target == 0:
                                side = swapped
                            col = pl.multiple_of(base + side * step, 128)
                            dst = targets[target].at[pl.ds(at, rows), pl.ds(col, size)]
                            sem = sems.at[target]
                        pltpu.make_async_copy(
                            source.at[p, :, pl.ds(src, size)], dst, sem
                        ).start()
        return ignored

    lax.fori_loop(0, half, one_block, 0)


def forward_kernel(plan, cells_count, where_ref, core_ref, *refs):
    joined = plan is not None
    weights, refs = (refs[:12], refs[12:]) if joined else (refs[:6], refs[6:])
    (reduced, reduced_other, cells), refs = refs[:3], refs[3:]
    start, normed_t, qkv_t, mixed_t, lse, middle, normed_two = refs[:7]
    refs = refs[7:]
    if joined:
        attn, gains, counts, turned, scores, probs, kernel_t, small, small_other, sems = refs
        targets = (kernel_t, attn, small, small_other)
    else:
        kernel_t, attn, small, small_other, gains, counts = weights
        turned, scores, probs = refs
    width = normed_t.shape[0]
    heads = width // HEAD_DIM
    first_image = pl.program_id(0) == 0

    if joined:
        @pl.when(first_image)
        def arrive():
            for later in (False, True):
                start_pieces(plan, where_ref, core_ref[0], weights, targets, sems, later)
            for number in (0, 2, 3):
                pltpu.make_async_copy(targets[number], targets[number], sems.at[number]).wait()
            rows = weights[0].shape[1]
            on_side = small[...].astype(FL).T
            gains[0:6, :] = on_side[cells_count : cells_count + 6, :]
            gains[6:8, :] = jnp.zeros((2, width), FL)
            at = slice(cells_count + 6, cells_count + 7)
            number = on_side[at, :] + small_other[...].astype(FL).T[at, :]
            counts[...] = jnp.sum(number, axis=1, keepdims=True) * (1.0 / rows)

    posemb = dot_t(cells[:, :SMALL], small[...]) + dot_t(cells[:, SMALL:], small[...])
    khalf = reduced.shape[1]
    x = dot_t(reduced[...], kernel_t[:, :khalf]) + dot_t(reduced_other[...], kernel_t[:, khalf:])
    x = x + posemb
    start[...] = x
    xhat, ignored = norm_parts(x)
    normed_t[...] = (xhat * gains[0:1, :] + gains[1:2, :]).astype(BF).T

    @pl.when(first_image)
    def turn():
        if joined:
            pltpu.make_async_copy(attn, attn, sems.at[1]).wait()
        for at in range(0, 3 * width, 256):
            turned[at : at + 256, :] = attn[:, at : at + 256].T

    qkv_t[...] = dot(turned[...], normed_t[...]).astype(BF)
    spans = [slice(head * HEAD_DIM, (head + 1) * HEAD_DIM) for head in range(heads)]
    for head, span in enumerate(spans):
        q = qkv_t[span, :] * jnp.asarray(HEAD_DIM**-0.5, BF)
        scores[head] = t_dot(qkv_t[width + span.start : width + span.stop, :], q)
    shares = []
    for head in range(heads):
        top = jnp.max(scores[head], axis=0, keepdims=True)
        expd = jnp.exp(scores[head] - top)
        total = jnp.sum(expd, axis=0, keepdims=True)
        probs[head] = expd.astype(BF)
        lse[0, head : head + 1, :] = top + jnp.log(total)
        shares.append(1.0 / total)
    for head, span in enumerate(spans):
        v = qkv_t[2 * width + span.start : 2 * width + span.stop, :]
        mixed_t[span, :] = (dot(v, probs[head]) * shares[head]).astype(BF)
    lse[0, heads:, :] = jnp.zeros((lse.shape[1] - heads, lse.shape[2]), FL)
    x = start[...] + t_dot(mixed_t[...], attn[:, 3 * width :])
    middle[...] = x
    xhat, ignored = norm_parts(x)
    normed_two[...] = (xhat * gains[2:3, :] + gains[3:4, :]).astype(BF)


def mlp_tile(chunk, normed_two, up, down, final, hidden, slope):
    count = normed_two.shape[0] // chunk
    rows = lambda i: slice(i * chunk, (i + 1) * chunk)
    pre, low = {0: dot(normed_two[rows(0), :], up[...])}, {}
    for i in range(count + 1):
        if i + 1 < count:
            pre[i + 1] = dot(normed_two[rows(i + 1), :], up[...])
        if i < count:
            value = pre.pop(i)
            cdf, bell = normal_cdf(value)
            low[i] = (value * cdf).astype(BF)
            hidden[rows(i), :] = low[i]
            slope[rows(i), :] = (cdf + value * bell * 0.3989422804014327).astype(BF)
        if i > 0:
            final[rows(i - 1), :] += dot_t(low.pop(i - 1), down[...])


def mlp_kernel(chunk, held, normed_two, up, down, final, hidden, slope):
    @pl.when(pl.program_id(0) == 0)
    def first():
        final[...] = held[...]

    mlp_tile(chunk, normed_two, up, down, final, hidden, slope)


def head_part(
    images, classes, core, final, labels, image_count, gains, own, other,
    d_final, e_low, own_grad, other_grad, row_grads, loss,
):
    tokens = final.shape[0] // images
    width = final.shape[1]
    chalf = own.shape[1]
    gain = gains[4:5, :]
    places = lax.broadcasted_iota(jnp.int32, (8, width), 0)
    means = jnp.zeros((8, width), FL)
    for image in range(images):
        xhat, ignored = norm_parts(final[image * tokens : (image + 1) * tokens, :])
        mean_row = jnp.mean(xhat, axis=0, keepdims=True)
        means = jnp.where(places == image, mean_row, means)
    pooled = jnp.where(places < images, means * gain + gains[5:6, :], 0.0).astype(BF)
    logits = [dot(pooled, own[...]), dot(pooled, other[...])]
    lane = lax.broadcasted_iota(jnp.int32, (8, chalf), 1)
    kinds = [lane + core * chalf, lane + (1 - core) * chalf]
    masked = [jnp.where(kinds[k] < classes, logits[k], -1e30) for k in range(2)]
    top = jnp.maximum(
        jnp.max(masked[0], axis=1, keepdims=True), jnp.max(masked[1], axis=1, keepdims=True)
    )
    expd = [jnp.where(kinds[k] < classes, jnp.exp(masked[k] - top), 0.0) for k in range(2)]
    total = jnp.sum(expd[0], axis=1, keepdims=True) + jnp.sum(expd[1], axis=1, keepdims=True)
    log_total = top + jnp.log(total)
    named = labels[...]
    onehot = [(kinds[k] == named).astype(FL) for k in range(2)]
    target = jnp.sum(onehot[0] * logits[0], axis=1, keepdims=True) + jnp.sum(
        onehot[1] * logits[1], axis=1, keepdims=True
    )
    counted = (named >= 0).astype(FL)
    losses = counted * (log_total - target)
    loss[...] = jnp.broadcast_to(jnp.sum(losses, axis=0, keepdims=True), loss.shape)
    share = counted / image_count[...]
    d_logits = [((expd[k] / total - onehot[k]) * share).astype(BF) for k in range(2)]
    own_grad[...] = t_dot(pooled, d_logits[0])
    other_grad[...] = t_dot(pooled, d_logits[1]).astype(BF)
    d_pooled = dot_t(d_logits[0], own[...]) + dot_t(d_logits[1], other[...])
    row_grads[0:1, :] = jnp.sum(d_pooled * means, axis=0, keepdims=True)
    row_grads[1:2, :] = jnp.sum(d_pooled, axis=0, keepdims=True)
    row_grads[2:8, :] = jnp.zeros((6, width), FL)
    for image in range(images):
        rows = slice(image * tokens, (image + 1) * tokens)
        xhat, inverse = norm_parts(final[rows, :])
        dy = d_pooled[image : image + 1, :] * (1.0 / tokens)
        back = norm_back(xhat, inverse, gain, dy)
        d_final[rows, :] = back
        e_low[rows, :] = back.astype(BF)


def middle_kernel(
    images, classes, chunk, core_ref, held, normed_two, up, down, labels, image_count, gains,
    head_own, head_other, d_final, e_low, own_grad, other_grad, row_grads, loss, hidden, slope, final,
):
    step = pl.program_id(0)

    @pl.when(step == 0)
    def first():
        final[...] = held[...]

    mlp_tile(chunk, normed_two, up, down, final, hidden, slope)

    @pl.when(step == pl.num_programs(0) - 1)
    def head():
        head_part(
            images, classes, core_ref[0], final, labels, image_count, gains, head_own, head_other,
            d_final, e_low, own_grad, other_grad, row_grads, loss,
        )


def mm(a, b, dims):
    return lax.dot_general(a, b, (dims, ((), ())), preferred_element_type=FL)


def norm_two_kernel(
    core_ref, d_normed, middle, d_final, gains, mixed_t, four_grads,
    d_middle, o_low, row_grads, out_grad, sums, product,
):
    image = pl.program_id(0)
    width = middle.shape[1]
    half = width // 2
    xhat, inverse = norm_parts(middle[...])
    dy = d_normed[...]
    back = d_final[...] + norm_back(xhat, inverse, gains[2:3, :], dy)
    d_middle[...] = back
    o_low[...] = back.astype(BF)

    @pl.when(image == 0)
    def first():
        sums[...] = jnp.zeros(sums.shape, FL)
        product[...] = jnp.zeros(product.shape, FL)

    sums[0:1, :] += jnp.sum(dy * xhat, axis=0, keepdims=True)
    sums[1:2, :] += jnp.sum(dy, axis=0, keepdims=True)
    other = pl.multiple_of((1 - core_ref[0]) * half, 128)
    product[...] += dot(mixed_t[...], o_low[:, pl.ds(other, half)])

    @pl.when(image == pl.num_programs(0) - 1)
    def last():
        row_grads[0:2, :] = jnp.zeros((2, width), FL)
        row_grads[2:4, :] = sums[0:2, :]
        row_grads[4:6, :] = four_grads[0:2, :]
        row_grads[6:8, :] = jnp.zeros((2, width), FL)
        out_grad[...] = product[...].astype(BF)


def place(where_ref, row, rows, value, held, keep, send, col):
    size = value.shape[1]
    if send is None:
        keep[:, col : col + size] = value.astype(BF)
        return
    held[:, :size] = value
    half = keep.shape[0]
    for p in range(half):
        low = pl.multiple_of(where_ref[row, p] * rows, rows)
        high = pl.multiple_of(where_ref[row, half + p] * rows, rows)
        keep[p, :, col : col + size] = held[pl.ds(low, rows), :size].astype(BF)
        send[p, :, col : col + size] = held[pl.ds(high, rows), :size].astype(BF)


def split_outs(refs, aligned, number):
    if aligned:
        return [(refs[2 * k], refs[2 * k + 1]) for k in range(number)], refs[2 * number :]
    return [(refs[k], None) for k in range(number)], refs[number:]


class Loads:
    def __init__(self, sems):
        self.sems, self.targets = sems, []

    def add(self, target, *pairs):
        sem = self.sems.at[len(self.targets)]
        for source, place in pairs:
            pltpu.make_async_copy(source, place, sem).start()
        self.targets.append(target)
        return len(self.targets) - 1

    def wait(self, number):
        target = self.targets[number]
        pltpu.make_async_copy(target, target, self.sems.at[number]).wait()


def in_turn(products, stores):
    value = products[0]()
    for number, store in enumerate(stores):
        following = products[number + 1]() if number + 1 < len(products) else None
        store(value)
        value = following


def attend_back_kernel(
    cells_count, final, core_ref, o_low, attn, qkv_t, lse, d_middle, start, gains, cells, grads_in, *refs
):
    sum_in, refs = (refs[0], refs[1:]) if final else (None, refs)
    d_own, sent, sum_out, grads_out, d_qkv_t, d_mixed_t, summed, row_grads = refs[:8]
    scores, d_probs, probs, d_scores = refs[8:]
    width = o_low.shape[1]
    heads = width // HEAD_DIM
    image = pl.program_id(0)

    @pl.when(image == 0)
    def first():
        summed[...] = sum_in[...] if final else jnp.zeros(summed.shape, FL)
        row_grads[...] = grads_in[...]

    scale = HEAD_DIM**-0.5
    d_mixed_t[...] = dot_t(attn[:, 3 * width :], o_low[...]).astype(BF)
    spans = [slice(head * HEAD_DIM, (head + 1) * HEAD_DIM) for head in range(heads)]
    part = lambda ref, k, span: ref[k * width + span.start : k * width + span.stop, :]
    for head, span in enumerate(spans):
        q = part(qkv_t, 0, span) * jnp.asarray(scale, BF)
        scores[head] = t_dot(part(qkv_t, 1, span), q)
        d_probs[head] = t_dot(part(qkv_t, 2, span), d_mixed_t[span, :])
    for head in range(heads):
        soft = jnp.exp(scores[head] - lse[0, head : head + 1, :])
        probs[head] = soft.astype(BF)
        delta = jnp.sum(soft * d_probs[head], axis=0, keepdims=True)
        d_scores[head] = (soft * (d_probs[head] - delta)).astype(BF)
    for head, span in enumerate(spans):
        q = part(qkv_t, 0, span) * jnp.asarray(scale, BF)
        at = span.start
        d_qkv_t[at : at + HEAD_DIM, :] = (
            dot(part(qkv_t, 1, span), d_scores[head]) * scale
        ).astype(BF)
        d_qkv_t[width + at : width + at + HEAD_DIM, :] = dot_t(q, d_scores[head]).astype(BF)
        d_qkv_t[2 * width + at : 2 * width + at + HEAD_DIM, :] = dot_t(
            d_mixed_t[span, :], probs[head]
        ).astype(BF)
    half = width // 2
    for k in range(3):
        for ref, side in ((d_own, core_ref[0]), (sent, 1 - core_ref[0])):
            at = pl.multiple_of(k * width + side * half, 128)
            ref[k * half : (k + 1) * half, :] = d_qkv_t[pl.ds(at, half), :]
    dy = dot(attn[:, : 3 * width], d_qkv_t[...]).T
    xhat, inverse = norm_parts(start[...])
    back = d_middle[...] + norm_back(xhat, inverse, gains[0:1, :], dy)
    sent[3 * half :, :] = back.astype(BF).T
    summed[...] += back
    row_grads[0:1, :] += jnp.sum(dy * xhat, axis=0, keepdims=True)
    row_grads[1:2, :] += jnp.sum(dy, axis=0, keepdims=True)

    @pl.when(image == pl.num_programs(0) - 1)
    def last():
        grads_out[...] = row_grads[...]
        if not final:
            sum_out[...] = summed[...]
            return
        total = lax.dot_general(
            cells[...], summed[...], (((0,), (0,)), ((), ())),
            preferred_element_type=FL, precision=lax.Precision.HIGHEST,
        )
        summed[0:SMALL, :] = total
        summed[cells_count : cells_count + 6, :] = row_grads[0:6, :]
        sum_out[...] = summed[0:SMALL, :].T


def tail_grad_kernel(aligned, rows, spread, where_ref, core_ref, *refs):
    n_parts, own_parts, sent_parts, got_parts, r_parts = (
        refs[:2], refs[2:4], refs[4:6], refs[6:8], refs[8:10]
    )
    (small_hbm, small_got_hbm, mixed_hbm, o_hbm, out_hbm), refs = refs[10:15], refs[15:]
    d_parts, s_parts = (*own_parts, *got_parts), (*sent_parts, *got_parts)
    outs, scratch = split_outs(refs, aligned, 3)
    held, n_t, d_t, s_t, reduced, small, small_got, mixed_t, o_low, out_got, sems = scratch
    half, span = d_t.shape[1], own_parts[0].shape[1]
    width = s_t.shape[0]
    tokens = r_parts[0].shape[0]
    loads = Loads(sems)
    own = pl.multiple_of(core_ref[0] * half, 128)

    def load_tile(tile):
        at = pl.ds(tile * half, half)
        pairs = [(r_parts[k].at[:, at], reduced.at[tile, pl.ds(k * tokens, tokens), :]) for k in range(2)]
        return loads.add(reduced.at[tile], *pairs)

    def load_rows(tile):
        at = pl.ds(tile * half, half)
        pairs = [(d_parts[k].at[at, :], d_t.at[tile, :, pl.ds(k * span, span)]) for k in range(4)]
        return loads.add(d_t.at[tile], *pairs)

    out_ready = [
        loads.add(mixed_t, (mixed_hbm, mixed_t)),
        loads.add(o_low, (o_hbm.at[:, pl.ds(own, half)], o_low)),
        loads.add(out_got, (out_hbm, out_got)),
    ]
    tile_ready = [load_tile(0)]
    s_ready = loads.add(s_t, *[
            (s_parts[k].at[pl.ds(3 * half, width), :], s_t.at[:, pl.ds(k * span, span)])
            for k in range(4)
        ])
    tile_ready += [load_tile(1), load_tile(2), load_tile(3)]
    n_ready = loads.add(n_t, *[(n_parts[k], n_t.at[:, pl.ds(k * tokens, tokens)]) for k in range(2)])
    row_ready = [load_rows(0), load_rows(1), load_rows(2)]
    small_ready = [loads.add(small, (small_hbm, small)), loads.add(small_got, (small_got_hbm, small_got))]

    def put(stream, col, number, value):
        place(where_ref, stream, rows, value, held.at[number], *outs[stream], col)

    def out_product():
        for number in out_ready:
            loads.wait(number)
        return dot(mixed_t[...], o_low[...])

    def out_store(value):
        put(2, half, 0, value + out_got[...].astype(FL))

    def kernel_product(tile):
        if tile == 0:
            loads.wait(s_ready)
        loads.wait(tile_ready[tile])
        return dot(s_t[...], reduced[tile])

    def kernel_store(tile, value):
        for stream, col, lo, hi in spread[tile]:
            put(stream, col, (tile + 1) % 2, value[:, lo:hi])

    def attend_product(tile):
        if tile == 0:
            loads.wait(n_ready)
        loads.wait(row_ready[tile])
        return dot_t(n_t[...], d_t[tile])

    def attend_store(tile, value):
        put(tile, 0, (tile + 1) % 2, value)

    in_turn(
        [out_product]
        + [partial(kernel_product, tile) for tile in range(4)]
        + [partial(attend_product, tile) for tile in range(3)],
        [out_store]
        + [partial(kernel_store, tile) for tile in range(4)]
        + [partial(attend_store, tile) for tile in range(3)],
    )
    for number in small_ready:
        loads.wait(number)
    put(0, half, 0, small[...] + small_got[...])


def square_kernel(low, high, loss, *refs):
    *parts, out = refs
    total = jnp.zeros((1, 1), FL)

    def squares(value):
        value = value.astype(FL)
        return jnp.sum(jnp.sum(value * value, axis=0, keepdims=True), axis=1, keepdims=True)

    for number, part in enumerate(parts):
        total += squares(part[...])
        if number == 0:
            total -= 0.5 * squares(part[:, low:high])
    lane = lax.broadcasted_iota(jnp.int32, out.shape, 1)
    out[...] = jnp.where(lane == 0, total, jnp.where(lane == 1, loss[...], 0.0))


def update_kernel(cells, classes, spread, core_ref, sums, turned, *refs):
    grads, refs = refs[:10], refs[10:]
    olds, news, lows = refs[:18], refs[18:36], refs[36:]
    core = core_ref[0]
    norm = jnp.sqrt(sums[0:1, 0:1])
    factor = jnp.minimum(1.0, CLIP / norm)

    def step(table, cols, gradient, rate, decay, low):
        weight, first, second = (olds[6 * k + table][cols] for k in range(3))
        results = adam_step(weight, first, second, gradient.astype(FL) * factor, rate, decay)
        for k in range(3):
            news[6 * k + table][cols] = results[k]
        if low is not None:
            lows[low][cols] = results[0].astype(BF)

    def part(side, index, lo, size):
        return grads[5 * side + index][:, lo : lo + size]

    def cols(base, side, half):
        place = 1 - core if side else core
        return (slice(None), pl.ds(pl.multiple_of(base + place * half, 128), half))

    width = olds[2].shape[1] // 4
    fhalf, half, khalf = olds[3].shape[1] // 4, width // 2, olds[0].shape[1] // 2
    chalf = grads[3].shape[1] - fhalf
    for side in range(2):
        for k in range(3):
            step(2, cols(k * width, side, half), part(side, k, 0, half), RATE, DECAY, 1)
        step(2, cols(3 * width, side, half), part(side, 2, half, half), RATE, DECAY, 1)
        place = 1 - core if side else core
        for tile in range(4):
            for stream, col, lo, hi in spread[tile]:
                at = pl.multiple_of(place * khalf + tile * half + lo, 128)
                value = part(side, stream, col, hi - lo)
                step(0, (slice(None), pl.ds(at, hi - lo)), value, RATE, DECAY, 0)
        for k in range(2):
            step(3, cols(k * 2 * fhalf, side, fhalf), part(side, 4 - k, 0, fhalf), RATE, DECAY, 2)
    own, other = part(0, 3, fhalf, chalf), part(1, 3, fhalf, chalf)
    low_half = jnp.where(core == 0, own.astype(FL), other.astype(FL))
    high_half = jnp.where(core == 0, other.astype(FL), own.astype(FL))
    step(4, (slice(None), slice(0, chalf)), low_half, RATE, DECAY, 3)
    step(4, (slice(None), slice(chalf, classes)), high_half[:, : classes - chalf], RATE, DECAY, 3)
    tiny = part(0, 0, half, SMALL)
    step(1, (slice(None), slice(0, cells)), tiny[:, :cells], RATE_TABLE, 0.0, None)

    @pl.when(pl.program_id(0) == 0)
    def gains():
        on_side = turned[:, half : half + SMALL].astype(FL).T
        step(5, (slice(None), slice(None)), on_side[cells : cells + 6, :], RATE_TABLE, 0.0, None)


def body(
    count,
    pixels,
    patch_kind,
    labels,
    resize,
    embed_kernel,
    pos_base,
    gains,
    attn_weight,
    mlp_weight,
    head_weight,
    embed_first,
    pos_first,
    gains_first,
    attn_first,
    mlp_first,
    head_first,
    embed_second,
    pos_second,
    gains_second,
    attn_second,
    mlp_second,
    head_second,
):
    me = lax.axis_index("fsdp")
    core = lax.axis_index("rep")
    core_at = core.astype(jnp.int32)[None]
    images, tokens = pixels.shape[:2]
    total = images * tokens
    rows, width = attn_weight.shape[0], attn_weight.shape[0] * count
    aligned = rows % 16 == 0 and count & (count - 1) == 0
    ffw = mlp_weight.shape[1] // 2
    classes = head_weight.shape[1]
    kdim = embed_kernel.shape[0]
    cells_count = pos_base.shape[0]
    feats, base = resize.shape[1:]
    chalf = -(-classes // 256) * 128
    half, fhalf, khalf = width // 2, ffw // 2, kdim // 2
    heads = width // HEAD_DIM
    lse_rows = -(-heads // 8) * 8
    chunk = min(total, 256)
    tiles = fhalf // TILE

    other_first = (khalf - 256) // 2
    widths = (width + 256 + SMALL, half + other_first, half + other_first)
    pieces = call(
        partial(prepare_kernel, cells_count),
        (1,),
        [
            whole((rows, kdim)),
            whole((rows, cells_count)),
            whole((6, rows)),
            whole((rows, 4 * width)),
        ],
        [whole((rows, size)) for size in widths],
        [sds((rows, size), BF) for size in widths],
        scratch=[pltpu.VMEM((128, 128), FL)],
        prefetch=2,
        limit=MOST,
    )(core_at, labels, embed_kernel.T, pos_base.T, gains, attn_weight)
    mlp_in, *pieces = tie(mlp_weight, *pieces)
    rest = call(
        prepare_rest_kernel,
        (1,),
        [whole((rows, 2 * ffw)), whole((rows, classes))],
        whole((rows, ffw + chalf)),
        sds((rows, ffw + chalf), BF),
        prefetch=1,
        limit=MOST,
    )(core_at, mlp_in, head_weight)

    fan_orders = [
        order_of(count, [1, 4, 8, 2]),
        order_of(count, [2, 1, 4, 8]),
        order_of(count, [4, 2, 1, 8]),
    ]
    if aligned:
        near, far, rest = gather_relative(pieces, count, fan_orders, rest, len(bits_of(count)) - 1)
        *near, patch_kind = tie(*near, patch_kind)
    rest_own = lax.all_gather(rest, "fsdp", axis=0, tiled=True)
    r_own, r_other = call(
        reduce_kernel,
        (images,),
        [
            pl.BlockSpec((1, 3 * feats, tokens), lambda b, kind, c: (b, 0, 0)),
            pl.BlockSpec((1, feats, base), lambda b, kind, c: (kind[b], 0, 0)),
        ],
        [pl.BlockSpec((tokens, khalf), lambda b, kind, c: (b, 0))] * 2,
        [sds((total, khalf), BF)] * 2,
        prefetch=2,
    )(patch_kind, core_at, jnp.transpose(pixels, (0, 2, 1)), resize)

    if aligned:
        *far, r_own, r_other = tie(*far, r_own, r_other)
        gathered = []
        for one, two in zip(near, far):
            gathered += [one, two, other_core(one), other_core(two)]
        where_fan = jnp.stack(
            [me ^ jnp.array(relative_masks(order), jnp.int32) for order in fan_orders]
        )
        plan = (
            (
                (0, half, 1, 0, half),
                (half, half, 1, width, half),
                (width, 256, 0, 0, khalf),
                (width + 256, SMALL, 2, 0, 0),
            ),
            ((0, half, 1, 2 * width, half), (half, other_first, 0, 256, khalf)),
            ((0, half, 1, 3 * width, half), (half, other_first, 0, 256 + other_first, khalf)),
        )
    else:
        where_fan = jnp.zeros((3, count), jnp.int32)
        own = [lax.all_gather(piece, "fsdp", axis=0, tiled=True) for piece in pieces]
        other = [other_core(value) for value in own]

        def joined(parts):
            one, two, three = parts
            return (
                jnp.concatenate([one[:, width : width + 256], two[:, half:], three[:, half:]], axis=1),
                jnp.stack([one[:, :half], one[:, half:width], two[:, :half], three[:, :half]], axis=1),
                one[:, width + 256 :],
            )

        own_e, own_a, small = joined(own)
        other_e, other_a, small_other = joined(other)
        kernel_t = jnp.concatenate([own_e, other_e], axis=1)
        attn_low = jnp.stack(halves(own_a, other_a, core), axis=2).reshape(width, 4 * width)
        gain_rows = jnp.pad(small[:, cells_count : cells_count + 6].astype(FL).T, ((0, 2), (0, 0)))
        number = (small[:, cells_count + 6] + small_other[:, cells_count + 6]).astype(FL)
        image_count = (jnp.sum(number) / rows)[None, None]

    table = np.zeros((tokens, SMALL), np.float32)
    table[:, :cells_count] = grid_matrix()
    high = table.astype(jnp.bfloat16)
    low = (table - high.astype(np.float32)).astype(jnp.bfloat16)
    by_image = pl.BlockSpec((tokens, width), lambda b, *c: (b, 0))
    by_lane = pl.BlockSpec((width, tokens), lambda b, *c: (0, b))
    qkv_spec = pl.BlockSpec((3 * width, tokens), lambda b, *c: (0, b))
    lse_spec = pl.BlockSpec((1, lse_rows, tokens), lambda b, *c: (b, 0, 0))
    if aligned:
        weights_in = gathered
        weight_specs = [pl.BlockSpec(memory_space=pl.ANY)] * 12
        more_out = [sds((width, 4 * width), BF), sds((8, width), FL), sds((1, 1), FL)]
        more_scratch = [
            pltpu.VMEM((width, kdim), BF),
            pltpu.VMEM((width, SMALL), BF),
            pltpu.VMEM((width, SMALL), BF),
            pltpu.SemaphoreType.DMA((4,)),
        ]
    else:
        plan = None
        weights_in = (kernel_t, attn_low, small, small_other, gain_rows, image_count)
        weight_specs = [whole(item.shape) for item in weights_in]
        more_out, more_scratch = [], []
    start, normed_t, qkv_t, mixed_t, lse, middle, normed_two, *more = call(
        partial(forward_kernel, plan, cells_count),
        (images,),
        weight_specs + [pl.BlockSpec((tokens, khalf), lambda b, *c: (b, 0))] * 2
        + [whole((tokens, 2 * SMALL))],
        [by_image, by_lane, qkv_spec, by_lane, lse_spec, by_image, by_image]
        + [whole(item.shape) for item in more_out],
        [
            sds((total, width), FL),
            sds((width, total), BF),
            sds((3 * width, total), BF),
            sds((width, total), BF),
            sds((images, lse_rows, tokens), FL),
            sds((total, width), FL),
            sds((total, width), BF),
        ]
        + more_out,
        scratch=[
            pltpu.VMEM((3 * width, width), BF),
            pltpu.VMEM((heads, tokens, tokens), FL),
            pltpu.VMEM((heads, tokens, tokens), BF),
        ]
        + more_scratch,
        limit=MOST,
        prefetch=2,
    )(where_fan, core_at, *weights_in, r_own, r_other, jnp.asarray(np.concatenate([high, low], axis=1)))
    if aligned:
        attn_low, gain_rows, image_count = more
    rest_own, normed_two = tie(rest_own, normed_two)
    rest_other = other_core(rest_own)
    r_got, n_got = other_core(r_other), other_core(normed_t)

    col = lambda offset: pl.BlockSpec((width, TILE), lambda j: (0, offset + j))
    tile_spec = pl.BlockSpec((total, TILE), lambda j: (0, j))
    final, hidden, slope = call(
        partial(mlp_kernel, chunk),
        (tiles,),
        [whole((total, width)), whole((total, width)), col(0), col(tiles)],
        [whole((total, width)), tile_spec, tile_spec],
        [sds((total, width), FL), sds((total, fhalf), BF), sds((total, fhalf), BF)],
        limit=MOST,
    )(middle, normed_two, rest_own, rest_own)

    labels_col = jnp.pad(labels, (0, 8 - images), constant_values=-1)[:, None]
    head_spec = pl.BlockSpec((width, chalf), lambda i, c: (0, ffw // chalf))
    colc = lambda offset: pl.BlockSpec((width, TILE), lambda j, c: (0, offset + j))
    tilec = pl.BlockSpec((total, TILE), lambda j, c: (0, j))
    (
        d_final, e_low, head_own, head_other, four_grads, loss_part, hidden_other, slope_other,
    ) = call(
        partial(middle_kernel, images, classes, chunk),
        (tiles,),
        [
            whole((total, width)),
            whole((total, width)),
            colc(0),
            colc(tiles),
            whole((8, 1)),
            whole((1, 1)),
            whole((8, width)),
            head_spec,
            head_spec,
        ],
        [
            whole((total, width)),
            whole((total, width)),
            whole((width, chalf)),
            whole((width, chalf)),
            whole((8, width)),
            whole((8, 128)),
            tilec,
            tilec,
        ],
        [
            sds((total, width), FL),
            sds((total, width), BF),
            sds((width, chalf), FL),
            sds((width, chalf), BF),
            sds((8, width), FL),
            sds((8, 128), FL),
            sds((total, fhalf), BF),
            sds((total, fhalf), BF),
        ],
        scratch=[pltpu.VMEM((total, width), FL)],
        prefetch=1,
    )(
        core_at, final, normed_two, rest_other, rest_other, labels_col, image_count, gain_rows,
        rest_own, rest_other,
    )

    up_of = lambda part: part[:, :fhalf]
    down_of = lambda part: part[:, fhalf:ffw]
    down_other = mm(e_low, hidden_other, ((0,), (0,))).astype(BF)
    down_got, head_got = other_core(down_other), other_core(head_other)
    e_one, ignored = tie(e_low, down_other)
    d_pre_other = (
        mm(e_one, down_of(rest_other), ((1,), (0,))) * slope_other.astype(FL)
    ).astype(BF)
    d_head = (head_own + head_got.astype(FL)).astype(BF)
    e_two, ignored = tie(e_one, d_pre_other)
    d_down = (mm(e_two, hidden, ((0,), (0,))) + down_got.astype(FL)).astype(BF)

    def split_shapes(size):
        if aligned:
            return [sds((count // 2, rows, size), BF)] * 2
        return [sds((width, size), BF)]

    def split_specs(size):
        return [whole(item.shape) for item in split_shapes(size)]

    def begin(parts, order):
        keep, send, held = split_sides(parts, count, order, me)
        return partner(send, count, order[0]), keep, held, order, me

    def arrive(flows, *others):
        given = tie(*[flow[0] for flow in flows], *others)
        following = []
        for (ignored, keep, held, order, who), got in zip(flows, given):
            keep, send, held = step_sides(keep, got, held, order[1:], who)
            got = None if send is None else partner(send, count, order[1])
            following.append((got, keep, held, order[1:], who))
        return following, given[len(flows) :]

    if aligned:
        flow_down = begin([d_down, d_head], order_of(count, [1, 4, 8, 2]))
    d_pre_other, ignored = tie(d_pre_other, d_down)
    up_other = mm(normed_two, d_pre_other, ((0,), (0,))).astype(BF)
    up_got = other_core(up_other)
    e_three, ignored = tie(e_two, up_other)
    d_pre = (mm(e_three, down_of(rest_own), ((1,), (0,))) * slope.astype(FL)).astype(BF)
    d_up = (mm(normed_two, d_pre, ((0,), (0,))) + up_got.astype(FL)).astype(BF)
    if aligned:
        flow_up = begin([d_up], order_of(count, [2, 1, 4, 8]))
    d_pre, d_pre_other, ignored = tie(d_pre, d_pre_other, d_up)
    d_normed_two = mm(d_pre_other, up_of(rest_other), ((1,), (1,))) + mm(
        d_pre, up_of(rest_own), ((1,), (1,))
    )
    row_image = pl.BlockSpec((tokens, width), lambda b, c: (b, 0))
    d_middle, o_low, grads_in, out_other = call(
        norm_two_kernel,
        (images,),
        [
            row_image,
            row_image,
            row_image,
            whole((8, width)),
            pl.BlockSpec((width, tokens), lambda b, c: (0, b)),
            whole((8, width)),
        ],
        [row_image, row_image, whole((8, width)), whole((width, half))],
        [
            sds((total, width), FL),
            sds((total, width), BF),
            sds((8, width), FL),
            sds((width, half), BF),
        ],
        scratch=[pltpu.VMEM((8, width), FL), pltpu.VMEM((width, half), FL)],
        prefetch=1,
    )(core_at, d_normed_two, middle, d_final, gain_rows, mixed_t, four_grads)
    out_got = other_core(out_other)
    pair = max(images // 2, 1)
    shift = lambda k: [
        pl.BlockSpec((tokens, width), lambda b, c: (b + k, 0)),
        pl.BlockSpec((3 * width, tokens), lambda b, c: (0, b + k)),
        pl.BlockSpec((1, lse_rows, tokens), lambda b, c: (b + k, 0, 0)),
        pl.BlockSpec((width, tokens), lambda b, c: (0, b + k)),
    ]

    def attend_back(k, final, grads_in, o_low, sum_in=()):
        image_spec, qkvs, lses, lanes = shift(k)
        sums = sds((width, SMALL), FL) if final else sds((tokens, width), FL)
        own_lanes = lambda size: pl.BlockSpec((size, tokens), lambda b, c: (0, b))
        return call(
            partial(attend_back_kernel, cells_count, final),
            (pair,),
            [
                image_spec,
                whole((width, 4 * width)),
                qkvs,
                lses,
                image_spec,
                image_spec,
                whole((8, width)),
                whole((tokens, SMALL)),
                whole((8, width)),
            ]
            + [whole((tokens, width))] * len(sum_in),
            [own_lanes(3 * half), own_lanes(3 * half + width), whole(sums.shape), whole((8, width))],
            [
                sds((3 * half, pair * tokens), BF),
                sds((3 * half + width, pair * tokens), BF),
                sums,
                sds((8, width), FL),
            ],
            scratch=[
                pltpu.VMEM((3 * width, tokens), BF),
                pltpu.VMEM((width, tokens), BF),
                pltpu.VMEM((tokens, width), FL),
                pltpu.VMEM((8, width), FL),
                pltpu.VMEM((heads, tokens, tokens), FL),
                pltpu.VMEM((heads, tokens, tokens), FL),
                pltpu.VMEM((heads, tokens, tokens), BF),
                pltpu.VMEM((heads, tokens, tokens), BF),
            ],
            prefetch=1,
        )(core_at, o_low, attn_low, qkv_t, lse, d_middle, start, gain_rows, jnp.asarray(table), grads_in, *sum_in)

    d_own_one, sent_one, sum_one, grads_one = attend_back(0, False, grads_in, o_low)
    if aligned:
        (flow_down, flow_up), (sum_one, sent_one) = arrive([flow_down, flow_up], sum_one, sent_one)
    got_one = other_core(sent_one)
    d_own_two, sent_two, d_small, ignored = attend_back(pair, True, grads_one, o_low, (sum_one,))
    if aligned:
        (flow_down, flow_up), (sent_two, d_small) = arrive([flow_down, flow_up], sent_two, d_small)
    got_two, small_got = other_core(sent_two), other_core(d_small)

    spread = (
        ((0, half + SMALL, 0, half),),
        ((1, half, 0, half),),
        ((1, 2 * half, 0, 2 * SMALL), (0, 2 * half + SMALL, 2 * SMALL, half)),
        ((0, 2 * half + 2 * SMALL, 0, SMALL), (2, 2 * half, SMALL, half)),
    )
    tail_widths = (2 * half + 3 * SMALL, 2 * half + 2 * SMALL, 3 * half - SMALL)
    tail_parts = call(
        partial(tail_grad_kernel, aligned, rows, spread),
        (1,),
        [pl.BlockSpec(memory_space=pl.ANY)] * 15,
        [spec for size in tail_widths for spec in split_specs(size)],
        [shape for size in tail_widths for shape in split_shapes(size)],
        scratch=[
            pltpu.VMEM((2, width, half), FL),
            pltpu.VMEM((width, 2 * total), BF),
            pltpu.VMEM((3, half, 2 * total), BF),
            pltpu.VMEM((width, 4 * pair * tokens), BF),
            pltpu.VMEM((4, 2 * total, half), BF),
            pltpu.VMEM((width, SMALL), FL),
            pltpu.VMEM((width, SMALL), FL),
            pltpu.VMEM((width, total), BF),
            pltpu.VMEM((total, half), BF),
            pltpu.VMEM((width, half), BF),
            pltpu.SemaphoreType.DMA((14,)),
        ],
        limit=MORE,
        prefetch=2,
    )(
        where_fan, core_at, normed_t, n_got, d_own_one, d_own_two, sent_one, sent_two, got_one, got_two,
        r_own, r_got, d_small, small_got,
        mixed_t, o_low, out_got,
    )
    if aligned:
        (flow_down, flow_up), tail_parts = arrive([flow_down, flow_up], *tail_parts)
        flows = [flow_down, flow_up]
        for k, order in enumerate(fan_orders):
            keep, send = tail_parts[2 * k : 2 * k + 2]
            shape = (2,) * (len(order) - 1) + keep.shape[1:]
            got = partner(send, count, order[0]).reshape(shape)
            flows.append((got, keep.reshape(shape), order[1:], order, None))
        while any(flow[0] is not None for flow in flows):
            live = [k for k, flow in enumerate(flows) if flow[0] is not None]
            after, ignored = arrive([flows[k] for k in live])
            for k, flow in zip(live, after):
                flows[k] = flow
        g_down, g_up, *g_tail = [flow[1] for flow in flows]
    else:
        g_down, g_up, *g_tail = [
            lax.psum_scatter(part, "fsdp", scatter_dimension=0, tiled=True)
            for part in (jnp.concatenate([d_down, d_head], axis=1), d_up, *tail_parts)
        ]

    own_shards = [*g_tail, g_down, g_up]
    other_shards = [other_core(item) for item in own_shards]
    sums = call(
        partial(square_kernel, half, half + SMALL),
        (1,),
        [whole((8, 128))] + [whole(item.shape) for item in own_shards],
        whole((8, 128)),
        sds((8, 128), FL),
    )(loss_part, *own_shards)
    sums = sum_everywhere(sums, count)
    tables = (embed_kernel.T, pos_base.T, attn_weight, mlp_weight, head_weight, gains)
    firsts = (embed_first.T, pos_first.T, attn_first, mlp_first, head_first, gains_first)
    seconds = (embed_second.T, pos_second.T, attn_second, mlp_second, head_second, gains_second)
    block = 16 if rows % 16 == 0 else rows

    def by_rows(item):
        if item.shape[0] != rows:
            return whole(item.shape)
        return pl.BlockSpec((block, item.shape[1]), lambda i, c: (i, 0))

    olds = (*tables, *firsts, *seconds)
    lows = [sds(tables[k].shape, BF) for k in (0, 2, 3, 4)]
    outs = call(
        partial(update_kernel, cells_count, classes, spread),
        (rows // block,),
        [whole((8, 128)), whole(g_tail[0].shape)]
        + [by_rows(item) for item in (*own_shards, *other_shards, *olds)],
        [by_rows(item) for item in (*olds, *lows)],
        [sds(item.shape, FL) for item in olds] + lows,
        prefetch=1,
    )(core_at, sums, g_tail[0], *own_shards, *other_shards, *olds)
    new, low = outs[:18], outs[18:]
    sets = [
        (new[6 * k].T, new[6 * k + 1].T, new[6 * k + 5], *new[6 * k + 2 : 6 * k + 5])
        for k in range(3)
    ]
    return (
        sums[0, 1],
        image_count[0, 0],
        jnp.sqrt(sums[0, 0]),
        *sets[0],
        *sets[1],
        *sets[2],
        low[0].T,
        *low[1:],
    )


def solution(mesh):
    data = P(("rep", "fsdp"))
    columns, rows = P(None, "fsdp"), P("fsdp", None)
    table = (columns, columns, columns, rows, rows, rows)
    in_specs = (P(("rep", "fsdp"), None, None), data, data, P()) + table * 3
    out_specs = (P(), P(), P()) + table * 3 + (columns, rows, rows, rows)
    return jax.shard_map(
        partial(body, mesh.shape["fsdp"]),
        mesh=mesh,
        in_specs=in_specs,
        out_specs=out_specs,
        check_vma=False,
    )
```

```python
from functools import partial

import jax
import jax.numpy as jnp
import numpy as np
from jax import lax
from jax.experimental import pallas as pl
from jax.experimental.pallas import tpu as pltpu
from jax.sharding import PartitionSpec as P

HEAD_DIM = 64
BASE = 32
GRID0 = 7
MAXP = 24
GRID = 16
STEP = 10
SIDES = (10, 15, 24)

NORM_EPS = 1e-06
CLIP = 0.02
BETA_ONE = 0.9
BETA_TWO = 0.999
ADAM_EPS = 1e-08
RATE = 0.1
RATE_TABLE = 1.0
DECAY = 0.05
BF = jnp.bfloat16
FL = jnp.float32
SMALL = 128
TILE = 512
LIMIT = 30 * 1024 * 1024
MORE = 40 * 1024 * 1024
MOST = 58 * 1024 * 1024


def grid_matrix():
    target = (np.arange(GRID, dtype=np.float32) + np.float32(0.5)) * (GRID0 / GRID) - 0.5
    target = np.clip(target, 0.0, GRID0 - 1.0)
    source = np.arange(GRID0, dtype=np.float32)
    line = np.maximum(0.0, 1.0 - np.abs(target[:, None] - source[None, :]))
    return (line[:, None, :, None] * line[None, :, None, :]).reshape(GRID * GRID, GRID0 * GRID0)


def adam_step(weight, first_old, second_old, gradient, step_rate, decay_rate):
    first_new = BETA_ONE * first_old + (1.0 - BETA_ONE) * gradient
    second_new = BETA_TWO * second_old + (1.0 - BETA_TWO) * gradient * gradient
    first_hat = first_new / (1.0 - BETA_ONE**STEP)
    second_hat = second_new / (1.0 - BETA_TWO**STEP)
    weight_new = weight - step_rate * (
        first_hat / (jnp.sqrt(second_hat) + ADAM_EPS) + decay_rate * weight
    )
    return (weight_new, first_new, second_new)


def partner(value, count, mask):
    return lax.ppermute(value, "fsdp", [(i, i ^ mask) for i in range(count)])


def other_core(value):
    return lax.ppermute(value, "rep", [(0, 1), (1, 0)])


def bits_of(count):
    return [1 << k for k in range(count.bit_length() - 1)]


def order_of(count, preferred):
    return preferred if sorted(preferred) == bits_of(count) else bits_of(count)


def relative_masks(order):
    masks = [0]
    for mask in reversed(order):
        masks = masks + [held ^ mask for held in masks]
    return masks


def tie(*values):
    return lax.optimization_barrier(values)


def gather_relative(shards, count, orders, late, late_step):
    held = [shard[None] for shard in shards]
    for step in range(len(orders[0]) - 1, 0, -1):
        got = [partner(value, count, order[step]) for value, order in zip(held, orders)]
        if step == late_step:
            *got, late = tie(*got, late)
        else:
            got = tie(*got)
        held = [jnp.concatenate(pair, axis=0) for pair in zip(held, got)]
    return held, [partner(value, count, order[0]) for value, order in zip(held, orders)], late


def axis_of(mask, held_masks):
    return held_masks.index(mask)


def side_of(value, mask, held_masks, me, other):
    if me is None:
        return lax.index_in_dim(value, int(other), axis_of(mask, held_masks), keepdims=False)
    bit = jnp.where((me & mask) != 0, 1, 0)
    at = 1 - bit if other else bit
    return lax.dynamic_index_in_dim(value, at, axis_of(mask, held_masks), keepdims=False)


def split_sides(parts, count, order, me):
    held = bits_of(count)[::-1]
    shaped = [part.reshape((2,) * len(held) + (part.shape[0] // count, -1)) for part in parts]
    sides = []
    for other in (False, True):
        pieces = []
        for value in shaped:
            for number, mask in enumerate(order):
                if number == 0:
                    value = side_of(value, mask, held, me, other)
            pieces.append(value)
        sides.append(jnp.concatenate(pieces, axis=-1))
    return sides[0], sides[1], [mask for mask in held if mask != order[0]]


def step_sides(keep, got, held, order, me):
    if not order:
        total = keep.astype(FL) + got.astype(FL)
        return total.astype(BF), None, held
    mask = order[0]
    sides = [
        (
            side_of(keep, mask, held, me, other).astype(FL)
            + side_of(got, mask, held, me, other).astype(FL)
        ).astype(BF)
        for other in (False, True)
    ]
    return sides[0], sides[1], [bit for bit in held if bit != mask]


def sum_everywhere(value, count):
    value = value + other_core(value)
    bits = bits_of(count)
    while bits:
        pair, bits = bits[:2], bits[2:]
        got = [partner(value, count, mask) for mask in (*pair, sum(pair))[: 2 * len(pair) - 1]]
        value = value + got[0]
        if len(pair) == 2:
            value = value + (got[1] + got[2])
    return value


def halves(own, other, core):
    return jnp.where(core == 0, own, other), jnp.where(core == 0, other, own)


def dot(a, b):
    return lax.dot_general(a, b, (((1,), (0,)), ((), ())), preferred_element_type=FL)


def dot_t(a, b):
    return lax.dot_general(a, b, (((1,), (1,)), ((), ())), preferred_element_type=FL)


def t_dot(a, b):
    return lax.dot_general(a, b, (((0,), (0,)), ((), ())), preferred_element_type=FL)


def call(kernel, grid, in_specs, out_specs, out_shape, scratch=(), prefetch=0, limit=LIMIT):
    return pl.pallas_call(
        kernel,
        grid_spec=pltpu.PrefetchScalarGridSpec(
            num_scalar_prefetch=prefetch,
            grid=grid,
            in_specs=in_specs,
            out_specs=out_specs,
            scratch_shapes=list(scratch),
        ),
        out_shape=out_shape,
        compiler_params=pltpu.CompilerParams(vmem_limit_bytes=limit),
        cost_estimate=pl.CostEstimate(flops=1, bytes_accessed=1, transcendentals=0),
    )


def whole(shape):
    zeros = (0,) * len(shape)
    return pl.BlockSpec(shape, lambda *a: zeros, pipeline_mode=pl.Buffered(1))


def sds(shape, dtype):
    return jax.ShapeDtypeStruct(shape, dtype)


def norm_parts(values_in):
    row_mean = jnp.mean(values_in, axis=-1, keepdims=True)
    centered = values_in - row_mean
    row_var = jnp.mean(centered * centered, axis=-1, keepdims=True)
    inverse = lax.rsqrt(row_var + NORM_EPS)
    return centered * inverse, inverse


def norm_back(xhat, inverse, gain, dy):
    gained = dy * gain
    one = jnp.mean(gained, axis=-1, keepdims=True)
    two = jnp.mean(gained * xhat, axis=-1, keepdims=True)
    return inverse * (gained - one - xhat * two)


def normal_cdf(x):
    return 0.5 + 0.5 * lax.erf(x * 0.7071067811865476), jnp.exp(-0.5 * x * x)


def prepare_kernel(cells, core_ref, labels_ref, embed, pos, gains, attn, one, two, three, held):
    core = core_ref[0]
    rows, width = attn.shape[0], attn.shape[1] // 4
    half, khalf = width // 2, embed.shape[1] // 2

    def cols(ref, base, step, size):
        return ref[:, pl.ds(pl.multiple_of(base + core * step, 128), size)].astype(BF)

    first, other = khalf - 2 * (khalf - 256) // 2, (khalf - 256) // 2
    one[:, :half] = cols(attn, 0, half, half)
    one[:, half : 2 * half] = cols(attn, width, half, half)
    one[:, 2 * half : 2 * half + first] = cols(embed, 0, khalf, first)
    two[:, :half] = cols(attn, 2 * width, half, half)
    two[:, half:] = cols(embed, first, khalf, other)
    three[:, :half] = cols(attn, 3 * width, half, half)
    three[:, half:] = cols(embed, first + other, khalf, other)
    total = jnp.int32(0)
    for image in range(labels_ref.shape[0]):
        total = total + jnp.where(labels_ref[image] >= 0, 1, 0)
    held[...] = jnp.zeros(held.shape, FL)
    held[cells : cells + 6, :rows] = gains[...]
    held[cells + 6 : cells + 7, :] = jnp.full((1, held.shape[1]), total.astype(FL))
    turned = held[...].T
    one[:, 2 * half + first :] = turned[:rows].astype(BF)
    one[:, 2 * half + first : 2 * half + first + cells] = pos[...].astype(BF)


def prepare_rest_kernel(core_ref, mlp, head, rest):
    core = core_ref[0]
    rows, fhalf = mlp.shape[0], mlp.shape[1] // 4

    def cols(base):
        return mlp[:, pl.ds(pl.multiple_of(base + core * fhalf, 128), fhalf)].astype(BF)

    rest[:, :fhalf] = cols(0)
    rest[:, fhalf : 2 * fhalf] = cols(2 * fhalf)
    chalf = rest.shape[1] - 2 * fhalf
    classes = head.shape[1]
    low_half = head[:, :chalf]
    high_half = jnp.concatenate(
        [head[:, chalf:classes], jnp.zeros((rows, 2 * chalf - classes), FL)], axis=1
    )
    rest[:, 2 * fhalf :] = jnp.where(core == 0, low_half, high_half).astype(BF)


def reduce_kernel(kind_ref, core_ref, pixels, resize, own, other):
    kind = kind_ref[pl.program_id(0)]
    side = jnp.where(kind == 0, SIDES[0], jnp.where(kind == 1, SIDES[1], SIDES[2]))
    feats, base = resize.shape[1], resize.shape[2]
    place = lax.broadcasted_iota(jnp.int32, (feats, base), 0)
    chosen = jnp.where(place < side * side, resize[0].astype(FL), 0.0).astype(BF)
    factor = 0.25 / side.astype(FL)
    half = own.shape[1]
    values = []
    for channel in range(3):
        part = pixels[0, channel * feats : (channel + 1) * feats, :]
        values.append((t_dot(part, chosen) * factor).astype(BF))
    for core, sides in enumerate(((own, other), (other, own))):
        @pl.when(core_ref[0] == core)
        def store(sides=sides):
            for channel, value in enumerate(values):
                lo, hi = channel * base, (channel + 1) * base
                for number, side in enumerate(sides):
                    left, right = max(lo, number * half), min(hi, (number + 1) * half)
                    if left < right:
                        side[:, left - number * half : right - number * half] = value[
                            :, left - lo : right - lo
                        ]


def start_pieces(plan, where_ref, core, pieces, targets, sems, later):
    rows, half = pieces[0].shape[1], pieces[0].shape[0]

    def one_block(p, ignored):
        for stream in range(3):
            for top in range(2):
                at = pl.multiple_of(where_ref[stream, p + top * half] * rows, rows)
                for swapped in range(2):
                    source = pieces[4 * stream + 2 * swapped + top]
                    for src, size, target, base, step in plan[stream]:
                        if (target == 1) != later:
                            continue
                        if target == 2:
                            dst = targets[2 + swapped].at[pl.ds(at, rows), :]
                            sem = sems.at[2 + swapped]
                        else:
                            side = 1 - core if swapped else core
                            if target == 0:
                                side = swapped
                            col = pl.multiple_of(base + side * step, 128)
                            dst = targets[target].at[pl.ds(at, rows), pl.ds(col, size)]
                            sem = sems.at[target]
                        pltpu.make_async_copy(
                            source.at[p, :, pl.ds(src, size)], dst, sem
                        ).start()
        return ignored

    lax.fori_loop(0, half, one_block, 0)


def forward_kernel(plan, cells_count, where_ref, core_ref, *refs):
    joined = plan is not None
    weights, refs = (refs[:12], refs[12:]) if joined else (refs[:6], refs[6:])
    (reduced, reduced_other, cells), refs = refs[:3], refs[3:]
    start, normed_t, qkv_t, mixed_t, lse, middle, normed_two = refs[:7]
    refs = refs[7:]
    if joined:
        attn, gains, counts, turned, scores, probs, kernel_t, small, small_other, sems = refs
        targets = (kernel_t, attn, small, small_other)
    else:
        kernel_t, attn, small, small_other, gains, counts = weights
        turned, scores, probs = refs
    width = normed_t.shape[0]
    heads = width // HEAD_DIM
    first_image = pl.program_id(0) == 0

    if joined:
        @pl.when(first_image)
        def arrive():
            for later in (False, True):
                start_pieces(plan, where_ref, core_ref[0], weights, targets, sems, later)
            for number in (0, 2, 3):
                pltpu.make_async_copy(targets[number], targets[number], sems.at[number]).wait()
            rows = weights[0].shape[1]
            on_side = small[...].astype(FL).T
            gains[0:6, :] = on_side[cells_count : cells_count + 6, :]
            gains[6:8, :] = jnp.zeros((2, width), FL)
            at = slice(cells_count + 6, cells_count + 7)
            number = on_side[at, :] + small_other[...].astype(FL).T[at, :]
            counts[...] = jnp.sum(number, axis=1, keepdims=True) * (1.0 / rows)

    posemb = dot_t(cells[:, :SMALL], small[...]) + dot_t(cells[:, SMALL:], small[...])
    khalf = reduced.shape[1]
    x = dot_t(reduced[...], kernel_t[:, :khalf]) + dot_t(reduced_other[...], kernel_t[:, khalf:])
    x = x + posemb
    start[...] = x
    xhat, ignored = norm_parts(x)
    normed_t[...] = (xhat * gains[0:1, :] + gains[1:2, :]).astype(BF).T

    @pl.when(first_image)
    def turn():
        if joined:
            pltpu.make_async_copy(attn, attn, sems.at[1]).wait()
        for at in range(0, 3 * width, 256):
            turned[at : at + 256, :] = attn[:, at : at + 256].T

    qkv_t[...] = dot(turned[...], normed_t[...]).astype(BF)
    spans = [slice(head * HEAD_DIM, (head + 1) * HEAD_DIM) for head in range(heads)]
    for head, span in enumerate(spans):
        q = qkv_t[span, :] * jnp.asarray(HEAD_DIM**-0.5, BF)
        scores[head] = t_dot(qkv_t[width + span.start : width + span.stop, :], q)
    shares = []
    for head in range(heads):
        top = jnp.max(scores[head], axis=0, keepdims=True)
        expd = jnp.exp(scores[head] - top)
        total = jnp.sum(expd, axis=0, keepdims=True)
        probs[head] = expd.astype(BF)
        lse[0, head : head + 1, :] = top + jnp.log(total)
        shares.append(1.0 / total)
    for head, span in enumerate(spans):
        v = qkv_t[2 * width + span.start : 2 * width + span.stop, :]
        mixed_t[span, :] = (dot(v, probs[head]) * shares[head]).astype(BF)
    lse[0, heads:, :] = jnp.zeros((lse.shape[1] - heads, lse.shape[2]), FL)
    x = start[...] + t_dot(mixed_t[...], attn[:, 3 * width :])
    middle[...] = x
    xhat, ignored = norm_parts(x)
    normed_two[...] = (xhat * gains[2:3, :] + gains[3:4, :]).astype(BF)


def mlp_tile(chunk, normed_two, up, down, final, hidden, slope):
    count = normed_two.shape[0] // chunk
    rows = lambda i: slice(i * chunk, (i + 1) * chunk)
    pre, low = {0: dot(normed_two[rows(0), :], up[...])}, {}
    for i in range(count + 1):
        if i + 1 < count:
            pre[i + 1] = dot(normed_two[rows(i + 1), :], up[...])
        if i < count:
            value = pre.pop(i)
            cdf, bell = normal_cdf(value)
            low[i] = (value * cdf).astype(BF)
            hidden[rows(i), :] = low[i]
            slope[rows(i), :] = (cdf + value * bell * 0.3989422804014327).astype(BF)
        if i > 0:
            final[rows(i - 1), :] += dot_t(low.pop(i - 1), down[...])


def mlp_kernel(chunk, held, normed_two, up, down, final, hidden, slope):
    @pl.when(pl.program_id(0) == 0)
    def first():
        final[...] = held[...]

    mlp_tile(chunk, normed_two, up, down, final, hidden, slope)


def head_part(
    images, classes, core, final, labels, image_count, gains, own, other,
    d_final, e_low, own_grad, other_grad, row_grads, loss,
):
    tokens = final.shape[0] // images
    width = final.shape[1]
    chalf = own.shape[1]
    gain = gains[4:5, :]
    places = lax.broadcasted_iota(jnp.int32, (8, width), 0)
    means = jnp.zeros((8, width), FL)
    for image in range(images):
        xhat, ignored = norm_parts(final[image * tokens : (image + 1) * tokens, :])
        mean_row = jnp.mean(xhat, axis=0, keepdims=True)
        means = jnp.where(places == image, mean_row, means)
    pooled = jnp.where(places < images, means * gain + gains[5:6, :], 0.0).astype(BF)
    logits = [dot(pooled, own[...]), dot(pooled, other[...])]
    lane = lax.broadcasted_iota(jnp.int32, (8, chalf), 1)
    kinds = [lane + core * chalf, lane + (1 - core) * chalf]
    masked = [jnp.where(kinds[k] < classes, logits[k], -1e30) for k in range(2)]
    top = jnp.maximum(
        jnp.max(masked[0], axis=1, keepdims=True), jnp.max(masked[1], axis=1, keepdims=True)
    )
    expd = [jnp.where(kinds[k] < classes, jnp.exp(masked[k] - top), 0.0) for k in range(2)]
    total = jnp.sum(expd[0], axis=1, keepdims=True) + jnp.sum(expd[1], axis=1, keepdims=True)
    log_total = top + jnp.log(total)
    named = labels[...]
    onehot = [(kinds[k] == named).astype(FL) for k in range(2)]
    target = jnp.sum(onehot[0] * logits[0], axis=1, keepdims=True) + jnp.sum(
        onehot[1] * logits[1], axis=1, keepdims=True
    )
    counted = (named >= 0).astype(FL)
    losses = counted * (log_total - target)
    loss[...] = jnp.broadcast_to(jnp.sum(losses, axis=0, keepdims=True), loss.shape)
    share = counted / image_count[...]
    d_logits = [((expd[k] / total - onehot[k]) * share).astype(BF) for k in range(2)]
    own_grad[...] = t_dot(pooled, d_logits[0])
    other_grad[...] = t_dot(pooled, d_logits[1]).astype(BF)
    d_pooled = dot_t(d_logits[0], own[...]) + dot_t(d_logits[1], other[...])
    row_grads[0:1, :] = jnp.sum(d_pooled * means, axis=0, keepdims=True)
    row_grads[1:2, :] = jnp.sum(d_pooled, axis=0, keepdims=True)
    row_grads[2:8, :] = jnp.zeros((6, width), FL)
    for image in range(images):
        rows = slice(image * tokens, (image + 1) * tokens)
        xhat, inverse = norm_parts(final[rows, :])
        dy = d_pooled[image : image + 1, :] * (1.0 / tokens)
        back = norm_back(xhat, inverse, gain, dy)
        d_final[rows, :] = back
        e_low[rows, :] = back.astype(BF)


def middle_kernel(
    images, classes, chunk, core_ref, held, normed_two, up, down, labels, image_count, gains,
    head_own, head_other, d_final, e_low, own_grad, other_grad, row_grads, loss, hidden, slope, final,
):
    step = pl.program_id(0)

    @pl.when(step == 0)
    def first():
        final[...] = held[...]

    mlp_tile(chunk, normed_two, up, down, final, hidden, slope)

    @pl.when(step == pl.num_programs(0) - 1)
    def head():
        head_part(
            images, classes, core_ref[0], final, labels, image_count, gains, head_own, head_other,
            d_final, e_low, own_grad, other_grad, row_grads, loss,
        )


def mm(a, b, dims):
    return lax.dot_general(a, b, (dims, ((), ())), preferred_element_type=FL)


def norm_two_kernel(
    core_ref, d_normed, middle, d_final, gains, mixed_t, four_grads,
    d_middle, o_low, row_grads, out_grad, sums, product,
):
    image = pl.program_id(0)
    width = middle.shape[1]
    half = width // 2
    xhat, inverse = norm_parts(middle[...])
    dy = d_normed[...]
    back = d_final[...] + norm_back(xhat, inverse, gains[2:3, :], dy)
    d_middle[...] = back
    o_low[...] = back.astype(BF)

    @pl.when(image == 0)
    def first():
        sums[...] = jnp.zeros(sums.shape, FL)
        product[...] = jnp.zeros(product.shape, FL)

    sums[0:1, :] += jnp.sum(dy * xhat, axis=0, keepdims=True)
    sums[1:2, :] += jnp.sum(dy, axis=0, keepdims=True)
    other = pl.multiple_of((1 - core_ref[0]) * half, 128)
    product[...] += dot(mixed_t[...], o_low[:, pl.ds(other, half)])

    @pl.when(image == pl.num_programs(0) - 1)
    def last():
        row_grads[0:2, :] = jnp.zeros((2, width), FL)
        row_grads[2:4, :] = sums[0:2, :]
        row_grads[4:6, :] = four_grads[0:2, :]
        row_grads[6:8, :] = jnp.zeros((2, width), FL)
        out_grad[...] = product[...].astype(BF)


def place(where_ref, row, rows, value, held, keep, send, col):
    size = value.shape[1]
    if send is None:
        keep[:, col : col + size] = value.astype(BF)
        return
    held[:, :size] = value
    half = keep.shape[0]
    for p in range(half):
        low = pl.multiple_of(where_ref[row, p] * rows, rows)
        high = pl.multiple_of(where_ref[row, half + p] * rows, rows)
        keep[p, :, col : col + size] = held[pl.ds(low, rows), :size].astype(BF)
        send[p, :, col : col + size] = held[pl.ds(high, rows), :size].astype(BF)


def split_outs(refs, aligned, number):
    if aligned:
        return [(refs[2 * k], refs[2 * k + 1]) for k in range(number)], refs[2 * number :]
    return [(refs[k], None) for k in range(number)], refs[number:]


class Loads:
    def __init__(self, sems):
        self.sems, self.targets = sems, []

    def add(self, target, *pairs):
        sem = self.sems.at[len(self.targets)]
        for source, place in pairs:
            pltpu.make_async_copy(source, place, sem).start()
        self.targets.append(target)
        return len(self.targets) - 1

    def wait(self, number):
        target = self.targets[number]
        pltpu.make_async_copy(target, target, self.sems.at[number]).wait()


def in_turn(products, stores):
    value = products[0]()
    for number, store in enumerate(stores):
        following = products[number + 1]() if number + 1 < len(products) else None
        store(value)
        value = following


def attend_back_kernel(
    cells_count, final, core_ref, o_low, attn, qkv_t, lse, d_middle, start, gains, cells, grads_in, *refs
):
    sum_in, refs = (refs[0], refs[1:]) if final else (None, refs)
    d_own, sent, sum_out, grads_out, d_qkv_t, d_mixed_t, summed, row_grads = refs[:8]
    scores, d_probs, probs, d_scores = refs[8:]
    width = o_low.shape[1]
    heads = width // HEAD_DIM
    image = pl.program_id(0)

    @pl.when(image == 0)
    def first():
        summed[...] = sum_in[...] if final else jnp.zeros(summed.shape, FL)
        row_grads[...] = grads_in[...]

    scale = HEAD_DIM**-0.5
    d_mixed_t[...] = dot_t(attn[:, 3 * width :], o_low[...]).astype(BF)
    spans = [slice(head * HEAD_DIM, (head + 1) * HEAD_DIM) for head in range(heads)]
    part = lambda ref, k, span: ref[k * width + span.start : k * width + span.stop, :]
    for head, span in enumerate(spans):
        q = part(qkv_t, 0, span) * jnp.asarray(scale, BF)
        scores[head] = t_dot(part(qkv_t, 1, span), q)
        d_probs[head] = t_dot(part(qkv_t, 2, span), d_mixed_t[span, :])
    for head in range(heads):
        soft = jnp.exp(scores[head] - lse[0, head : head + 1, :])
        probs[head] = soft.astype(BF)
        delta = jnp.sum(soft * d_probs[head], axis=0, keepdims=True)
        d_scores[head] = (soft * (d_probs[head] - delta)).astype(BF)
    for head, span in enumerate(spans):
        q = part(qkv_t, 0, span) * jnp.asarray(scale, BF)
        at = span.start
        d_qkv_t[at : at + HEAD_DIM, :] = (
            dot(part(qkv_t, 1, span), d_scores[head]) * scale
        ).astype(BF)
        d_qkv_t[width + at : width + at + HEAD_DIM, :] = dot_t(q, d_scores[head]).astype(BF)
        d_qkv_t[2 * width + at : 2 * width + at + HEAD_DIM, :] = dot_t(
            d_mixed_t[span, :], probs[head]
        ).astype(BF)
    half = width // 2
    for k in range(3):
        for ref, side in ((d_own, core_ref[0]), (sent, 1 - core_ref[0])):
            at = pl.multiple_of(k * width + side * half, 128)
            ref[k * half : (k + 1) * half, :] = d_qkv_t[pl.ds(at, half), :]
    dy = dot(attn[:, : 3 * width], d_qkv_t[...]).T
    xhat, inverse = norm_parts(start[...])
    back = d_middle[...] + norm_back(xhat, inverse, gains[0:1, :], dy)
    sent[3 * half :, :] = back.astype(BF).T
    summed[...] += back
    row_grads[0:1, :] += jnp.sum(dy * xhat, axis=0, keepdims=True)
    row_grads[1:2, :] += jnp.sum(dy, axis=0, keepdims=True)

    @pl.when(image == pl.num_programs(0) - 1)
    def last():
        grads_out[...] = row_grads[...]
        if not final:
            sum_out[...] = summed[...]
            return
        total = lax.dot_general(
            cells[...], summed[...], (((0,), (0,)), ((), ())),
            preferred_element_type=FL, precision=lax.Precision.HIGHEST,
        )
        summed[0:SMALL, :] = total
        summed[cells_count : cells_count + 6, :] = row_grads[0:6, :]
        sum_out[...] = summed[0:SMALL, :].T


def tail_grad_kernel(aligned, rows, spread, where_ref, core_ref, *refs):
    n_parts, own_parts, sent_parts, got_parts, r_parts = (
        refs[:2], refs[2:4], refs[4:6], refs[6:8], refs[8:10]
    )
    (small_hbm, small_got_hbm, mixed_hbm, o_hbm, out_hbm), refs = refs[10:15], refs[15:]
    d_parts, s_parts = (*own_parts, *got_parts), (*sent_parts, *got_parts)
    outs, scratch = split_outs(refs, aligned, 3)
    held, n_t, d_t, s_t, reduced, small, small_got, mixed_t, o_low, out_got, sems = scratch
    half, span = d_t.shape[1], own_parts[0].shape[1]
    width = s_t.shape[0]
    tokens = r_parts[0].shape[0]
    loads = Loads(sems)
    own = pl.multiple_of(core_ref[0] * half, 128)

    def load_tile(tile):
        at = pl.ds(tile * half, half)
        pairs = [(r_parts[k].at[:, at], reduced.at[tile, pl.ds(k * tokens, tokens), :]) for k in range(2)]
        return loads.add(reduced.at[tile], *pairs)

    def load_rows(tile):
        at = pl.ds(tile * half, half)
        pairs = [(d_parts[k].at[at, :], d_t.at[tile, :, pl.ds(k * span, span)]) for k in range(4)]
        return loads.add(d_t.at[tile], *pairs)

    out_ready = [
        loads.add(mixed_t, (mixed_hbm, mixed_t)),
        loads.add(o_low, (o_hbm.at[:, pl.ds(own, half)], o_low)),
        loads.add(out_got, (out_hbm, out_got)),
    ]
    tile_ready = [load_tile(0)]
    s_ready = loads.add(s_t, *[
            (s_parts[k].at[pl.ds(3 * half, width), :], s_t.at[:, pl.ds(k * span, span)])
            for k in range(4)
        ])
    tile_ready += [load_tile(1), load_tile(2), load_tile(3)]
    n_ready = loads.add(n_t, *[(n_parts[k], n_t.at[:, pl.ds(k * tokens, tokens)]) for k in range(2)])
    row_ready = [load_rows(0), load_rows(1), load_rows(2)]
    small_ready = [loads.add(small, (small_hbm, small)), loads.add(small_got, (small_got_hbm, small_got))]

    def put(stream, col, number, value):
        place(where_ref, stream, rows, value, held.at[number], *outs[stream], col)

    def out_product():
        for number in out_ready:
            loads.wait(number)
        return dot(mixed_t[...], o_low[...])

    def out_store(value):
        put(2, half, 0, value + out_got[...].astype(FL))

    def kernel_product(tile):
        if tile == 0:
            loads.wait(s_ready)
        loads.wait(tile_ready[tile])
        return dot(s_t[...], reduced[tile])

    def kernel_store(tile, value):
        for stream, col, lo, hi in spread[tile]:
            put(stream, col, (tile + 1) % 2, value[:, lo:hi])

    def attend_product(tile):
        if tile == 0:
            loads.wait(n_ready)
        loads.wait(row_ready[tile])
        return dot_t(n_t[...], d_t[tile])

    def attend_store(tile, value):
        put(tile, 0, (tile + 1) % 2, value)

    in_turn(
        [out_product]
        + [partial(kernel_product, tile) for tile in range(4)]
        + [partial(attend_product, tile) for tile in range(3)],
        [out_store]
        + [partial(kernel_store, tile) for tile in range(4)]
        + [partial(attend_store, tile) for tile in range(3)],
    )
    for number in small_ready:
        loads.wait(number)
    put(0, half, 0, small[...] + small_got[...])


def square_kernel(low, high, loss, *refs):
    *parts, out = refs
    total = jnp.zeros((1, 1), FL)

    def squares(value):
        value = value.astype(FL)
        return jnp.sum(jnp.sum(value * value, axis=0, keepdims=True), axis=1, keepdims=True)

    for number, part in enumerate(parts):
        total += squares(part[...])
        if number == 0:
            total -= 0.5 * squares(part[:, low:high])
    lane = lax.broadcasted_iota(jnp.int32, out.shape, 1)
    out[...] = jnp.where(lane == 0, total, jnp.where(lane == 1, loss[...], 0.0))


def update_kernel(cells, classes, spread, core_ref, sums, turned, *refs):
    grads, refs = refs[:10], refs[10:]
    olds, news, lows = refs[:18], refs[18:36], refs[36:]
    core = core_ref[0]
    norm = jnp.sqrt(sums[0:1, 0:1])
    factor = jnp.minimum(1.0, CLIP / norm)

    def step(table, cols, gradient, rate, decay, low):
        weight, first, second = (olds[6 * k + table][cols] for k in range(3))
        results = adam_step(weight, first, second, gradient.astype(FL) * factor, rate, decay)
        for k in range(3):
            news[6 * k + table][cols] = results[k]
        if low is not None:
            lows[low][cols] = results[0].astype(BF)

    def part(side, index, lo, size):
        return grads[5 * side + index][:, lo : lo + size]

    def cols(base, side, half):
        place = 1 - core if side else core
        return (slice(None), pl.ds(pl.multiple_of(base + place * half, 128), half))

    width = olds[2].shape[1] // 4
    fhalf, half, khalf = olds[3].shape[1] // 4, width // 2, olds[0].shape[1] // 2
    chalf = grads[3].shape[1] - fhalf
    for side in range(2):
        for k in range(3):
            step(2, cols(k * width, side, half), part(side, k, 0, half), RATE, DECAY, 1)
        step(2, cols(3 * width, side, half), part(side, 2, half, half), RATE, DECAY, 1)
        place = 1 - core if side else core
        for tile in range(4):
            for stream, col, lo, hi in spread[tile]:
                at = pl.multiple_of(place * khalf + tile * half + lo, 128)
                value = part(side, stream, col, hi - lo)
                step(0, (slice(None), pl.ds(at, hi - lo)), value, RATE, DECAY, 0)
        for k in range(2):
            step(3, cols(k * 2 * fhalf, side, fhalf), part(side, 4 - k, 0, fhalf), RATE, DECAY, 2)
    own, other = part(0, 3, fhalf, chalf), part(1, 3, fhalf, chalf)
    low_half = jnp.where(core == 0, own.astype(FL), other.astype(FL))
    high_half = jnp.where(core == 0, other.astype(FL), own.astype(FL))
    step(4, (slice(None), slice(0, chalf)), low_half, RATE, DECAY, 3)
    step(4, (slice(None), slice(chalf, classes)), high_half[:, : classes - chalf], RATE, DECAY, 3)
    tiny = part(0, 0, half, SMALL)
    step(1, (slice(None), slice(0, cells)), tiny[:, :cells], RATE_TABLE, 0.0, None)

    @pl.when(pl.program_id(0) == 0)
    def gains():
        on_side = turned[:, half : half + SMALL].astype(FL).T
        step(5, (slice(None), slice(None)), on_side[cells : cells + 6, :], RATE_TABLE, 0.0, None)


def body(
    count,
    pixels,
    patch_kind,
    labels,
    resize,
    embed_kernel,
    pos_base,
    gains,
    attn_weight,
    mlp_weight,
    head_weight,
    embed_first,
    pos_first,
    gains_first,
    attn_first,
    mlp_first,
    head_first,
    embed_second,
    pos_second,
    gains_second,
    attn_second,
    mlp_second,
    head_second,
):
    me = lax.axis_index("fsdp")
    core = lax.axis_index("rep")
    core_at = core.astype(jnp.int32)[None]
    images, tokens = pixels.shape[:2]
    total = images * tokens
    rows, width = attn_weight.shape[0], attn_weight.shape[0] * count
    aligned = rows % 16 == 0 and count & (count - 1) == 0
    ffw = mlp_weight.shape[1] // 2
    classes = head_weight.shape[1]
    kdim = embed_kernel.shape[0]
    cells_count = pos_base.shape[0]
    feats, base = resize.shape[1:]
    chalf = -(-classes // 256) * 128
    half, fhalf, khalf = width // 2, ffw // 2, kdim // 2
    heads = width // HEAD_DIM
    lse_rows = -(-heads // 8) * 8
    chunk = min(total, 256)
    tiles = fhalf // TILE

    other_first = (khalf - 256) // 2
    widths = (width + 256 + SMALL, half + other_first, half + other_first)
    pieces = call(
        partial(prepare_kernel, cells_count),
        (1,),
        [
            whole((rows, kdim)),
            whole((rows, cells_count)),
            whole((6, rows)),
            whole((rows, 4 * width)),
        ],
        [whole((rows, size)) for size in widths],
        [sds((rows, size), BF) for size in widths],
        scratch=[pltpu.VMEM((128, 128), FL)],
        prefetch=2,
        limit=MOST,
    )(core_at, labels, embed_kernel.T, pos_base.T, gains, attn_weight)
    mlp_in, *pieces = tie(mlp_weight, *pieces)
    rest = call(
        prepare_rest_kernel,
        (1,),
        [whole((rows, 2 * ffw)), whole((rows, classes))],
        whole((rows, ffw + chalf)),
        sds((rows, ffw + chalf), BF),
        prefetch=1,
        limit=MOST,
    )(core_at, mlp_in, head_weight)

    fan_orders = [
        order_of(count, [1, 4, 8, 2]),
        order_of(count, [2, 1, 4, 8]),
        order_of(count, [4, 2, 1, 8]),
    ]
    if aligned:
        near, far, rest = gather_relative(pieces, count, fan_orders, rest, len(bits_of(count)) - 1)
        *near, patch_kind = tie(*near, patch_kind)
    rest_own = lax.all_gather(rest, "fsdp", axis=0, tiled=True)
    r_own, r_other = call(
        reduce_kernel,
        (images,),
        [
            pl.BlockSpec((1, 3 * feats, tokens), lambda b, kind, c: (b, 0, 0)),
            pl.BlockSpec((1, feats, base), lambda b, kind, c: (kind[b], 0, 0)),
        ],
        [pl.BlockSpec((tokens, khalf), lambda b, kind, c: (b, 0))] * 2,
        [sds((total, khalf), BF)] * 2,
        prefetch=2,
    )(patch_kind, core_at, jnp.transpose(pixels, (0, 2, 1)), resize)

    if aligned:
        *far, r_own, r_other = tie(*far, r_own, r_other)
        gathered = []
        for one, two in zip(near, far):
            gathered += [one, two, other_core(one), other_core(two)]
        where_fan = jnp.stack(
            [me ^ jnp.array(relative_masks(order), jnp.int32) for order in fan_orders]
        )
        plan = (
            (
                (0, half, 1, 0, half),
                (half, half, 1, width, half),
                (width, 256, 0, 0, khalf),
                (width + 256, SMALL, 2, 0, 0),
            ),
            ((0, half, 1, 2 * width, half), (half, other_first, 0, 256, khalf)),
            ((0, half, 1, 3 * width, half), (half, other_first, 0, 256 + other_first, khalf)),
        )
    else:
        where_fan = jnp.zeros((3, count), jnp.int32)
        own = [lax.all_gather(piece, "fsdp", axis=0, tiled=True) for piece in pieces]
        other = [other_core(value) for value in own]

        def joined(parts):
            one, two, three = parts
            return (
                jnp.concatenate([one[:, width : width + 256], two[:, half:], three[:, half:]], axis=1),
                jnp.stack([one[:, :half], one[:, half:width], two[:, :half], three[:, :half]], axis=1),
                one[:, width + 256 :],
            )

        own_e, own_a, small = joined(own)
        other_e, other_a, small_other = joined(other)
        kernel_t = jnp.concatenate([own_e, other_e], axis=1)
        attn_low = jnp.stack(halves(own_a, other_a, core), axis=2).reshape(width, 4 * width)
        gain_rows = jnp.pad(small[:, cells_count : cells_count + 6].astype(FL).T, ((0, 2), (0, 0)))
        number = (small[:, cells_count + 6] + small_other[:, cells_count + 6]).astype(FL)
        image_count = (jnp.sum(number) / rows)[None, None]

    table = np.zeros((tokens, SMALL), np.float32)
    table[:, :cells_count] = grid_matrix()
    high = table.astype(jnp.bfloat16)
    low = (table - high.astype(np.float32)).astype(jnp.bfloat16)
    by_image = pl.BlockSpec((tokens, width), lambda b, *c: (b, 0))
    by_lane = pl.BlockSpec((width, tokens), lambda b, *c: (0, b))
    qkv_spec = pl.BlockSpec((3 * width, tokens), lambda b, *c: (0, b))
    lse_spec = pl.BlockSpec((1, lse_rows, tokens), lambda b, *c: (b, 0, 0))
    if aligned:
        weights_in = gathered
        weight_specs = [pl.BlockSpec(memory_space=pltpu.HBM)] * 12
        more_out = [sds((width, 4 * width), BF), sds((8, width), FL), sds((1, 1), FL)]
        more_scratch = [
            pltpu.VMEM((width, kdim), BF),
            pltpu.VMEM((width, SMALL), BF),
            pltpu.VMEM((width, SMALL), BF),
            pltpu.SemaphoreType.DMA((4,)),
        ]
    else:
        plan = None
        weights_in = (kernel_t, attn_low, small, small_other, gain_rows, image_count)
        weight_specs = [whole(item.shape) for item in weights_in]
        more_out, more_scratch = [], []
    start, normed_t, qkv_t, mixed_t, lse, middle, normed_two, *more = call(
        partial(forward_kernel, plan, cells_count),
        (images,),
        weight_specs + [pl.BlockSpec((tokens, khalf), lambda b, *c: (b, 0))] * 2
        + [whole((tokens, 2 * SMALL))],
        [by_image, by_lane, qkv_spec, by_lane, lse_spec, by_image, by_image]
        + [whole(item.shape) for item in more_out],
        [
            sds((total, width), FL),
            sds((width, total), BF),
            sds((3 * width, total), BF),
            sds((width, total), BF),
            sds((images, lse_rows, tokens), FL),
            sds((total, width), FL),
            sds((total, width), BF),
        ]
        + more_out,
        scratch=[
            pltpu.VMEM((3 * width, width), BF),
            pltpu.VMEM((heads, tokens, tokens), FL),
            pltpu.VMEM((heads, tokens, tokens), BF),
        ]
        + more_scratch,
        limit=MOST,
        prefetch=2,
    )(where_fan, core_at, *weights_in, r_own, r_other, jnp.asarray(np.concatenate([high, low], axis=1)))
    if aligned:
        attn_low, gain_rows, image_count = more
    rest_own, normed_two = tie(rest_own, normed_two)
    rest_other = other_core(rest_own)
    r_got, n_got = other_core(r_other), other_core(normed_t)

    col = lambda offset: pl.BlockSpec((width, TILE), lambda j: (0, offset + j))
    tile_spec = pl.BlockSpec((total, TILE), lambda j: (0, j))
    final, hidden, slope = call(
        partial(mlp_kernel, chunk),
        (tiles,),
        [whole((total, width)), whole((total, width)), col(0), col(tiles)],
        [whole((total, width)), tile_spec, tile_spec],
        [sds((total, width), FL), sds((total, fhalf), BF), sds((total, fhalf), BF)],
        limit=MOST,
    )(middle, normed_two, rest_own, rest_own)

    labels_col = jnp.pad(labels, (0, 8 - images), constant_values=-1)[:, None]
    head_spec = pl.BlockSpec((width, chalf), lambda i, c: (0, ffw // chalf))
    colc = lambda offset: pl.BlockSpec((width, TILE), lambda j, c: (0, offset + j))
    tilec = pl.BlockSpec((total, TILE), lambda j, c: (0, j))
    (
        d_final, e_low, head_own, head_other, four_grads, loss_part, hidden_other, slope_other,
    ) = call(
        partial(middle_kernel, images, classes, chunk),
        (tiles,),
        [
            whole((total, width)),
            whole((total, width)),
            colc(0),
            colc(tiles),
            whole((8, 1)),
            whole((1, 1)),
            whole((8, width)),
            head_spec,
            head_spec,
        ],
        [
            whole((total, width)),
            whole((total, width)),
            whole((width, chalf)),
            whole((width, chalf)),
            whole((8, width)),
            whole((8, 128)),
            tilec,
            tilec,
        ],
        [
            sds((total, width), FL),
            sds((total, width), BF),
            sds((width, chalf), FL),
            sds((width, chalf), BF),
            sds((8, width), FL),
            sds((8, 128), FL),
            sds((total, fhalf), BF),
            sds((total, fhalf), BF),
        ],
        scratch=[pltpu.VMEM((total, width), FL)],
        prefetch=1,
    )(
        core_at, final, normed_two, rest_other, rest_other, labels_col, image_count, gain_rows,
        rest_own, rest_other,
    )

    up_of = lambda part: part[:, :fhalf]
    down_of = lambda part: part[:, fhalf:ffw]
    down_other = mm(e_low, hidden_other, ((0,), (0,))).astype(BF)
    down_got, head_got = other_core(down_other), other_core(head_other)
    e_one, ignored = tie(e_low, down_other)
    d_pre_other = (
        mm(e_one, down_of(rest_other), ((1,), (0,))) * slope_other.astype(FL)
    ).astype(BF)
    d_head = (head_own + head_got.astype(FL)).astype(BF)
    e_two, ignored = tie(e_one, d_pre_other)
    d_down = (mm(e_two, hidden, ((0,), (0,))) + down_got.astype(FL)).astype(BF)

    def split_shapes(size):
        if aligned:
            return [sds((count // 2, rows, size), BF)] * 2
        return [sds((width, size), BF)]

    def split_specs(size):
        return [whole(item.shape) for item in split_shapes(size)]

    def begin(parts, order):
        keep, send, held = split_sides(parts, count, order, me)
        return partner(send, count, order[0]), keep, held, order, me

    def arrive(flows, *others):
        given = tie(*[flow[0] for flow in flows], *others)
        following = []
        for (ignored, keep, held, order, who), got in zip(flows, given):
            keep, send, held = step_sides(keep, got, held, order[1:], who)
            got = None if send is None else partner(send, count, order[1])
            following.append((got, keep, held, order[1:], who))
        return following, given[len(flows) :]

    if aligned:
        flow_down = begin([d_down, d_head], order_of(count, [1, 4, 8, 2]))
    d_pre_other, ignored = tie(d_pre_other, d_down)
    up_other = mm(normed_two, d_pre_other, ((0,), (0,))).astype(BF)
    up_got = other_core(up_other)
    e_three, ignored = tie(e_two, up_other)
    d_pre = (mm(e_three, down_of(rest_own), ((1,), (0,))) * slope.astype(FL)).astype(BF)
    d_up = (mm(normed_two, d_pre, ((0,), (0,))) + up_got.astype(FL)).astype(BF)
    if aligned:
        flow_up = begin([d_up], order_of(count, [2, 1, 4, 8]))
    d_pre, d_pre_other, ignored = tie(d_pre, d_pre_other, d_up)
    d_normed_two = mm(d_pre_other, up_of(rest_other), ((1,), (1,))) + mm(
        d_pre, up_of(rest_own), ((1,), (1,))
    )
    row_image = pl.BlockSpec((tokens, width), lambda b, c: (b, 0))
    d_middle, o_low, grads_in, out_other = call(
        norm_two_kernel,
        (images,),
        [
            row_image,
            row_image,
            row_image,
            whole((8, width)),
            pl.BlockSpec((width, tokens), lambda b, c: (0, b)),
            whole((8, width)),
        ],
        [row_image, row_image, whole((8, width)), whole((width, half))],
        [
            sds((total, width), FL),
            sds((total, width), BF),
            sds((8, width), FL),
            sds((width, half), BF),
        ],
        scratch=[pltpu.VMEM((8, width), FL), pltpu.VMEM((width, half), FL)],
        prefetch=1,
    )(core_at, d_normed_two, middle, d_final, gain_rows, mixed_t, four_grads)
    out_got = other_core(out_other)
    pair = max(images // 2, 1)
    shift = lambda k: [
        pl.BlockSpec((tokens, width), lambda b, c: (b + k, 0)),
        pl.BlockSpec((3 * width, tokens), lambda b, c: (0, b + k)),
        pl.BlockSpec((1, lse_rows, tokens), lambda b, c: (b + k, 0, 0)),
        pl.BlockSpec((width, tokens), lambda b, c: (0, b + k)),
    ]

    def attend_back(k, final, grads_in, o_low, sum_in=()):
        image_spec, qkvs, lses, lanes = shift(k)
        sums = sds((width, SMALL), FL) if final else sds((tokens, width), FL)
        own_lanes = lambda size: pl.BlockSpec((size, tokens), lambda b, c: (0, b))
        return call(
            partial(attend_back_kernel, cells_count, final),
            (pair,),
            [
                image_spec,
                whole((width, 4 * width)),
                qkvs,
                lses,
                image_spec,
                image_spec,
                whole((8, width)),
                whole((tokens, SMALL)),
                whole((8, width)),
            ]
            + [whole((tokens, width))] * len(sum_in),
            [own_lanes(3 * half), own_lanes(3 * half + width), whole(sums.shape), whole((8, width))],
            [
                sds((3 * half, pair * tokens), BF),
                sds((3 * half + width, pair * tokens), BF),
                sums,
                sds((8, width), FL),
            ],
            scratch=[
                pltpu.VMEM((3 * width, tokens), BF),
                pltpu.VMEM((width, tokens), BF),
                pltpu.VMEM((tokens, width), FL),
                pltpu.VMEM((8, width), FL),
                pltpu.VMEM((heads, tokens, tokens), FL),
                pltpu.VMEM((heads, tokens, tokens), FL),
                pltpu.VMEM((heads, tokens, tokens), BF),
                pltpu.VMEM((heads, tokens, tokens), BF),
            ],
            prefetch=1,
            limit=MORE,
        )(core_at, o_low, attn_low, qkv_t, lse, d_middle, start, gain_rows, jnp.asarray(table), grads_in, *sum_in)

    d_own_one, sent_one, sum_one, grads_one = attend_back(0, False, grads_in, o_low)
    if aligned:
        (flow_down, flow_up), (sum_one, sent_one) = arrive([flow_down, flow_up], sum_one, sent_one)
    got_one = other_core(sent_one)
    d_own_two, sent_two, d_small, ignored = attend_back(pair, True, grads_one, o_low, (sum_one,))
    if aligned:
        (flow_down, flow_up), (sent_two, d_small) = arrive([flow_down, flow_up], sent_two, d_small)
    got_two, small_got = other_core(sent_two), other_core(d_small)

    spread = (
        ((0, half + SMALL, 0, half),),
        ((1, half, 0, half),),
        ((1, 2 * half, 0, 2 * SMALL), (0, 2 * half + SMALL, 2 * SMALL, half)),
        ((0, 2 * half + 2 * SMALL, 0, SMALL), (2, 2 * half, SMALL, half)),
    )
    tail_widths = (2 * half + 3 * SMALL, 2 * half + 2 * SMALL, 3 * half - SMALL)
    tail_parts = call(
        partial(tail_grad_kernel, aligned, rows, spread),
        (1,),
        [pl.BlockSpec(memory_space=pltpu.HBM)] * 15,
        [spec for size in tail_widths for spec in split_specs(size)],
        [shape for size in tail_widths for shape in split_shapes(size)],
        scratch=[
            pltpu.VMEM((2, width, half), FL),
            pltpu.VMEM((width, 2 * total), BF),
            pltpu.VMEM((3, half, 2 * total), BF),
            pltpu.VMEM((width, 4 * pair * tokens), BF),
            pltpu.VMEM((4, 2 * total, half), BF),
            pltpu.VMEM((width, SMALL), FL),
            pltpu.VMEM((width, SMALL), FL),
            pltpu.VMEM((width, total), BF),
            pltpu.VMEM((total, half), BF),
            pltpu.VMEM((width, half), BF),
            pltpu.SemaphoreType.DMA((14,)),
        ],
        limit=MORE,
        prefetch=2,
    )(
        where_fan, core_at, normed_t, n_got, d_own_one, d_own_two, sent_one, sent_two, got_one, got_two,
        r_own, r_got, d_small, small_got,
        mixed_t, o_low, out_got,
    )
    if aligned:
        (flow_down, flow_up), tail_parts = arrive([flow_down, flow_up], *tail_parts)
        flows = [flow_down, flow_up]
        for k, order in enumerate(fan_orders):
            keep, send = tail_parts[2 * k : 2 * k + 2]
            shape = (2,) * (len(order) - 1) + keep.shape[1:]
            got = partner(send, count, order[0]).reshape(shape)
            flows.append((got, keep.reshape(shape), order[1:], order, None))
        while any(flow[0] is not None for flow in flows):
            live = [k for k, flow in enumerate(flows) if flow[0] is not None]
            after, ignored = arrive([flows[k] for k in live])
            for k, flow in zip(live, after):
                flows[k] = flow
        g_down, g_up, *g_tail = [flow[1] for flow in flows]
    else:
        g_down, g_up, *g_tail = [
            lax.psum_scatter(part, "fsdp", scatter_dimension=0, tiled=True)
            for part in (jnp.concatenate([d_down, d_head], axis=1), d_up, *tail_parts)
        ]

    own_shards = [*g_tail, g_down, g_up]
    other_shards = [other_core(item) for item in own_shards]
    sums = call(
        partial(square_kernel, half, half + SMALL),
        (1,),
        [whole((8, 128))] + [whole(item.shape) for item in own_shards],
        whole((8, 128)),
        sds((8, 128), FL),
    )(loss_part, *own_shards)
    sums = sum_everywhere(sums, count)
    tables = (embed_kernel.T, pos_base.T, attn_weight, mlp_weight, head_weight, gains)
    firsts = (embed_first.T, pos_first.T, attn_first, mlp_first, head_first, gains_first)
    seconds = (embed_second.T, pos_second.T, attn_second, mlp_second, head_second, gains_second)
    block = 16 if rows % 16 == 0 else rows

    def by_rows(item):
        if item.shape[0] != rows:
            return whole(item.shape)
        return pl.BlockSpec((block, item.shape[1]), lambda i, c: (i, 0))

    olds = (*tables, *firsts, *seconds)
    lows = [sds(tables[k].shape, BF) for k in (0, 2, 3, 4)]
    outs = call(
        partial(update_kernel, cells_count, classes, spread),
        (rows // block,),
        [whole((8, 128)), whole(g_tail[0].shape)]
        + [by_rows(item) for item in (*own_shards, *other_shards, *olds)],
        [by_rows(item) for item in (*olds, *lows)],
        [sds(item.shape, FL) for item in olds] + lows,
        prefetch=1,
    )(core_at, sums, g_tail[0], *own_shards, *other_shards, *olds)
    new, low = outs[:18], outs[18:]
    sets = [
        (new[6 * k].T, new[6 * k + 1].T, new[6 * k + 5], *new[6 * k + 2 : 6 * k + 5])
        for k in range(3)
    ]
    return (
        sums[0, 1],
        image_count[0, 0],
        jnp.sqrt(sums[0, 0]),
        *sets[0],
        *sets[1],
        *sets[2],
        low[0].T,
        *low[1:],
    )


def solution(mesh):
    data = P(("rep", "fsdp"))
    columns, rows = P(None, "fsdp"), P("fsdp", None)
    table = (columns, columns, columns, rows, rows, rows)
    in_specs = (P(("rep", "fsdp"), None, None), data, data, P()) + table * 3
    out_specs = (P(), P(), P()) + table * 3 + (columns, rows, rows, rows)
    return jax.shard_map(
        partial(body, mesh.shape["fsdp"]),
        mesh=mesh,
        in_specs=in_specs,
        out_specs=out_specs,
        check_vma=False,
    )
```

```python
from functools import partial

import jax
import jax.numpy as jnp
import numpy as np
from jax import lax
from jax.experimental import pallas as pl
from jax.experimental.pallas import tpu as pltpu
from jax.sharding import PartitionSpec as P

HEAD_DIM = 64
BASE = 32
GRID0 = 7
MAXP = 24
GRID = 16
STEP = 10
SIDES = (10, 15, 24)

NORM_EPS = 1e-06
CLIP = 0.02
BETA_ONE = 0.9
BETA_TWO = 0.999
ADAM_EPS = 1e-08
RATE = 0.1
RATE_TABLE = 1.0
DECAY = 0.05
BF = jnp.bfloat16
FL = jnp.float32
SMALL = 128
TILE = 512
LIMIT = 30 * 1024 * 1024
MORE = 40 * 1024 * 1024
MOST = 58 * 1024 * 1024


def grid_matrix():
    target = (np.arange(GRID, dtype=np.float32) + np.float32(0.5)) * (GRID0 / GRID) - 0.5
    target = np.clip(target, 0.0, GRID0 - 1.0)
    source = np.arange(GRID0, dtype=np.float32)
    line = np.maximum(0.0, 1.0 - np.abs(target[:, None] - source[None, :]))
    return (line[:, None, :, None] * line[None, :, None, :]).reshape(GRID * GRID, GRID0 * GRID0)


def adam_step(weight, first_old, second_old, gradient, step_rate, decay_rate):
    first_new = BETA_ONE * first_old + (1.0 - BETA_ONE) * gradient
    second_new = BETA_TWO * second_old + (1.0 - BETA_TWO) * gradient * gradient
    first_hat = first_new / (1.0 - BETA_ONE**STEP)
    second_hat = second_new / (1.0 - BETA_TWO**STEP)
    weight_new = weight - step_rate * (
        first_hat / (jnp.sqrt(second_hat) + ADAM_EPS) + decay_rate * weight
    )
    return (weight_new, first_new, second_new)


def partner(value, count, mask):
    return lax.ppermute(value, "fsdp", [(i, i ^ mask) for i in range(count)])


def other_core(value):
    return lax.ppermute(value, "rep", [(0, 1), (1, 0)])


def bits_of(count):
    return [1 << k for k in range(count.bit_length() - 1)]


def order_of(count, preferred):
    return preferred if sorted(preferred) == bits_of(count) else bits_of(count)


def relative_masks(order):
    masks = [0]
    for mask in reversed(order):
        masks = masks + [held ^ mask for held in masks]
    return masks


def tie(*values):
    return lax.optimization_barrier(values)


def gather_relative(shards, count, orders, late, late_step):
    held = [shard[None] for shard in shards]
    for step in range(len(orders[0]) - 1, 0, -1):
        got = [partner(value, count, order[step]) for value, order in zip(held, orders)]
        if step == late_step:
            *got, late = tie(*got, late)
        else:
            got = tie(*got)
        held = [jnp.concatenate(pair, axis=0) for pair in zip(held, got)]
    return held, [partner(value, count, order[0]) for value, order in zip(held, orders)], late


def axis_of(mask, held_masks):
    return held_masks.index(mask)


def side_of(value, mask, held_masks, me, other):
    if me is None:
        return lax.index_in_dim(value, int(other), axis_of(mask, held_masks), keepdims=False)
    bit = jnp.where((me & mask) != 0, 1, 0)
    at = 1 - bit if other else bit
    return lax.dynamic_index_in_dim(value, at, axis_of(mask, held_masks), keepdims=False)


def split_sides(parts, count, order, me):
    held = bits_of(count)[::-1]
    shaped = [part.reshape((2,) * len(held) + (part.shape[0] // count, -1)) for part in parts]
    sides = []
    for other in (False, True):
        pieces = []
        for value in shaped:
            for number, mask in enumerate(order):
                if number == 0:
                    value = side_of(value, mask, held, me, other)
            pieces.append(value)
        sides.append(jnp.concatenate(pieces, axis=-1))
    return sides[0], sides[1], [mask for mask in held if mask != order[0]]


def step_sides(keep, got, held, order, me):
    if not order:
        total = keep.astype(FL) + got.astype(FL)
        return total.astype(BF), None, held
    mask = order[0]
    sides = [
        (
            side_of(keep, mask, held, me, other).astype(FL)
            + side_of(got, mask, held, me, other).astype(FL)
        ).astype(BF)
        for other in (False, True)
    ]
    return sides[0], sides[1], [bit for bit in held if bit != mask]


def sum_everywhere(value, count):
    value = value + other_core(value)
    bits = bits_of(count)
    while bits:
        pair, bits = bits[:2], bits[2:]
        got = [partner(value, count, mask) for mask in (*pair, sum(pair))[: 2 * len(pair) - 1]]
        value = value + got[0]
        if len(pair) == 2:
            value = value + (got[1] + got[2])
    return value


def halves(own, other, core):
    return jnp.where(core == 0, own, other), jnp.where(core == 0, other, own)


def dot(a, b):
    return lax.dot_general(a, b, (((1,), (0,)), ((), ())), preferred_element_type=FL)


def dot_t(a, b):
    return lax.dot_general(a, b, (((1,), (1,)), ((), ())), preferred_element_type=FL)


def t_dot(a, b):
    return lax.dot_general(a, b, (((0,), (0,)), ((), ())), preferred_element_type=FL)


def call(kernel, grid, in_specs, out_specs, out_shape, scratch=(), prefetch=0, limit=LIMIT):
    return pl.pallas_call(
        kernel,
        grid_spec=pltpu.PrefetchScalarGridSpec(
            num_scalar_prefetch=prefetch,
            grid=grid,
            in_specs=in_specs,
            out_specs=out_specs,
            scratch_shapes=list(scratch),
        ),
        out_shape=out_shape,
        compiler_params=pltpu.CompilerParams(vmem_limit_bytes=limit),
        cost_estimate=pl.CostEstimate(flops=1, bytes_accessed=1, transcendentals=0),
    )


def whole(shape):
    zeros = (0,) * len(shape)
    return pl.BlockSpec(shape, lambda *a: zeros, pipeline_mode=pl.Buffered(1))


def sds(shape, dtype):
    return jax.ShapeDtypeStruct(shape, dtype)


def norm_parts(values_in):
    row_mean = jnp.mean(values_in, axis=-1, keepdims=True)
    centered = values_in - row_mean
    row_var = jnp.mean(centered * centered, axis=-1, keepdims=True)
    inverse = lax.rsqrt(row_var + NORM_EPS)
    return centered * inverse, inverse


def norm_back(xhat, inverse, gain, dy):
    gained = dy * gain
    one = jnp.mean(gained, axis=-1, keepdims=True)
    two = jnp.mean(gained * xhat, axis=-1, keepdims=True)
    return inverse * (gained - one - xhat * two)


def normal_cdf(x):
    return 0.5 + 0.5 * lax.erf(x * 0.7071067811865476), jnp.exp(-0.5 * x * x)


def prepare_kernel(cells, core_ref, labels_ref, embed, pos, gains, attn, one, two, three, held):
    core = core_ref[0]
    rows, width = attn.shape[0], attn.shape[1] // 4
    half, khalf = width // 2, embed.shape[1] // 2

    def cols(ref, base, step, size):
        return ref[:, pl.ds(pl.multiple_of(base + core * step, 128), size)].astype(BF)

    first, second = one.shape[1] - 2 * half - SMALL, two.shape[1] - half
    third = three.shape[1] - half
    one[:, :half] = cols(attn, 0, half, half)
    one[:, half : 2 * half] = cols(attn, width, half, half)
    one[:, 2 * half : 2 * half + first] = cols(embed, 0, khalf, first)
    two[:, :half] = cols(attn, 2 * width, half, half)
    two[:, half:] = cols(embed, first, khalf, second)
    three[:, :half] = cols(attn, 3 * width, half, half)
    three[:, half:] = cols(embed, first + second, khalf, third)
    total = jnp.int32(0)
    for image in range(labels_ref.shape[0]):
        total = total + jnp.where(labels_ref[image] >= 0, 1, 0)
    held[...] = jnp.zeros(held.shape, FL)
    held[cells : cells + 6, :rows] = gains[...]
    held[cells + 6 : cells + 7, :] = jnp.full((1, held.shape[1]), total.astype(FL))
    turned = held[...].T
    one[:, 2 * half + first :] = turned[:rows].astype(BF)
    one[:, 2 * half + first : 2 * half + first + cells] = pos[...].astype(BF)


def prepare_rest_kernel(core_ref, mlp, head, rest):
    core = core_ref[0]
    rows, fhalf = mlp.shape[0], mlp.shape[1] // 4

    def cols(base):
        return mlp[:, pl.ds(pl.multiple_of(base + core * fhalf, 128), fhalf)].astype(BF)

    rest[:, :fhalf] = cols(0)
    rest[:, fhalf : 2 * fhalf] = cols(2 * fhalf)
    chalf = rest.shape[1] - 2 * fhalf
    classes = head.shape[1]
    low_half = head[:, :chalf]
    high_half = jnp.concatenate(
        [head[:, chalf:classes], jnp.zeros((rows, 2 * chalf - classes), FL)], axis=1
    )
    rest[:, 2 * fhalf :] = jnp.where(core == 0, low_half, high_half).astype(BF)


def reduce_kernel(kind_ref, core_ref, pixels, resize, own, other):
    kind = kind_ref[pl.program_id(0)]
    side = jnp.where(kind == 0, SIDES[0], jnp.where(kind == 1, SIDES[1], SIDES[2]))
    feats, base = resize.shape[1], resize.shape[2]
    place = lax.broadcasted_iota(jnp.int32, (feats, base), 0)
    chosen = jnp.where(place < side * side, resize[0].astype(FL), 0.0).astype(BF)
    factor = 0.25 / side.astype(FL)
    half = own.shape[1]
    values = []
    for channel in range(3):
        part = pixels[0, channel * feats : (channel + 1) * feats, :]
        values.append((t_dot(part, chosen) * factor).astype(BF))
    for core, sides in enumerate(((own, other), (other, own))):
        @pl.when(core_ref[0] == core)
        def store(sides=sides):
            for channel, value in enumerate(values):
                lo, hi = channel * base, (channel + 1) * base
                for number, side in enumerate(sides):
                    left, right = max(lo, number * half), min(hi, (number + 1) * half)
                    if left < right:
                        side[:, left - number * half : right - number * half] = value[
                            :, left - lo : right - lo
                        ]


def start_pieces(plan, where_ref, core, pieces, targets, sems, later):
    rows, half = pieces[0].shape[1], pieces[0].shape[0]

    def one_block(p, ignored):
        for stream in range(3):
            for top in range(2):
                at = pl.multiple_of(where_ref[stream, p + top * half] * rows, rows)
                for swapped in range(2):
                    source = pieces[4 * stream + 2 * swapped + top]
                    for src, size, target, base, step in plan[stream]:
                        if (target == 1) != later:
                            continue
                        if target == 2:
                            dst = targets[2 + swapped].at[pl.ds(at, rows), :]
                            sem = sems.at[2 + swapped]
                        else:
                            side = 1 - core if swapped else core
                            if target == 0:
                                side = swapped
                            col = pl.multiple_of(base + side * step, 128)
                            dst = targets[target].at[pl.ds(at, rows), pl.ds(col, size)]
                            sem = sems.at[target]
                        pltpu.make_async_copy(
                            source.at[p, :, pl.ds(src, size)], dst, sem
                        ).start()
        return ignored

    lax.fori_loop(0, half, one_block, 0)


def forward_kernel(plan, cells_count, where_ref, core_ref, *refs):
    joined = plan is not None
    weights, refs = (refs[:12], refs[12:]) if joined else (refs[:6], refs[6:])
    (reduced, reduced_other, cells), refs = refs[:3], refs[3:]
    start, normed_t, qkv_t, mixed_t, lse, middle, normed_two = refs[:7]
    refs = refs[7:]
    if joined:
        attn, gains, counts, turned, scores, probs, kernel_t, small, small_other, sems = refs
        targets = (kernel_t, attn, small, small_other)
    else:
        kernel_t, attn, small, small_other, gains, counts = weights
        turned, scores, probs = refs
    width = normed_t.shape[0]
    heads = width // HEAD_DIM
    first_image = pl.program_id(0) == 0

    if joined:
        @pl.when(first_image)
        def arrive():
            for later in (False, True):
                start_pieces(plan, where_ref, core_ref[0], weights, targets, sems, later)
            for number in (0, 2, 3):
                pltpu.make_async_copy(targets[number], targets[number], sems.at[number]).wait()
            rows = weights[0].shape[1]
            on_side = small[...].astype(FL).T
            gains[0:6, :] = on_side[cells_count : cells_count + 6, :]
            gains[6:8, :] = jnp.zeros((2, width), FL)
            at = slice(cells_count + 6, cells_count + 7)
            number = on_side[at, :] + small_other[...].astype(FL).T[at, :]
            counts[...] = jnp.sum(number, axis=1, keepdims=True) * (1.0 / rows)

    posemb = dot_t(cells[:, :SMALL], small[...]) + dot_t(cells[:, SMALL:], small[...])
    khalf = reduced.shape[1]
    x = dot_t(reduced[...], kernel_t[:, :khalf]) + dot_t(reduced_other[...], kernel_t[:, khalf:])
    x = x + posemb
    start[...] = x
    xhat, ignored = norm_parts(x)
    normed_t[...] = (xhat * gains[0:1, :] + gains[1:2, :]).astype(BF).T

    @pl.when(first_image)
    def turn():
        if joined:
            pltpu.make_async_copy(attn, attn, sems.at[1]).wait()
        for at in range(0, 3 * width, 256):
            turned[at : at + 256, :] = attn[:, at : at + 256].T

    qkv_t[...] = dot(turned[...], normed_t[...]).astype(BF)
    spans = [slice(head * HEAD_DIM, (head + 1) * HEAD_DIM) for head in range(heads)]
    for head, span in enumerate(spans):
        q = qkv_t[span, :] * jnp.asarray(HEAD_DIM**-0.5, BF)
        scores[head] = t_dot(qkv_t[width + span.start : width + span.stop, :], q)
    shares = []
    for head in range(heads):
        top = jnp.max(scores[head], axis=0, keepdims=True)
        expd = jnp.exp(scores[head] - top)
        total = jnp.sum(expd, axis=0, keepdims=True)
        probs[head] = expd.astype(BF)
        lse[0, head : head + 1, :] = top + jnp.log(total)
        shares.append(1.0 / total)
    for head, span in enumerate(spans):
        v = qkv_t[2 * width + span.start : 2 * width + span.stop, :]
        mixed_t[span, :] = (dot(v, probs[head]) * shares[head]).astype(BF)
    lse[0, heads:, :] = jnp.zeros((lse.shape[1] - heads, lse.shape[2]), FL)
    x = start[...] + t_dot(mixed_t[...], attn[:, 3 * width :])
    middle[...] = x
    xhat, ignored = norm_parts(x)
    normed_two[...] = (xhat * gains[2:3, :] + gains[3:4, :]).astype(BF)


def mlp_tile(chunk, normed_two, up, down, final, hidden, slope):
    count = normed_two.shape[0] // chunk
    rows = lambda i: slice(i * chunk, (i + 1) * chunk)
    pre, low = {0: dot(normed_two[rows(0), :], up[...])}, {}
    for i in range(count + 1):
        if i + 1 < count:
            pre[i + 1] = dot(normed_two[rows(i + 1), :], up[...])
        if i < count:
            value = pre.pop(i)
            cdf, bell = normal_cdf(value)
            low[i] = (value * cdf).astype(BF)
            hidden[rows(i), :] = low[i]
            slope[rows(i), :] = (cdf + value * bell * 0.3989422804014327).astype(BF)
        if i > 0:
            final[rows(i - 1), :] += dot_t(low.pop(i - 1), down[...])


def mlp_kernel(chunk, held, normed_two, up, down, final, hidden, slope):
    @pl.when(pl.program_id(0) == 0)
    def first():
        final[...] = held[...]

    mlp_tile(chunk, normed_two, up, down, final, hidden, slope)


def head_part(
    images, classes, core, final, labels, image_count, gains, own, other,
    d_final, e_low, own_grad, other_grad, row_grads, loss,
):
    tokens = final.shape[0] // images
    width = final.shape[1]
    chalf = own.shape[1]
    gain = gains[4:5, :]
    places = lax.broadcasted_iota(jnp.int32, (8, width), 0)
    means = jnp.zeros((8, width), FL)
    for image in range(images):
        xhat, ignored = norm_parts(final[image * tokens : (image + 1) * tokens, :])
        mean_row = jnp.mean(xhat, axis=0, keepdims=True)
        means = jnp.where(places == image, mean_row, means)
    pooled = jnp.where(places < images, means * gain + gains[5:6, :], 0.0).astype(BF)
    logits = [dot(pooled, own[...]), dot(pooled, other[...])]
    lane = lax.broadcasted_iota(jnp.int32, (8, chalf), 1)
    kinds = [lane + core * chalf, lane + (1 - core) * chalf]
    masked = [jnp.where(kinds[k] < classes, logits[k], -1e30) for k in range(2)]
    top = jnp.maximum(
        jnp.max(masked[0], axis=1, keepdims=True), jnp.max(masked[1], axis=1, keepdims=True)
    )
    expd = [jnp.where(kinds[k] < classes, jnp.exp(masked[k] - top), 0.0) for k in range(2)]
    total = jnp.sum(expd[0], axis=1, keepdims=True) + jnp.sum(expd[1], axis=1, keepdims=True)
    log_total = top + jnp.log(total)
    named = labels[...]
    onehot = [(kinds[k] == named).astype(FL) for k in range(2)]
    target = jnp.sum(onehot[0] * logits[0], axis=1, keepdims=True) + jnp.sum(
        onehot[1] * logits[1], axis=1, keepdims=True
    )
    counted = (named >= 0).astype(FL)
    losses = counted * (log_total - target)
    loss[...] = jnp.broadcast_to(jnp.sum(losses, axis=0, keepdims=True), loss.shape)
    share = counted / image_count[...]
    d_logits = [((expd[k] / total - onehot[k]) * share).astype(BF) for k in range(2)]
    own_grad[...] = t_dot(pooled, d_logits[0])
    other_grad[...] = t_dot(pooled, d_logits[1]).astype(BF)
    d_pooled = dot_t(d_logits[0], own[...]) + dot_t(d_logits[1], other[...])
    row_grads[0:1, :] = jnp.sum(d_pooled * means, axis=0, keepdims=True)
    row_grads[1:2, :] = jnp.sum(d_pooled, axis=0, keepdims=True)
    row_grads[2:8, :] = jnp.zeros((6, width), FL)
    for image in range(images):
        rows = slice(image * tokens, (image + 1) * tokens)
        xhat, inverse = norm_parts(final[rows, :])
        dy = d_pooled[image : image + 1, :] * (1.0 / tokens)
        back = norm_back(xhat, inverse, gain, dy)
        d_final[rows, :] = back
        e_low[rows, :] = back.astype(BF)


def middle_kernel(
    images, classes, chunk, core_ref, held, normed_two, up, down, labels, image_count, gains,
    head_own, head_other, d_final, e_low, own_grad, other_grad, row_grads, loss, hidden, slope, final,
):
    step = pl.program_id(0)

    @pl.when(step == 0)
    def first():
        final[...] = held[...]

    mlp_tile(chunk, normed_two, up, down, final, hidden, slope)

    @pl.when(step == pl.num_programs(0) - 1)
    def head():
        head_part(
            images, classes, core_ref[0], final, labels, image_count, gains, head_own, head_other,
            d_final, e_low, own_grad, other_grad, row_grads, loss,
        )


def mm(a, b, dims):
    return lax.dot_general(a, b, (dims, ((), ())), preferred_element_type=FL)


def norm_two_kernel(
    core_ref, d_normed, middle, d_final, gains, mixed_t, four_grads,
    d_middle, o_low, row_grads, out_grad, sums, product,
):
    image = pl.program_id(0)
    width = middle.shape[1]
    half = width // 2
    xhat, inverse = norm_parts(middle[...])
    dy = d_normed[...]
    back = d_final[...] + norm_back(xhat, inverse, gains[2:3, :], dy)
    d_middle[...] = back
    o_low[...] = back.astype(BF)

    @pl.when(image == 0)
    def first():
        sums[...] = jnp.zeros(sums.shape, FL)
        product[...] = jnp.zeros(product.shape, FL)

    sums[0:1, :] += jnp.sum(dy * xhat, axis=0, keepdims=True)
    sums[1:2, :] += jnp.sum(dy, axis=0, keepdims=True)
    other = pl.multiple_of((1 - core_ref[0]) * half, 128)
    product[...] += dot(mixed_t[...], o_low[:, pl.ds(other, half)])

    @pl.when(image == pl.num_programs(0) - 1)
    def last():
        row_grads[0:2, :] = jnp.zeros((2, width), FL)
        row_grads[2:4, :] = sums[0:2, :]
        row_grads[4:6, :] = four_grads[0:2, :]
        row_grads[6:8, :] = jnp.zeros((2, width), FL)
        out_grad[...] = product[...].astype(BF)


def place(where_ref, row, rows, value, held, keep, send, col):
    size = value.shape[1]
    if send is None:
        keep[:, col : col + size] = value.astype(BF)
        return
    held[:, :size] = value
    half = keep.shape[0]
    for p in range(half):
        low = pl.multiple_of(where_ref[row, p] * rows, rows)
        high = pl.multiple_of(where_ref[row, half + p] * rows, rows)
        keep[p, :, col : col + size] = held[pl.ds(low, rows), :size].astype(BF)
        send[p, :, col : col + size] = held[pl.ds(high, rows), :size].astype(BF)


def split_outs(refs, aligned, number):
    if aligned:
        return [(refs[2 * k], refs[2 * k + 1]) for k in range(number)], refs[2 * number :]
    return [(refs[k], None) for k in range(number)], refs[number:]


class Loads:
    def __init__(self, sems):
        self.sems, self.targets = sems, []

    def add(self, target, *pairs):
        sem = self.sems.at[len(self.targets)]
        for source, place in pairs:
            pltpu.make_async_copy(source, place, sem).start()
        self.targets.append(target)
        return len(self.targets) - 1

    def wait(self, number):
        target = self.targets[number]
        pltpu.make_async_copy(target, target, self.sems.at[number]).wait()


def in_turn(products, stores):
    value = products[0]()
    for number, store in enumerate(stores):
        following = products[number + 1]() if number + 1 < len(products) else None
        store(value)
        value = following


def attend_back_kernel(
    cells_count, final, core_ref, o_low, attn, qkv_t, lse, d_middle, start, gains, cells, grads_in, *refs
):
    sum_in, refs = (refs[0], refs[1:]) if final else (None, refs)
    d_own, sent, sum_out, grads_out, d_qkv_t, d_mixed_t, summed, row_grads = refs[:8]
    scores, d_probs, probs, d_scores = refs[8:]
    width = o_low.shape[1]
    heads = width // HEAD_DIM
    image = pl.program_id(0)

    @pl.when(image == 0)
    def first():
        summed[...] = sum_in[...] if final else jnp.zeros(summed.shape, FL)
        row_grads[...] = grads_in[...]

    scale = HEAD_DIM**-0.5
    d_mixed_t[...] = dot_t(attn[:, 3 * width :], o_low[...]).astype(BF)
    spans = [slice(head * HEAD_DIM, (head + 1) * HEAD_DIM) for head in range(heads)]
    part = lambda ref, k, span: ref[k * width + span.start : k * width + span.stop, :]
    for head, span in enumerate(spans):
        q = part(qkv_t, 0, span) * jnp.asarray(scale, BF)
        scores[head] = t_dot(part(qkv_t, 1, span), q)
        d_probs[head] = t_dot(part(qkv_t, 2, span), d_mixed_t[span, :])
    for head in range(heads):
        soft = jnp.exp(scores[head] - lse[0, head : head + 1, :])
        probs[head] = soft.astype(BF)
        delta = jnp.sum(soft * d_probs[head], axis=0, keepdims=True)
        d_scores[head] = (soft * (d_probs[head] - delta)).astype(BF)
    for head, span in enumerate(spans):
        q = part(qkv_t, 0, span) * jnp.asarray(scale, BF)
        at = span.start
        d_qkv_t[at : at + HEAD_DIM, :] = (
            dot(part(qkv_t, 1, span), d_scores[head]) * scale
        ).astype(BF)
        d_qkv_t[width + at : width + at + HEAD_DIM, :] = dot_t(q, d_scores[head]).astype(BF)
        d_qkv_t[2 * width + at : 2 * width + at + HEAD_DIM, :] = dot_t(
            d_mixed_t[span, :], probs[head]
        ).astype(BF)
    half = width // 2
    for k in range(3):
        for ref, side in ((d_own, core_ref[0]), (sent, 1 - core_ref[0])):
            at = pl.multiple_of(k * width + side * half, 128)
            ref[k * half : (k + 1) * half, :] = d_qkv_t[pl.ds(at, half), :]
    dy = dot(attn[:, : 3 * width], d_qkv_t[...]).T
    xhat, inverse = norm_parts(start[...])
    back = d_middle[...] + norm_back(xhat, inverse, gains[0:1, :], dy)
    sent[3 * half :, :] = back.astype(BF).T
    summed[...] += back
    row_grads[0:1, :] += jnp.sum(dy * xhat, axis=0, keepdims=True)
    row_grads[1:2, :] += jnp.sum(dy, axis=0, keepdims=True)

    @pl.when(image == pl.num_programs(0) - 1)
    def last():
        grads_out[...] = row_grads[...]
        if not final:
            sum_out[...] = summed[...]
            return
        total = lax.dot_general(
            cells[...], summed[...], (((0,), (0,)), ((), ())),
            preferred_element_type=FL, precision=lax.Precision.HIGHEST,
        )
        summed[0:SMALL, :] = total
        summed[cells_count : cells_count + 6, :] = row_grads[0:6, :]
        sum_out[...] = summed[0:SMALL, :].T


def tail_grad_kernel(aligned, rows, spread, where_ref, core_ref, *refs):
    n_parts, own_parts, sent_parts, got_parts, r_parts = (
        refs[:2], refs[2:4], refs[4:6], refs[6:8], refs[8:10]
    )
    (small_hbm, small_got_hbm, mixed_hbm, o_hbm, out_hbm), refs = refs[10:15], refs[15:]
    d_parts, s_parts = (*own_parts, *got_parts), (*sent_parts, *got_parts)
    outs, scratch = split_outs(refs, aligned, 3)
    held, n_t, d_t, s_t, reduced, small, small_got, mixed_t, o_low, out_got, sems = scratch
    half, span = d_t.shape[1], own_parts[0].shape[1]
    width = s_t.shape[0]
    tokens = r_parts[0].shape[0]
    loads = Loads(sems)
    own = pl.multiple_of(core_ref[0] * half, 128)

    def load_tile(tile):
        at = pl.ds(tile * half, half)
        pairs = [(r_parts[k].at[:, at], reduced.at[tile, pl.ds(k * tokens, tokens), :]) for k in range(2)]
        return loads.add(reduced.at[tile], *pairs)

    def load_rows(tile):
        at = pl.ds(tile * half, half)
        pairs = [(d_parts[k].at[at, :], d_t.at[tile, :, pl.ds(k * span, span)]) for k in range(4)]
        return loads.add(d_t.at[tile], *pairs)

    out_ready = [
        loads.add(mixed_t, (mixed_hbm, mixed_t)),
        loads.add(o_low, (o_hbm.at[:, pl.ds(own, half)], o_low)),
        loads.add(out_got, (out_hbm, out_got)),
    ]
    tile_ready = [load_tile(0)]
    s_ready = loads.add(s_t, *[
            (s_parts[k].at[pl.ds(3 * half, width), :], s_t.at[:, pl.ds(k * span, span)])
            for k in range(4)
        ])
    tile_ready += [load_tile(1), load_tile(2), load_tile(3)]
    n_ready = loads.add(n_t, *[(n_parts[k], n_t.at[:, pl.ds(k * tokens, tokens)]) for k in range(2)])
    row_ready = [load_rows(0), load_rows(1), load_rows(2)]
    small_ready = [loads.add(small, (small_hbm, small)), loads.add(small_got, (small_got_hbm, small_got))]

    def put(stream, col, number, value):
        place(where_ref, stream, rows, value, held.at[number], *outs[stream], col)

    def out_product():
        for number in out_ready:
            loads.wait(number)
        return dot(mixed_t[...], o_low[...])

    def out_store(value):
        put(2, half, 0, value + out_got[...].astype(FL))

    def kernel_product(tile):
        if tile == 0:
            loads.wait(s_ready)
        loads.wait(tile_ready[tile])
        return dot(s_t[...], reduced[tile])

    def kernel_store(tile, value):
        for stream, col, lo, hi in spread[tile]:
            put(stream, col, (tile + 1) % 2, value[:, lo:hi])

    def attend_product(tile):
        if tile == 0:
            loads.wait(n_ready)
        loads.wait(row_ready[tile])
        return dot_t(n_t[...], d_t[tile])

    def attend_store(tile, value):
        put(tile, 0, (tile + 1) % 2, value)

    in_turn(
        [out_product]
        + [partial(kernel_product, tile) for tile in range(4)]
        + [partial(attend_product, tile) for tile in range(3)],
        [out_store]
        + [partial(kernel_store, tile) for tile in range(4)]
        + [partial(attend_store, tile) for tile in range(3)],
    )
    for number in small_ready:
        loads.wait(number)
    put(0, half, 0, small[...] + small_got[...])


def square_kernel(low, high, loss, *refs):
    *parts, out = refs
    total = jnp.zeros((1, 1), FL)

    def squares(value):
        value = value.astype(FL)
        return jnp.sum(jnp.sum(value * value, axis=0, keepdims=True), axis=1, keepdims=True)

    for number, part in enumerate(parts):
        total += squares(part[...])
        if number == 0:
            total -= 0.5 * squares(part[:, low:high])
    lane = lax.broadcasted_iota(jnp.int32, out.shape, 1)
    out[...] = jnp.where(lane == 0, total, jnp.where(lane == 1, loss[...], 0.0))


def update_kernel(cells, classes, spread, core_ref, sums, turned, *refs):
    grads, refs = refs[:10], refs[10:]
    olds, news, lows = refs[:18], refs[18:36], refs[36:]
    core = core_ref[0]
    norm = jnp.sqrt(sums[0:1, 0:1])
    factor = jnp.minimum(1.0, CLIP / norm)

    def step(table, cols, gradient, rate, decay, low):
        weight, first, second = (olds[6 * k + table][cols] for k in range(3))
        results = adam_step(weight, first, second, gradient.astype(FL) * factor, rate, decay)
        for k in range(3):
            news[6 * k + table][cols] = results[k]
        if low is not None:
            lows[low][cols] = results[0].astype(BF)

    def part(side, index, lo, size):
        return grads[5 * side + index][:, lo : lo + size]

    def cols(base, side, half):
        place = 1 - core if side else core
        return (slice(None), pl.ds(pl.multiple_of(base + place * half, 128), half))

    width = olds[2].shape[1] // 4
    fhalf, half, khalf = olds[3].shape[1] // 4, width // 2, olds[0].shape[1] // 2
    chalf = grads[3].shape[1] - fhalf
    for side in range(2):
        for k in range(3):
            step(2, cols(k * width, side, half), part(side, k, 0, half), RATE, DECAY, 1)
        step(2, cols(3 * width, side, half), part(side, 2, half, half), RATE, DECAY, 1)
        place = 1 - core if side else core
        for tile in range(4):
            for stream, col, lo, hi in spread[tile]:
                at = pl.multiple_of(place * khalf + tile * half + lo, 128)
                value = part(side, stream, col, hi - lo)
                step(0, (slice(None), pl.ds(at, hi - lo)), value, RATE, DECAY, 0)
        for k in range(2):
            step(3, cols(k * 2 * fhalf, side, fhalf), part(side, 4 - k, 0, fhalf), RATE, DECAY, 2)
    own, other = part(0, 3, fhalf, chalf), part(1, 3, fhalf, chalf)
    low_half = jnp.where(core == 0, own.astype(FL), other.astype(FL))
    high_half = jnp.where(core == 0, other.astype(FL), own.astype(FL))
    step(4, (slice(None), slice(0, chalf)), low_half, RATE, DECAY, 3)
    step(4, (slice(None), slice(chalf, classes)), high_half[:, : classes - chalf], RATE, DECAY, 3)
    tiny = part(0, 0, half, SMALL)
    step(1, (slice(None), slice(0, cells)), tiny[:, :cells], RATE_TABLE, 0.0, None)

    @pl.when(pl.program_id(0) == 0)
    def gains():
        on_side = turned[:, half : half + SMALL].astype(FL).T
        step(5, (slice(None), slice(None)), on_side[cells : cells + 6, :], RATE_TABLE, 0.0, None)


def body(
    count,
    pixels,
    patch_kind,
    labels,
    resize,
    embed_kernel,
    pos_base,
    gains,
    attn_weight,
    mlp_weight,
    head_weight,
    embed_first,
    pos_first,
    gains_first,
    attn_first,
    mlp_first,
    head_first,
    embed_second,
    pos_second,
    gains_second,
    attn_second,
    mlp_second,
    head_second,
):
    me = lax.axis_index("fsdp")
    core = lax.axis_index("rep")
    core_at = core.astype(jnp.int32)[None]
    images, tokens = pixels.shape[:2]
    total = images * tokens
    rows, width = attn_weight.shape[0], attn_weight.shape[0] * count
    aligned = rows % 16 == 0 and count & (count - 1) == 0
    ffw = mlp_weight.shape[1] // 2
    classes = head_weight.shape[1]
    kdim = embed_kernel.shape[0]
    cells_count = pos_base.shape[0]
    feats, base = resize.shape[1:]
    chalf = -(-classes // 256) * 128
    half, fhalf, khalf = width // 2, ffw // 2, kdim // 2
    heads = width // HEAD_DIM
    lse_rows = -(-heads // 8) * 8
    chunk = min(total, 256)
    tiles = fhalf // TILE

    first, second = khalf // 4, khalf // 4 + 2 * SMALL
    third = khalf - first - second
    widths = (width + first + SMALL, half + second, half + third)
    pieces = call(
        partial(prepare_kernel, cells_count),
        (1,),
        [
            whole((rows, kdim)),
            whole((rows, cells_count)),
            whole((6, rows)),
            whole((rows, 4 * width)),
        ],
        [whole((rows, size)) for size in widths],
        [sds((rows, size), BF) for size in widths],
        scratch=[pltpu.VMEM((128, 128), FL)],
        prefetch=2,
        limit=MOST,
    )(core_at, labels, embed_kernel.T, pos_base.T, gains, attn_weight)
    mlp_in, *pieces = tie(mlp_weight, *pieces)
    rest = call(
        prepare_rest_kernel,
        (1,),
        [whole((rows, 2 * ffw)), whole((rows, classes))],
        whole((rows, ffw + chalf)),
        sds((rows, ffw + chalf), BF),
        prefetch=1,
        limit=MOST,
    )(core_at, mlp_in, head_weight)

    fan_orders = [
        order_of(count, [1, 4, 8, 2]),
        order_of(count, [2, 1, 4, 8]),
        order_of(count, [4, 2, 1, 8]),
    ]
    if aligned:
        near, far, rest = gather_relative(pieces, count, fan_orders, rest, len(bits_of(count)) - 1)
        *near, patch_kind = tie(*near, patch_kind)
    rest_own = lax.all_gather(rest, "fsdp", axis=0, tiled=True)
    r_own, r_other = call(
        reduce_kernel,
        (images,),
        [
            pl.BlockSpec((1, 3 * feats, tokens), lambda b, kind, c: (b, 0, 0)),
            pl.BlockSpec((1, feats, base), lambda b, kind, c: (kind[b], 0, 0)),
        ],
        [pl.BlockSpec((tokens, khalf), lambda b, kind, c: (b, 0))] * 2,
        [sds((total, khalf), BF)] * 2,
        prefetch=2,
    )(patch_kind, core_at, jnp.transpose(pixels, (0, 2, 1)), resize)

    if aligned:
        *far, r_own, r_other = tie(*far, r_own, r_other)
        gathered = []
        for one, two in zip(near, far):
            gathered += [one, two, other_core(one), other_core(two)]
        where_fan = jnp.stack(
            [me ^ jnp.array(relative_masks(order), jnp.int32) for order in fan_orders]
        )
        plan = (
            (
                (0, half, 1, 0, half),
                (half, half, 1, width, half),
                (width, first, 0, 0, khalf),
                (width + first, SMALL, 2, 0, 0),
            ),
            ((0, half, 1, 2 * width, half), (half, second, 0, first, khalf)),
            ((0, half, 1, 3 * width, half), (half, third, 0, first + second, khalf)),
        )
    else:
        where_fan = jnp.zeros((3, count), jnp.int32)
        own = [lax.all_gather(piece, "fsdp", axis=0, tiled=True) for piece in pieces]
        other = [other_core(value) for value in own]

        def joined(parts):
            one, two, three = parts
            return (
                jnp.concatenate([one[:, width : width + first], two[:, half:], three[:, half:]], axis=1),
                jnp.stack([one[:, :half], one[:, half:width], two[:, :half], three[:, :half]], axis=1),
                one[:, width + first :],
            )

        own_e, own_a, small = joined(own)
        other_e, other_a, small_other = joined(other)
        kernel_t = jnp.concatenate([own_e, other_e], axis=1)
        attn_low = jnp.stack(halves(own_a, other_a, core), axis=2).reshape(width, 4 * width)
        gain_rows = jnp.pad(small[:, cells_count : cells_count + 6].astype(FL).T, ((0, 2), (0, 0)))
        number = (small[:, cells_count + 6] + small_other[:, cells_count + 6]).astype(FL)
        image_count = (jnp.sum(number) / rows)[None, None]

    table = np.zeros((tokens, SMALL), np.float32)
    table[:, :cells_count] = grid_matrix()
    high = table.astype(jnp.bfloat16)
    low = (table - high.astype(np.float32)).astype(jnp.bfloat16)
    by_image = pl.BlockSpec((tokens, width), lambda b, *c: (b, 0))
    by_lane = pl.BlockSpec((width, tokens), lambda b, *c: (0, b))
    qkv_spec = pl.BlockSpec((3 * width, tokens), lambda b, *c: (0, b))
    lse_spec = pl.BlockSpec((1, lse_rows, tokens), lambda b, *c: (b, 0, 0))
    if aligned:
        weights_in = gathered
        weight_specs = [pl.BlockSpec(memory_space=pltpu.HBM)] * 12
        more_out = [sds((width, 4 * width), BF), sds((8, width), FL), sds((1, 1), FL)]
        more_scratch = [
            pltpu.VMEM((width, kdim), BF),
            pltpu.VMEM((width, SMALL), BF),
            pltpu.VMEM((width, SMALL), BF),
            pltpu.SemaphoreType.DMA((4,)),
        ]
    else:
        plan = None
        weights_in = (kernel_t, attn_low, small, small_other, gain_rows, image_count)
        weight_specs = [whole(item.shape) for item in weights_in]
        more_out, more_scratch = [], []
    start, normed_t, qkv_t, mixed_t, lse, middle, normed_two, *more = call(
        partial(forward_kernel, plan, cells_count),
        (images,),
        weight_specs + [pl.BlockSpec((tokens, khalf), lambda b, *c: (b, 0))] * 2
        + [whole((tokens, 2 * SMALL))],
        [by_image, by_lane, qkv_spec, by_lane, lse_spec, by_image, by_image]
        + [whole(item.shape) for item in more_out],
        [
            sds((total, width), FL),
            sds((width, total), BF),
            sds((3 * width, total), BF),
            sds((width, total), BF),
            sds((images, lse_rows, tokens), FL),
            sds((total, width), FL),
            sds((total, width), BF),
        ]
        + more_out,
        scratch=[
            pltpu.VMEM((3 * width, width), BF),
            pltpu.VMEM((heads, tokens, tokens), FL),
            pltpu.VMEM((heads, tokens, tokens), BF),
        ]
        + more_scratch,
        limit=MOST,
        prefetch=2,
    )(where_fan, core_at, *weights_in, r_own, r_other, jnp.asarray(np.concatenate([high, low], axis=1)))
    if aligned:
        attn_low, gain_rows, image_count = more
    rest_own, normed_two = tie(rest_own, normed_two)
    rest_other = other_core(rest_own)
    r_got, n_got = other_core(r_other), other_core(normed_t)

    col = lambda offset: pl.BlockSpec((width, TILE), lambda j: (0, offset + j))
    tile_spec = pl.BlockSpec((total, TILE), lambda j: (0, j))
    final, hidden, slope = call(
        partial(mlp_kernel, chunk),
        (tiles,),
        [whole((total, width)), whole((total, width)), col(0), col(tiles)],
        [whole((total, width)), tile_spec, tile_spec],
        [sds((total, width), FL), sds((total, fhalf), BF), sds((total, fhalf), BF)],
        limit=MOST,
    )(middle, normed_two, rest_own, rest_own)

    labels_col = jnp.pad(labels, (0, 8 - images), constant_values=-1)[:, None]
    head_spec = pl.BlockSpec((width, chalf), lambda i, c: (0, ffw // chalf))
    colc = lambda offset: pl.BlockSpec((width, TILE), lambda j, c: (0, offset + j))
    tilec = pl.BlockSpec((total, TILE), lambda j, c: (0, j))
    (
        d_final, e_low, head_own, head_other, four_grads, loss_part, hidden_other, slope_other,
    ) = call(
        partial(middle_kernel, images, classes, chunk),
        (tiles,),
        [
            whole((total, width)),
            whole((total, width)),
            colc(0),
            colc(tiles),
            whole((8, 1)),
            whole((1, 1)),
            whole((8, width)),
            head_spec,
            head_spec,
        ],
        [
            whole((total, width)),
            whole((total, width)),
            whole((width, chalf)),
            whole((width, chalf)),
            whole((8, width)),
            whole((8, 128)),
            tilec,
            tilec,
        ],
        [
            sds((total, width), FL),
            sds((total, width), BF),
            sds((width, chalf), FL),
            sds((width, chalf), BF),
            sds((8, width), FL),
            sds((8, 128), FL),
            sds((total, fhalf), BF),
            sds((total, fhalf), BF),
        ],
        scratch=[pltpu.VMEM((total, width), FL)],
        prefetch=1,
    )(
        core_at, final, normed_two, rest_other, rest_other, labels_col, image_count, gain_rows,
        rest_own, rest_other,
    )

    up_of = lambda part: part[:, :fhalf]
    down_of = lambda part: part[:, fhalf:ffw]
    down_other = mm(e_low, hidden_other, ((0,), (0,))).astype(BF)
    down_got, head_got = other_core(down_other), other_core(head_other)
    e_one, ignored = tie(e_low, down_other)
    d_pre_other = (
        mm(e_one, down_of(rest_other), ((1,), (0,))) * slope_other.astype(FL)
    ).astype(BF)
    d_head = (head_own + head_got.astype(FL)).astype(BF)
    e_two, ignored = tie(e_one, d_pre_other)
    d_down = (mm(e_two, hidden, ((0,), (0,))) + down_got.astype(FL)).astype(BF)

    def split_shapes(size):
        if aligned:
            return [sds((count // 2, rows, size), BF)] * 2
        return [sds((width, size), BF)]

    def split_specs(size):
        return [whole(item.shape) for item in split_shapes(size)]

    def begin(parts, order):
        keep, send, held = split_sides(parts, count, order, me)
        return partner(send, count, order[0]), keep, held, order, me

    def arrive(flows, *others):
        given = tie(*[flow[0] for flow in flows], *others)
        following = []
        for (ignored, keep, held, order, who), got in zip(flows, given):
            keep, send, held = step_sides(keep, got, held, order[1:], who)
            got = None if send is None else partner(send, count, order[1])
            following.append((got, keep, held, order[1:], who))
        return following, given[len(flows) :]

    if aligned:
        flow_down = begin([d_down, d_head], order_of(count, [1, 4, 8, 2]))
    d_pre_other, ignored = tie(d_pre_other, d_down)
    up_other = mm(normed_two, d_pre_other, ((0,), (0,))).astype(BF)
    up_got = other_core(up_other)
    e_three, ignored = tie(e_two, up_other)
    d_pre = (mm(e_three, down_of(rest_own), ((1,), (0,))) * slope.astype(FL)).astype(BF)
    d_up = (mm(normed_two, d_pre, ((0,), (0,))) + up_got.astype(FL)).astype(BF)
    if aligned:
        flow_up = begin([d_up], order_of(count, [2, 1, 4, 8]))
    d_pre, d_pre_other, ignored = tie(d_pre, d_pre_other, d_up)
    d_normed_two = mm(d_pre_other, up_of(rest_other), ((1,), (1,))) + mm(
        d_pre, up_of(rest_own), ((1,), (1,))
    )
    row_image = pl.BlockSpec((tokens, width), lambda b, c: (b, 0))
    d_middle, o_low, grads_in, out_other = call(
        norm_two_kernel,
        (images,),
        [
            row_image,
            row_image,
            row_image,
            whole((8, width)),
            pl.BlockSpec((width, tokens), lambda b, c: (0, b)),
            whole((8, width)),
        ],
        [row_image, row_image, whole((8, width)), whole((width, half))],
        [
            sds((total, width), FL),
            sds((total, width), BF),
            sds((8, width), FL),
            sds((width, half), BF),
        ],
        scratch=[pltpu.VMEM((8, width), FL), pltpu.VMEM((width, half), FL)],
        prefetch=1,
    )(core_at, d_normed_two, middle, d_final, gain_rows, mixed_t, four_grads)
    out_got = other_core(out_other)
    pair = max(images // 2, 1)
    shift = lambda k: [
        pl.BlockSpec((tokens, width), lambda b, c: (b + k, 0)),
        pl.BlockSpec((3 * width, tokens), lambda b, c: (0, b + k)),
        pl.BlockSpec((1, lse_rows, tokens), lambda b, c: (b + k, 0, 0)),
        pl.BlockSpec((width, tokens), lambda b, c: (0, b + k)),
    ]

    def attend_back(k, final, grads_in, o_low, sum_in=()):
        image_spec, qkvs, lses, lanes = shift(k)
        sums = sds((width, SMALL), FL) if final else sds((tokens, width), FL)
        own_lanes = lambda size: pl.BlockSpec((size, tokens), lambda b, c: (0, b))
        return call(
            partial(attend_back_kernel, cells_count, final),
            (pair,),
            [
                image_spec,
                whole((width, 4 * width)),
                qkvs,
                lses,
                image_spec,
                image_spec,
                whole((8, width)),
                whole((tokens, SMALL)),
                whole((8, width)),
            ]
            + [whole((tokens, width))] * len(sum_in),
            [own_lanes(3 * half), own_lanes(3 * half + width), whole(sums.shape), whole((8, width))],
            [
                sds((3 * half, pair * tokens), BF),
                sds((3 * half + width, pair * tokens), BF),
                sums,
                sds((8, width), FL),
            ],
            scratch=[
                pltpu.VMEM((3 * width, tokens), BF),
                pltpu.VMEM((width, tokens), BF),
                pltpu.VMEM((tokens, width), FL),
                pltpu.VMEM((8, width), FL),
                pltpu.VMEM((heads, tokens, tokens), FL),
                pltpu.VMEM((heads, tokens, tokens), FL),
                pltpu.VMEM((heads, tokens, tokens), BF),
                pltpu.VMEM((heads, tokens, tokens), BF),
            ],
            prefetch=1,
            limit=MORE,
        )(core_at, o_low, attn_low, qkv_t, lse, d_middle, start, gain_rows, jnp.asarray(table), grads_in, *sum_in)

    d_own_one, sent_one, sum_one, grads_one = attend_back(0, False, grads_in, o_low)
    if aligned:
        (flow_down, flow_up), (sum_one, sent_one) = arrive([flow_down, flow_up], sum_one, sent_one)
    got_one = other_core(sent_one)
    d_own_two, sent_two, d_small, ignored = attend_back(pair, True, grads_one, o_low, (sum_one,))
    if aligned:
        (flow_down, flow_up), (sent_two, d_small) = arrive([flow_down, flow_up], sent_two, d_small)
    got_two, small_got = other_core(sent_two), other_core(d_small)

    spread = (
        ((0, half + SMALL, 0, half),),
        ((1, half, 0, half),),
        ((1, 2 * half, 0, 2 * SMALL), (0, 2 * half + SMALL, 2 * SMALL, half)),
        ((0, 2 * half + 2 * SMALL, 0, SMALL), (2, 2 * half, SMALL, half)),
    )
    tail_widths = (2 * half + 3 * SMALL, 2 * half + 2 * SMALL, 3 * half - SMALL)
    tail_parts = call(
        partial(tail_grad_kernel, aligned, rows, spread),
        (1,),
        [pl.BlockSpec(memory_space=pltpu.HBM)] * 15,
        [spec for size in tail_widths for spec in split_specs(size)],
        [shape for size in tail_widths for shape in split_shapes(size)],
        scratch=[
            pltpu.VMEM((2, width, half), FL),
            pltpu.VMEM((width, 2 * total), BF),
            pltpu.VMEM((3, half, 2 * total), BF),
            pltpu.VMEM((width, 4 * pair * tokens), BF),
            pltpu.VMEM((4, 2 * total, half), BF),
            pltpu.VMEM((width, SMALL), FL),
            pltpu.VMEM((width, SMALL), FL),
            pltpu.VMEM((width, total), BF),
            pltpu.VMEM((total, half), BF),
            pltpu.VMEM((width, half), BF),
            pltpu.SemaphoreType.DMA((14,)),
        ],
        limit=MORE,
        prefetch=2,
    )(
        where_fan, core_at, normed_t, n_got, d_own_one, d_own_two, sent_one, sent_two, got_one, got_two,
        r_own, r_got, d_small, small_got,
        mixed_t, o_low, out_got,
    )
    if aligned:
        (flow_down, flow_up), tail_parts = arrive([flow_down, flow_up], *tail_parts)
        flows = [flow_down, flow_up]
        for k, order in enumerate(fan_orders):
            keep, send = tail_parts[2 * k : 2 * k + 2]
            shape = (2,) * (len(order) - 1) + keep.shape[1:]
            got = partner(send, count, order[0]).reshape(shape)
            flows.append((got, keep.reshape(shape), order[1:], order, None))
        while any(flow[0] is not None for flow in flows):
            live = [k for k, flow in enumerate(flows) if flow[0] is not None]
            after, ignored = arrive([flows[k] for k in live])
            for k, flow in zip(live, after):
                flows[k] = flow
        g_down, g_up, *g_tail = [flow[1] for flow in flows]
    else:
        g_down, g_up, *g_tail = [
            lax.psum_scatter(part, "fsdp", scatter_dimension=0, tiled=True)
            for part in (jnp.concatenate([d_down, d_head], axis=1), d_up, *tail_parts)
        ]

    own_shards = [*g_tail, g_down, g_up]
    other_shards = [other_core(item) for item in own_shards]
    sums = call(
        partial(square_kernel, half, half + SMALL),
        (1,),
        [whole((8, 128))] + [whole(item.shape) for item in own_shards],
        whole((8, 128)),
        sds((8, 128), FL),
    )(loss_part, *own_shards)
    sums = sum_everywhere(sums, count)
    tables = (embed_kernel.T, pos_base.T, attn_weight, mlp_weight, head_weight, gains)
    firsts = (embed_first.T, pos_first.T, attn_first, mlp_first, head_first, gains_first)
    seconds = (embed_second.T, pos_second.T, attn_second, mlp_second, head_second, gains_second)
    block = 16 if rows % 16 == 0 else rows

    def by_rows(item):
        if item.shape[0] != rows:
            return whole(item.shape)
        return pl.BlockSpec((block, item.shape[1]), lambda i, c: (i, 0))

    olds = (*tables, *firsts, *seconds)
    lows = [sds(tables[k].shape, BF) for k in (0, 2, 3, 4)]
    outs = call(
        partial(update_kernel, cells_count, classes, spread),
        (rows // block,),
        [whole((8, 128)), whole(g_tail[0].shape)]
        + [by_rows(item) for item in (*own_shards, *other_shards, *olds)],
        [by_rows(item) for item in (*olds, *lows)],
        [sds(item.shape, FL) for item in olds] + lows,
        prefetch=1,
    )(core_at, sums, g_tail[0], *own_shards, *other_shards, *olds)
    new, low = outs[:18], outs[18:]
    sets = [
        (new[6 * k].T, new[6 * k + 1].T, new[6 * k + 5], *new[6 * k + 2 : 6 * k + 5])
        for k in range(3)
    ]
    return (
        sums[0, 1],
        image_count[0, 0],
        jnp.sqrt(sums[0, 0]),
        *sets[0],
        *sets[1],
        *sets[2],
        low[0].T,
        *low[1:],
    )


def solution(mesh):
    data = P(("rep", "fsdp"))
    columns, rows = P(None, "fsdp"), P("fsdp", None)
    table = (columns, columns, columns, rows, rows, rows)
    in_specs = (P(("rep", "fsdp"), None, None), data, data, P()) + table * 3
    out_specs = (P(), P(), P()) + table * 3 + (columns, rows, rows, rows)
    return jax.shard_map(
        partial(body, mesh.shape["fsdp"]),
        mesh=mesh,
        in_specs=in_specs,
        out_specs=out_specs,
        check_vma=False,
    )
```
